32 devices in a mesh: sweep: 2 (over core), leaf: 16 (over z, y, x).
Axes of the slice: x: 2, y: 2, z: 4, core: 2. Of those that a mesh axis runs over, the one named last changes fastest.
Arguments:
- sources: bfloat16 [2, 16, 128, 384], P('sweep', 'leaf'), may hold values from -6 to 6
- solve_tiles: bfloat16 [2, 16, 384, 384], P('sweep', 'leaf'), may hold values from -0.3125 to 0.3125
- self_merge: bfloat16 [2, 16, 4, 384, 384], P('sweep', 'leaf'), may hold values from -0.21875 to 0.21875
- partner_merge: bfloat16 [2, 16, 4, 384, 384], P('sweep', 'leaf'), may hold values from -0.21875 to 0.21875
- coupling: bfloat16 [2, 16, 384, 384], P('sweep', 'leaf'), may hold values from -0.3125 to 0.3125
- front_map: int32 [2, 16, 4, 384], P('sweep', 'leaf'), may hold values from 0 to 383, each once within a row
Outputs:
- fronts: bfloat16 [2, 16, 128, 384], P('sweep', 'leaf')
The draws below stay inside these ranges and needn't reach their ends.
Inputs may be any that keep to these rules, and one draw needn't show every extreme that they name: Each row front_map[s, l, j, :] is a permutation of 0 to 383.
All inputs are finite; a program needn't handle non-finite values.
Results may differ from the reference program's by a relative error of at most 0.039.
Values may be sent and summed in bfloat16 or wider, within the bound.
No kernel may reach another device: no remote copies, remote signals or barrier semaphores. Data moves between devices by JAX's collectives and lax.ppermute only.
A program may use at most 64 MiB of HBM per device.

```python
import jax
import jax.numpy as jnp
from jax import lax

U = 384
R = 128
LEVELS = 4
SECTIONS = 2
LEAVES = 16


def levels(own_key, extent, shards, least, high):
    def one(position, blocks):
        draws = jax.random.uniform(jax.random.fold_in(jax.random.fold_in(own_key, 6), position), (blocks,), jnp.float32, least / len(shards), high / len(shards))
        return jnp.repeat(jnp.exp(draws), extent[position] // blocks).reshape((-1,) + (1,) * (len(extent) - position - 1))

    factor_of = one(*shards[0])
    for cut in shards[1:]:
        factor_of = factor_of * one(*cut)
    return factor_of


def centred(rng, extent, deviation, most, cuts=(), kind=jnp.bfloat16):
    array = jax.random.normal(rng, extent, jnp.float32) * deviation
    if len(cuts) > 0:
        array = levels(rng, extent, cuts, -0.22, 0.18) * array
    return jnp.clip(array, min=-most, max=most).astype(kind)


def setup_inputs(seed: int = 0) -> dict:
    key_of = jax.random.split(jax.random.key(seed), 7)
    return {
        "sources": centred(key_of[0], (SECTIONS, LEAVES, R, U), 1.0, 6.0, ((0, 2), (1, 16))),
        "solve_tiles": centred(key_of[1], (SECTIONS, LEAVES, U, U), U ** -0.5, 0.3125, ((0, 2), (1, 16))),
        "self_merge": centred(key_of[2], (SECTIONS, LEAVES, LEVELS, U, U), (2 * U) ** -0.5, 0.21875, ((0, 2), (1, 16))),
        "partner_merge": centred(key_of[3], (SECTIONS, LEAVES, LEVELS, U, U), (2 * U) ** -0.5, 0.21875, ((0, 2), (1, 16))),
        "coupling": centred(key_of[4], (SECTIONS, LEAVES, U, U), U ** -0.5, 0.3125, ((0, 2), (1, 16))),
        "front_map": jax.vmap(lambda own: jax.random.permutation(own, U))(jax.random.split(key_of[5], SECTIONS * LEAVES * LEVELS)).reshape((SECTIONS, LEAVES, LEVELS, U)).astype(jnp.int32),
    }


def batched(left, right):
    return jnp.einsum("lru,luv->lrv", left.astype(jnp.float32), right.astype(jnp.float32), precision=lax.Precision.HIGHEST)


def flip_pairs(front, level_index):
    count = front.shape[0]
    stride = 2 ** level_index
    shaped = front.reshape(count // (2 * stride), 2, stride, front.shape[1], front.shape[2])
    return shaped[:, ::-1].reshape(front.shape)


def reference(sources, solve_tiles, self_merge, partner_merge, coupling, front_map):
    plane = jnp.zeros(sources.shape[1:], jnp.bfloat16)
    results = []
    for section in range(SECTIONS):
        carried = batched(plane, coupling[section])
        loaded = (sources[section].astype(jnp.float32) + carried).astype(jnp.bfloat16)
        front = batched(loaded, solve_tiles[section]).astype(jnp.bfloat16)
        for level_index in range(LEVELS):
            partner = flip_pairs(front, level_index)
            mapped = jnp.take_along_axis(partner, front_map[section, :, level_index][:, None, :], axis=2)
            total = batched(front, self_merge[section, :, level_index]) + batched(mapped, partner_merge[section, :, level_index])
            front = total.astype(jnp.bfloat16)
        results.append(front)
        plane = front
    return jnp.stack(results)
```

```python
import jax
import jax.numpy as jnp
from jax import lax
from jax.sharding import PartitionSpec as P

BF = jnp.bfloat16
F32 = jnp.float32


def mm(left, right):
    return jnp.dot(left, right, preferred_element_type=F32)


def fold(index_map, factor):
    width = factor.shape[0]
    rows = lax.broadcasted_iota(jnp.int32, (width, width), 0)
    hot = (rows == index_map[None, :]).astype(BF)
    return mm(hot, factor).astype(BF)


def body(sources, solve_tiles, self_merge, partner_merge, coupling, front_map):
    source_rows = sources[0, 0]
    solve = solve_tiles[0, 0]
    plane_factor = coupling[0, 0]
    sections = lax.axis_size("sweep")
    leaves = lax.axis_size("leaf")
    count = self_merge.shape[2]
    me = lax.axis_index("sweep")

    own = [self_merge[0, 0, j] for j in range(count)]
    folded = [fold(front_map[0, 0, j], partner_merge[0, 0, j]) for j in range(count)]

    def swap(value, section, bit):
        pairs = [(section * leaves + l, section * leaves + (l ^ bit)) for l in range(leaves)]
        return lax.ppermute(value, ("sweep", "leaf"), pairs)

    def hand_on(value, section):
        pairs = [((section - 1) * leaves + l, section * leaves + l) for l in range(leaves)]
        return lax.ppermute(value, ("sweep", "leaf"), pairs)

    out = None
    for section in range(sections):
        loaded = source_rows
        if section > 0:
            incoming = hand_on(current, section)
            loaded = (source_rows.astype(F32) + mm(incoming, plane_factor)).astype(BF)
        current = mm(loaded, solve).astype(BF)
        for j in range(count):
            partner = swap(current, section, 2**j)
            current = (mm(current, own[j]) + mm(partner, folded[j])).astype(BF)
        out = current if out is None else jnp.where(me == section, current, out)
    return out[None, None]


def solution(mesh):
    spec = P("sweep", "leaf")
    return jax.shard_map(
        body,
        mesh=mesh,
        in_specs=(spec,) * 6,
        out_specs=spec,
        check_vma=False,
    )
```

```python
import jax
import jax.numpy as jnp
from jax import lax
from jax.experimental import pallas as pl
from jax.experimental.pallas import tpu as pltpu
from jax.sharding import PartitionSpec as P

BF = jnp.bfloat16
F32 = jnp.float32
SPLIT = 1


def mm(left, right):
    return jnp.dot(left, right, preferred_element_type=F32)


def load_kernel(rows_hbm, solve_hbm, out_ref, rows_ref, solve_ref, sems):
    copies = [
        pltpu.make_async_copy(rows_hbm, rows_ref, sems.at[0]),
        pltpu.make_async_copy(solve_hbm, solve_ref, sems.at[1]),
    ]
    for copy in copies:
        copy.start()
    for copy in copies:
        copy.wait()
    out_ref[...] = mm(rows_ref[...], solve_ref[...]).astype(BF)


def load(rows, solve):
    hbm = pl.BlockSpec(memory_space=pl.ANY)
    return pl.pallas_call(
        load_kernel,
        out_shape=jax.ShapeDtypeStruct(rows.shape, BF),
        in_specs=[hbm, hbm],
        out_specs=pl.BlockSpec(memory_space=pltpu.VMEM),
        scratch_shapes=[
            pltpu.VMEM(rows.shape, BF),
            pltpu.VMEM(solve.shape, BF),
            pltpu.SemaphoreType.DMA((2,)),
        ],
        cost_estimate=pl.CostEstimate(
            flops=2 * rows.size * solve.shape[1],
            bytes_accessed=2 * (2 * rows.size + solve.size),
            transcendentals=0,
        ),
    )(rows, solve)


def prepare_kernel(
    split, own_hbm, partner_hbm, map_hbm, low_ref, high_ref, partner_ref, map_ref, sems, map_sem
):
    count, width, _ = partner_ref.shape
    map_copy = pltpu.make_async_copy(map_hbm, map_ref, map_sem)
    map_copy.start()
    copies = []
    for j in range(count):
        out, at = (low_ref, 2 * j) if j < split else (high_ref, 2 * (j - split))
        pair = (
            pltpu.make_async_copy(partner_hbm.at[j], partner_ref.at[j], sems.at[2 * j]),
            pltpu.make_async_copy(own_hbm.at[j], out.at[at], sems.at[2 * j + 1]),
        )
        for copy in pair:
            copy.start()
        copies.append(pair)
    map_copy.wait()
    rows = lax.broadcasted_iota(jnp.int32, (width, width), 0)
    for j in range(count):
        copies[j][0].wait()
        out, at = (low_ref, 2 * j) if j < split else (high_ref, 2 * (j - split))
        hot = (rows == map_ref[j : j + 1, :]).astype(BF)
        out[at + 1] = mm(hot, partner_ref[j]).astype(BF)
    for pair in copies:
        pair[1].wait()


def prepare(own, partner, index_map):
    count, width, _ = own.shape
    split = min(SPLIT, count - 1)
    vmem = pl.BlockSpec(memory_space=pltpu.VMEM)
    hbm = pl.BlockSpec(memory_space=pl.ANY)
    return pl.pallas_call(
        lambda *refs: prepare_kernel(split, *refs),
        out_shape=(
            jax.ShapeDtypeStruct((2 * split, width, width), BF),
            jax.ShapeDtypeStruct((2 * (count - split), width, width), BF),
        ),
        in_specs=[hbm] * 3,
        out_specs=(vmem, vmem),
        scratch_shapes=[
            pltpu.VMEM(partner.shape, BF),
            pltpu.VMEM(index_map.shape, jnp.int32),
            pltpu.SemaphoreType.DMA((2 * count,)),
            pltpu.SemaphoreType.DMA,
        ],
        compiler_params=pltpu.CompilerParams(vmem_limit_bytes=32 * 2**20),
        cost_estimate=pl.CostEstimate(
            flops=2 * count * width**3, bytes_accessed=8 * count * width**2, transcendentals=0
        ),
    )(own, partner, index_map)


def body(sources, solve_tiles, self_merge, partner_merge, coupling, front_map):
    source_rows = sources[0, 0]
    solve = solve_tiles[0, 0]
    plane_factor = coupling[0, 0]
    sections = lax.axis_size("sweep")
    leaves = lax.axis_size("leaf")
    count = self_merge.shape[2]
    split = min(SPLIT, count - 1)
    me = lax.axis_index("sweep")

    def host(section):
        return min(section | 1, sections - 1)

    def permute(value, target):
        pairs = []
        for s in range(sections):
            for l in range(leaves):
                to, leaf = target(s, l)
                pairs.append((s * leaves + l, to * leaves + leaf))
        return lax.ppermute(value, ("sweep", "leaf"), pairs)

    def twin(s):
        return s ^ 1 if (s ^ 1) < sections else s

    def swap(value, row, bit):
        return permute(value, lambda s, l: (s, l ^ bit) if s == row else (s, l))

    def cross(value, pair, bit=0):
        return permute(
            value, lambda s, l: (twin(s), l ^ bit) if s in (pair, twin(pair)) else (s, l)
        )

    x = load(source_rows, solve)
    x, *raw = lax.optimization_barrier((x, self_merge, partner_merge, front_map))
    low, high = prepare(*(value[0, 0] for value in raw))
    moved = permute(high, lambda s, l: (twin(s), l))

    def factors(j, table):
        if j < split:
            return low[2 * j], low[2 * j + 1]
        return table[2 * (j - split)], table[2 * (j - split) + 1]

    results = []
    pending = None
    for section in range(sections):
        home = host(section)
        if section > 0:
            plane = front
            if host(section - 1) != section:
                last = host(section - 1)
                turn = {last: section, section: last}
                plane = permute(front, lambda s, l: (turn.get(s, s), l))
            loaded = (source_rows.astype(F32) + mm(plane, plane_factor)).astype(BF)
            x = mm(loaded, solve).astype(BF)
        for j in range(count):
            bit = 2**j
            own, other = factors(j, moved if home != section else high)
            if home != section and j == split:
                mine, partner = cross(x, section), cross(x, section, bit)
            else:
                row = section if j < split else home
                mine, partner = x, swap(x, row, bit)
            own_term = lax.optimization_barrier(mm(mine, own))
            if pending is not None and j == min(1, count - 1):
                back, owner = pending
                back, own_term = lax.optimization_barrier((back, own_term))
                results.append((owner, cross(back, owner)))
                pending = None
            x = (own_term + mm(partner, other)).astype(BF)
        front = x
        if home == section:
            results.append((section, front))
        else:
            pending = (front, section)
    if pending is not None:
        results.append((pending[1], cross(*pending)))
    out = results[0][1]
    for section, result in results[1:]:
        out = jnp.where(me == section, result, out)
    return out[None, None]


def solution(mesh):
    spec = P("sweep", "leaf")
    return jax.shard_map(
        body,
        mesh=mesh,
        in_specs=(spec,) * 6,
        out_specs=spec,
        check_vma=False,
    )
```

```python
import jax
import jax.numpy as jnp
from jax import lax
from jax.experimental import pallas as pl
from jax.experimental.pallas import tpu as pltpu
from jax.sharding import PartitionSpec as P

BF = jnp.bfloat16
F32 = jnp.float32
SPLIT = 1


def mm(left, right):
    return jnp.dot(left, right, preferred_element_type=F32)


def in_hbm(value):
    return pltpu.with_memory_space_constraint(value, pltpu.HBM)


def load_kernel(rows_hbm, solve_hbm, out_ref, rows_ref, solve_ref, sems):
    copies = [
        pltpu.make_async_copy(rows_hbm, rows_ref, sems.at[0]),
        pltpu.make_async_copy(solve_hbm, solve_ref, sems.at[1]),
    ]
    for copy in copies:
        copy.start()
    for copy in copies:
        copy.wait()
    out_ref[...] = mm(rows_ref[...], solve_ref[...]).astype(BF)


def load(rows, solve):
    hbm = pl.BlockSpec(memory_space=pltpu.HBM)
    return pl.pallas_call(
        load_kernel,
        out_shape=pltpu.VMEM(rows.shape, BF),
        in_specs=[hbm, hbm],
        out_specs=pl.BlockSpec(memory_space=pltpu.VMEM),
        scratch_shapes=[
            pltpu.VMEM(rows.shape, BF),
            pltpu.VMEM(solve.shape, BF),
            pltpu.SemaphoreType.DMA((2,)),
        ],
        cost_estimate=pl.CostEstimate(
            flops=2 * rows.size * solve.shape[1],
            bytes_accessed=2 * (2 * rows.size + solve.size),
            transcendentals=0,
        ),
    )(in_hbm(rows), in_hbm(solve))


def prepare_kernel(
    split, own_hbm, partner_hbm, map_hbm, low_ref, high_ref, partner_ref, map_ref, sems, map_sem
):
    count, width, _ = partner_ref.shape
    map_copy = pltpu.make_async_copy(map_hbm, map_ref, map_sem)
    map_copy.start()
    copies = []
    for j in range(count):
        out, at = (low_ref, 2 * j) if j < split else (high_ref, 2 * (j - split))
        pair = (
            pltpu.make_async_copy(partner_hbm.at[j], partner_ref.at[j], sems.at[2 * j]),
            pltpu.make_async_copy(own_hbm.at[j], out.at[at], sems.at[2 * j + 1]),
        )
        for copy in pair:
            copy.start()
        copies.append(pair)
    map_copy.wait()
    rows = lax.broadcasted_iota(jnp.int32, (width, width), 0)
    for j in range(count):
        copies[j][0].wait()
        out, at = (low_ref, 2 * j) if j < split else (high_ref, 2 * (j - split))
        hot = (rows == map_ref[j : j + 1, :]).astype(BF)
        out[at + 1] = mm(hot, partner_ref[j]).astype(BF)
    for pair in copies:
        pair[1].wait()


def prepare(own, partner, index_map):
    count, width, _ = own.shape
    split = min(SPLIT, count - 1)
    vmem = pl.BlockSpec(memory_space=pltpu.VMEM)
    hbm = pl.BlockSpec(memory_space=pltpu.HBM)
    return pl.pallas_call(
        lambda *refs: prepare_kernel(split, *refs),
        out_shape=(
            pltpu.VMEM((2 * split, width, width), BF),
            pltpu.VMEM((2 * (count - split), width, width), BF),
        ),
        in_specs=[hbm] * 3,
        out_specs=(vmem, vmem),
        scratch_shapes=[
            pltpu.VMEM(partner.shape, BF),
            pltpu.VMEM(index_map.shape, jnp.int32),
            pltpu.SemaphoreType.DMA((2 * count,)),
            pltpu.SemaphoreType.DMA,
        ],
        compiler_params=pltpu.CompilerParams(vmem_limit_bytes=32 * 2**20),
        cost_estimate=pl.CostEstimate(
            flops=2 * count * width**3, bytes_accessed=8 * count * width**2, transcendentals=0
        ),
    )(in_hbm(own), in_hbm(partner), in_hbm(index_map))


def stage_kernel(source, target, sem):
    copy = pltpu.make_async_copy(source, target, sem)
    copy.start()
    copy.wait()


def stage(table):
    return pl.pallas_call(
        stage_kernel,
        out_shape=pltpu.VMEM(table.shape, table.dtype),
        in_specs=[pl.BlockSpec(memory_space=pl.ANY)],
        out_specs=pl.BlockSpec(memory_space=pltpu.VMEM),
        scratch_shapes=[pltpu.SemaphoreType.DMA],
        compiler_params=pltpu.CompilerParams(vmem_limit_bytes=32 * 2**20),
        cost_estimate=pl.CostEstimate(
            flops=0, bytes_accessed=2 * 2 * table.size, transcendentals=0
        ),
    )(table)


def body(sources, solve_tiles, self_merge, partner_merge, coupling, front_map):
    source_rows = sources[0, 0]
    solve = solve_tiles[0, 0]
    plane_factor = coupling[0, 0]
    sections = lax.axis_size("sweep")
    leaves = lax.axis_size("leaf")
    count = self_merge.shape[2]
    split = min(SPLIT, count - 1)
    me = lax.axis_index("sweep")

    def host(section):
        return min(section | 1, sections - 1)

    def permute(value, target):
        pairs = []
        for s in range(sections):
            for l in range(leaves):
                to, leaf = target(s, l)
                pairs.append((s * leaves + l, to * leaves + leaf))
        return lax.ppermute(value, ("sweep", "leaf"), pairs)

    def twin(s):
        return s ^ 1 if (s ^ 1) < sections else s

    def swap(value, bit):
        return permute(value, lambda s, l: (s, l ^ bit))

    def cross(value, bit=0):
        return permute(value, lambda s, l: (twin(s), l ^ bit))

    x = load(source_rows, solve)
    x, *raw = lax.optimization_barrier((x, self_merge, partner_merge, front_map))
    low, high = prepare(*(value[0, 0] for value in raw))

    def factors(j, table):
        if j < split:
            return low[2 * j], low[2 * j + 1]
        return table[2 * (j - split)], table[2 * (j - split) + 1]

    results = []
    moved = None
    pending = None
    for section in range(sections):
        home = host(section)
        if section > 0:
            plane = front
            if host(section - 1) != section:
                last = host(section - 1)
                turn = {last: section, section: last}
                plane = permute(front, lambda s, l: (turn.get(s, s), l))
            loaded = (source_rows.astype(F32) + mm(plane, plane_factor)).astype(BF)
            x = mm(loaded, solve).astype(BF)
        for j in range(count):
            bit = 2**j
            if section == 0 and j == split:
                sent = high
                if j > 0:
                    sent, x = lax.optimization_barrier((high, x))
                moved = stage(cross(sent))
            own, other = factors(j, moved if home != section else high)
            if home != section and j == split:
                mine, partner = cross(x), cross(x, bit)
            else:
                mine, partner = x, swap(x, bit)
            own_term = lax.optimization_barrier(mm(mine, own))
            if pending is not None and j == min(1, count - 1):
                back, owner = pending
                back, own_term = lax.optimization_barrier((back, own_term))
                results.append((owner, cross(back)))
                pending = None
            x = (own_term + mm(partner, other)).astype(BF)
        front = x
        if home == section:
            results.append((section, front))
        else:
            pending = (front, section)
    if pending is not None:
        results.append((pending[1], cross(pending[0])))
    out = results[0][1]
    for section, result in results[1:]:
        out = jnp.where(me == section, result, out)
    return out[None, None]


def solution(mesh):
    spec = P("sweep", "leaf")
    return jax.shard_map(
        body,
        mesh=mesh,
        in_specs=(spec,) * 6,
        out_specs=spec,
        check_vma=False,
    )
```

```python
import functools

import jax
import jax.numpy as jnp
from jax import lax
from jax.experimental import pallas as pl
from jax.experimental.pallas import tpu as pltpu
from jax.sharding import PartitionSpec as P

BF = jnp.bfloat16
F32 = jnp.float32
MIB = 2**20
ALL_TO_ALL = True


def mm(left, right):
    return jnp.dot(left, right, preferred_element_type=F32)


def in_hbm(value):
    return pltpu.with_memory_space_constraint(value, pltpu.HBM)


def cost(flops, moved):
    return pl.CostEstimate(flops=flops, bytes_accessed=moved, transcendentals=0)


HBM = pl.BlockSpec(memory_space=pltpu.HBM)
VMEM = pl.BlockSpec(memory_space=pltpu.VMEM)
SMEM = pl.BlockSpec(memory_space=pltpu.SMEM)


def load_kernel(rows_hbm, solve_hbm, out_ref, rows_ref, solve_ref, sems):
    copies = [
        pltpu.make_async_copy(rows_hbm, rows_ref, sems.at[0]),
        pltpu.make_async_copy(solve_hbm, solve_ref, sems.at[1]),
    ]
    for copy in copies:
        copy.start()
    for copy in copies:
        copy.wait()
    out_ref[...] = mm(rows_ref[...], solve_ref[...]).astype(BF)


def load(rows, solve):
    return pl.pallas_call(
        load_kernel,
        out_shape=pltpu.VMEM(rows.shape, BF),
        in_specs=[HBM, HBM],
        out_specs=VMEM,
        scratch_shapes=[
            pltpu.VMEM(rows.shape, BF),
            pltpu.VMEM(solve.shape, BF),
            pltpu.SemaphoreType.DMA((2,)),
        ],
        cost_estimate=cost(2 * rows.size * solve.shape[1], 4 * rows.size + 2 * solve.size),
    )(in_hbm(rows), in_hbm(solve))


def prepare_kernel(own_hbm, partner_hbm, map_hbm, *refs):
    count = own_hbm.shape[0]
    width = own_hbm.shape[1]
    outs, (partner_ref, map_ref, sems, map_sem) = refs[:count], refs[count:]
    map_copy = pltpu.make_async_copy(map_hbm, map_ref, map_sem)
    map_copy.start()
    copies = []
    for j in range(count):
        pair = (
            pltpu.make_async_copy(partner_hbm.at[j], partner_ref.at[j], sems.at[2 * j]),
            pltpu.make_async_copy(own_hbm.at[j], outs[j].at[0], sems.at[2 * j + 1]),
        )
        for copy in pair:
            copy.start()
        copies.append(pair)
    map_copy.wait()
    rows = lax.broadcasted_iota(jnp.int32, (width, width), 0)
    for j in range(count):
        copies[j][0].wait()
        hot = (rows == map_ref[j : j + 1, :]).astype(BF)
        outs[j][1] = mm(hot, partner_ref[j]).astype(BF)
    for pair in copies:
        pair[1].wait()


def prepare(own, partner, index_map):
    count, width, _ = own.shape
    return pl.pallas_call(
        prepare_kernel,
        out_shape=tuple(pltpu.VMEM((2, width, width), BF) for _ in range(count)),
        in_specs=[HBM] * 3,
        out_specs=(VMEM,) * count,
        scratch_shapes=[
            pltpu.VMEM(partner.shape, BF),
            pltpu.VMEM(index_map.shape, jnp.int32),
            pltpu.SemaphoreType.DMA((2 * count,)),
            pltpu.SemaphoreType.DMA,
        ],
        compiler_params=pltpu.CompilerParams(vmem_limit_bytes=32 * MIB),
        cost_estimate=cost(2 * count * width**3, 8 * count * width**2),
    )(in_hbm(own), in_hbm(partner), in_hbm(index_map))


def pair_kernel(place_ref, low_ref, other_ref, high_ref, out_ref):
    place = place_ref[0]
    for k in range(4):
        left = (low_ref if k < 2 else other_ref)[k % 2]
        out_ref[lax.bitwise_xor(place, k)] = mm(left, high_ref[k // 2]).astype(BF)


def pair_factors(place, low, other, high):
    width = low.shape[1]
    return pl.pallas_call(
        pair_kernel,
        out_shape=pltpu.VMEM((4, width, width), BF),
        in_specs=[SMEM, VMEM, VMEM, VMEM],
        out_specs=VMEM,
        compiler_params=pltpu.CompilerParams(vmem_limit_bytes=32 * MIB),
        cost_estimate=cost(8 * width**3, 20 * width**2),
    )(place, low, other, high)


def combine_kernel(parts, factors_ref, out_ref):
    total = mm(parts[0][...], factors_ref[0])
    for k in range(1, 4):
        total += mm(parts[k][...], factors_ref[k])
    out_ref[...] = total.astype(BF)


def combine(parts, factors):
    stacked = not isinstance(parts, (list, tuple))

    def kernel(*refs):
        blocks = [refs[0].at[k] for k in range(4)] if stacked else refs[:4]
        combine_kernel(blocks, *refs[-2:])

    args = [parts] if stacked else list(parts)
    rows, width = args[0].shape[-2:]
    return pl.pallas_call(
        kernel,
        out_shape=pltpu.VMEM((rows, width), BF),
        in_specs=[VMEM] * (len(args) + 1),
        out_specs=VMEM,
        compiler_params=pltpu.CompilerParams(vmem_limit_bytes=32 * MIB),
        cost_estimate=cost(8 * rows * width**2, 10 * rows * width + 8 * width**2),
    )(*args, factors)


def body(sources, solve_tiles, self_merge, partner_merge, coupling, front_map):
    source_rows = sources[0, 0]
    solve = solve_tiles[0, 0]
    plane_factor = coupling[0, 0]
    sections = lax.axis_size("sweep")
    leaves = lax.axis_size("leaf")
    count = self_merge.shape[2]
    me = lax.axis_index("sweep")
    leaf = lax.axis_index("leaf")

    def permute(value, target):
        pairs = []
        for s in range(sections):
            for l in range(leaves):
                to = target(s, l)
                if to is not None:
                    pairs.append((s * leaves + l, to[0] * leaves + to[1]))
        return lax.ppermute(value, ("sweep", "leaf"), pairs)

    def swap(value, bit):
        return permute(value, lambda s, l: (s, l ^ bit))

    def hand_on(value, section):
        return permute(value, lambda s, l: (section, l) if s == section - 1 else None)

    def gather(value, near, far):
        if not ALL_TO_ALL:
            return [value] + [swap(value, bits) for bits in (near, far, near ^ far)]
        groups = [
            [l, l ^ near, l ^ far, l ^ near ^ far]
            for l in range(leaves)
            if not l & (near | far)
        ]
        copies = jnp.broadcast_to(value[None], (4,) + value.shape)
        return lax.all_to_all(copies, "leaf", 0, 0, axis_index_groups=groups)

    x = load(source_rows, solve)
    x, *raw = lax.optimization_barrier((x, self_merge, partner_merge, front_map))
    table = prepare(*(value[0, 0] for value in raw))
    pairs = [(j, j + 1) for j in range(0, count - 1, 2)]

    front = None
    out = None
    fetched = [
        permute(
            table[low], lambda s, l, bit=2**high: (s, l ^ bit) if s > 0 else None
        )
        for low, high in pairs
    ]
    for section in range(sections):
        if section > 0:
            plane = hand_on(front, section)
            loaded = (source_rows.astype(F32) + mm(plane, plane_factor)).astype(BF)
            x = mm(loaded, solve).astype(BF)
        j = 0
        while j < count:
            if section > 0 and (j, j + 1) in pairs:
                near, far = 2**j, 2 ** (j + 1)
                place = jnp.where(leaf & near != 0, 1, 0) + jnp.where(leaf & far != 0, 2, 0)
                place = place if ALL_TO_ALL else 0 * place
                factors = pair_factors(
                    place[None].astype(jnp.int32), table[j], fetched[j // 2], table[j + 1]
                )
                x = combine(gather(x, near, far), factors)
                j += 2
                continue
            partner = swap(x, 2**j)
            own_term = lax.optimization_barrier(mm(x, table[j][0]))
            if section == 0 and sections > 1 and j == count - 1:
                own_term, fetched = lax.optimization_barrier((own_term, fetched))
            x = (own_term + mm(partner, table[j][1])).astype(BF)
            j += 1
        front = x
        out = front if out is None else jnp.where(me == section, front, out)
    return out[None, None]


def solution(mesh):
    spec = P("sweep", "leaf")
    return jax.shard_map(
        body,
        mesh=mesh,
        in_specs=(spec,) * 6,
        out_specs=spec,
        check_vma=False,
    )
```

```python
import jax
import jax.numpy as jnp
from jax import lax
from jax.experimental import pallas as pl
from jax.experimental.pallas import tpu as pltpu
from jax.sharding import PartitionSpec as P

BF = jnp.bfloat16
F32 = jnp.float32
MIB = 2**20

HBM = pl.BlockSpec(memory_space=pltpu.HBM)
VMEM = pl.BlockSpec(memory_space=pltpu.VMEM)


def mm(left, right):
    return jnp.dot(left, right, preferred_element_type=F32)


def in_hbm(value):
    return pltpu.with_memory_space_constraint(value, pltpu.HBM)


def cost(flops, moved):
    return pl.CostEstimate(flops=flops, bytes_accessed=moved, transcendentals=0)


def load_kernel(rows_hbm, solve_hbm, out_ref, rows_ref, solve_ref, sems):
    copies = [
        pltpu.make_async_copy(rows_hbm, rows_ref, sems.at[0]),
        pltpu.make_async_copy(solve_hbm, solve_ref, sems.at[1]),
    ]
    for copy in copies:
        copy.start()
    for copy in copies:
        copy.wait()
    out_ref[...] = mm(rows_ref[...], solve_ref[...]).astype(BF)


def load(rows, solve):
    return pl.pallas_call(
        load_kernel,
        out_shape=pltpu.VMEM(rows.shape, BF),
        in_specs=[HBM, HBM],
        out_specs=VMEM,
        scratch_shapes=[
            pltpu.VMEM(rows.shape, BF),
            pltpu.VMEM(solve.shape, BF),
            pltpu.SemaphoreType.DMA((2,)),
        ],
        compiler_params=pltpu.CompilerParams(vmem_limit_bytes=2 * MIB),
        cost_estimate=cost(2 * rows.size * solve.shape[1], 4 * rows.size + 2 * solve.size),
    )(in_hbm(rows), in_hbm(solve))


def prepare_kernel(groups, own_hbm, partner_hbm, map_hbm, *refs):
    count, width, _ = own_hbm.shape
    outs, refs = refs[: len(groups)], refs[len(groups) :]
    sends, refs = refs[: len(groups) - 1], refs[len(groups) - 1 :]
    partner_ref, map_ref, sems, send_sems, map_sem = refs
    map_copy = pltpu.make_async_copy(map_hbm, map_ref, map_sem)
    map_copy.start()
    slots = [(g, k) for g, group in enumerate(groups) for k in range(len(group))]
    copies = []
    for j, (g, k) in enumerate(slots):
        pair = (
            pltpu.make_async_copy(partner_hbm.at[j], partner_ref.at[j], sems.at[2 * j]),
            pltpu.make_async_copy(own_hbm.at[j], outs[g].at[2 * k], sems.at[2 * j + 1]),
        )
        for copy in pair:
            copy.start()
        copies.append(pair)
    map_copy.wait()
    rows = lax.broadcasted_iota(jnp.int32, (width, width), 0)
    pending = []
    for j, (g, k) in enumerate(slots):
        for copy in copies[j]:
            copy.wait()
        hot = (rows == map_ref[j : j + 1, :]).astype(BF)
        outs[g][2 * k + 1] = mm(hot, partner_ref[j]).astype(BF)
        if g > 0:
            both = pl.ds(2 * k, 2)
            send = pltpu.make_async_copy(outs[g].at[both], sends[g - 1].at[both], send_sems.at[j])
            send.start()
            pending.append(send)
    for send in pending:
        send.wait()


def prepare(own, partner, index_map, groups):
    count, width, _ = own.shape
    shapes = [(2 * len(group), width, width) for group in groups]
    outs = pl.pallas_call(
        lambda *refs: prepare_kernel(groups, *refs),
        out_shape=tuple(pltpu.VMEM(shape, BF) for shape in shapes)
        + tuple(pltpu.HBM(shape, BF) for shape in shapes[1:]),
        in_specs=[HBM] * 3,
        out_specs=(VMEM,) * len(groups) + (HBM,) * (len(groups) - 1),
        scratch_shapes=[
            pltpu.VMEM(partner.shape, BF),
            pltpu.VMEM(index_map.shape, jnp.int32),
            pltpu.SemaphoreType.DMA((2 * count,)),
            pltpu.SemaphoreType.DMA((count,)),
            pltpu.SemaphoreType.DMA,
        ],
        compiler_params=pltpu.CompilerParams(vmem_limit_bytes=8 * MIB),
        cost_estimate=cost(2 * count * width**3, 8 * count * width**2),
    )(in_hbm(own), in_hbm(partner), in_hbm(index_map))
    return outs[: len(groups)], outs[len(groups) :]


def body(sources, solve_tiles, self_merge, partner_merge, coupling, front_map):
    source_rows = sources[0, 0]
    solve = solve_tiles[0, 0]
    plane_factor = coupling[0, 0]
    sections = lax.axis_size("sweep")
    leaves = lax.axis_size("leaf")
    count = self_merge.shape[2]
    me = lax.axis_index("sweep")
    groups = [[0], [1], list(range(2, count))]

    def host(section):
        return min(section | 1, sections - 1)

    def twin(s):
        return s ^ 1 if (s ^ 1) < sections else s

    def permute(value, target):
        pairs = []
        for s in range(sections):
            for l in range(leaves):
                to, leaf = target(s, l)
                pairs.append((s * leaves + l, to * leaves + leaf))
        return lax.ppermute(value, ("sweep", "leaf"), pairs)

    def swap(value, row, bit):
        idle = 2 if bit == 1 else 1
        return permute(value, lambda s, l: (s, l ^ (bit if s == row else idle)))

    def cross(value, bit=0):
        return permute(value, lambda s, l: (twin(s), l ^ bit))

    x = load(source_rows, solve)
    x, *raw = lax.optimization_barrier((x, self_merge, partner_merge, front_map))
    tables, sends = prepare(*(value[0, 0] for value in raw), groups)
    moved = [None, None, cross(sends[1])]

    def factors(j, hosted):
        g, k = (j, 0) if j < 2 else (2, j - 2)
        table = (moved if hosted else tables)[g]
        return table[2 * k], table[2 * k + 1]

    results = []
    pending = None
    for section in range(sections):
        home = host(section)
        if section > 0:
            plane = front
            last = host(section - 1)
            if last != section:
                turn = {last: section, section: last}
                plane = permute(front, lambda s, l: (turn.get(s, s), l))
            loaded = (source_rows.astype(F32) + mm(plane, plane_factor)).astype(BF)
            x = mm(loaded, solve).astype(BF)
        for j in range(count):
            bit = 2**j
            if section == 0 and j == 1:
                sent, x = lax.optimization_barrier((sends[0], x))
                moved[1] = cross(sent)
            hosted = home != section and j > 0
            own, other = factors(j, hosted)
            if hosted and j == 1:
                mine, partner = cross(x), cross(x, bit)
            else:
                mine, partner = x, swap(x, home if hosted else section, bit)
            own_term = lax.optimization_barrier(mm(mine, own))
            if pending is not None and j == 1:
                back, owner = pending
                back, own_term = lax.optimization_barrier((back, own_term))
                results.append((owner, cross(back)))
                pending = None
            x = (own_term + mm(partner, other)).astype(BF)
        front = x
        if home == section:
            results.append((section, front))
        else:
            pending = (front, section)
    if pending is not None:
        results.append((pending[1], cross(pending[0])))
    out = results[0][1]
    for section, result in results[1:]:
        out = jnp.where(me == section, result, out)
    return out[None, None]


def solution(mesh):
    spec = P("sweep", "leaf")
    return jax.shard_map(
        body,
        mesh=mesh,
        in_specs=(spec,) * 6,
        out_specs=spec,
        check_vma=False,
    )
```

```python
import jax
import jax.numpy as jnp
from jax import lax
from jax.experimental import pallas as pl
from jax.experimental.pallas import tpu as pltpu
from jax.sharding import PartitionSpec as P

BF = jnp.bfloat16
F32 = jnp.float32
MIB = 2**20
PARTS = 2

HBM = pl.BlockSpec(memory_space=pltpu.HBM)
VMEM = pl.BlockSpec(memory_space=pltpu.VMEM)


def mm(left, right):
    return jnp.dot(left, right, preferred_element_type=F32)


def in_hbm(value):
    return pltpu.with_memory_space_constraint(value, pltpu.HBM)


def cost(flops, moved):
    return pl.CostEstimate(flops=flops, bytes_accessed=moved, transcendentals=0)


def load_kernel(rows_hbm, solve_hbm, out_ref, rows_ref, solve_ref, sems):
    copies = [
        pltpu.make_async_copy(rows_hbm, rows_ref, sems.at[0]),
        pltpu.make_async_copy(solve_hbm, solve_ref, sems.at[1]),
    ]
    for copy in copies:
        copy.start()
    for copy in copies:
        copy.wait()
    out_ref[...] = mm(rows_ref[...], solve_ref[...]).astype(BF)


def load(rows, solve):
    return pl.pallas_call(
        load_kernel,
        out_shape=pltpu.VMEM(rows.shape, BF),
        in_specs=[HBM, HBM],
        out_specs=VMEM,
        scratch_shapes=[
            pltpu.VMEM(rows.shape, BF),
            pltpu.VMEM(solve.shape, BF),
            pltpu.SemaphoreType.DMA((2,)),
        ],
        compiler_params=pltpu.CompilerParams(vmem_limit_bytes=2 * MIB),
        cost_estimate=cost(2 * rows.size * solve.shape[1], 4 * rows.size + 2 * solve.size),
    )(in_hbm(rows), in_hbm(solve))


def prepare_kernel(levels, kept, own_hbm, partner_hbm, map_hbm, *refs):
    number = len(levels)
    width = own_hbm.shape[1]
    outs, refs = refs[:number], refs[number:]
    sends, refs = refs[: number - kept], refs[number - kept :]
    partner_ref, map_ref, sems, send_sems, map_sem = refs
    map_copy = pltpu.make_async_copy(map_hbm, map_ref, map_sem)
    map_copy.start()
    copies = []
    for k, j in enumerate(levels):
        pair = (
            pltpu.make_async_copy(partner_hbm.at[j], partner_ref.at[k], sems.at[2 * k]),
            pltpu.make_async_copy(own_hbm.at[j], outs[k].at[0], sems.at[2 * k + 1]),
        )
        for copy in pair:
            copy.start()
        copies.append(pair)
    map_copy.wait()
    rows = lax.broadcasted_iota(jnp.int32, (width, width), 0)
    pending = []
    for k, j in enumerate(levels):
        for copy in copies[k]:
            copy.wait()
        hot = (rows == map_ref[j : j + 1, :]).astype(BF)
        outs[k][1] = mm(hot, partner_ref[k]).astype(BF)
        if k >= kept:
            send = pltpu.make_async_copy(outs[k], sends[k - kept], send_sems.at[k])
            send.start()
            pending.append(send)
    for send in pending:
        send.wait()


def prepare(own, partner, index_map, levels, kept):
    width = own.shape[1]
    number = len(levels)
    shape = (2, width, width)
    outs = pl.pallas_call(
        lambda *refs: prepare_kernel(levels, kept, *refs),
        out_shape=(pltpu.VMEM(shape, BF),) * number + (pltpu.HBM(shape, BF),) * (number - kept),
        in_specs=[HBM] * 3,
        out_specs=(VMEM,) * number + (HBM,) * (number - kept),
        scratch_shapes=[
            pltpu.VMEM((number, width, width), BF),
            pltpu.VMEM(index_map.shape, jnp.int32),
            pltpu.SemaphoreType.DMA((2 * number,)),
            pltpu.SemaphoreType.DMA((number,)),
            pltpu.SemaphoreType.DMA,
        ],
        compiler_params=pltpu.CompilerParams(vmem_limit_bytes=8 * MIB),
        cost_estimate=cost(2 * number * width**3, 8 * number * width**2),
    )(in_hbm(own), in_hbm(partner), in_hbm(index_map))
    return list(outs[:number]), list(outs[number:])


def body(sources, solve_tiles, self_merge, partner_merge, coupling, front_map):
    source_rows = sources[0, 0]
    solve = solve_tiles[0, 0]
    plane_factor = coupling[0, 0]
    sections = lax.axis_size("sweep")
    leaves = lax.axis_size("leaf")
    count = self_merge.shape[2]
    me = lax.axis_index("sweep")
    def host(section):
        return min(section | 1, sections - 1)

    def twin(s):
        return s ^ 1 if (s ^ 1) < sections else s

    def permute(value, target):
        pairs = []
        for s in range(sections):
            for l in range(leaves):
                to, leaf = target(s, l)
                pairs.append((s * leaves + l, to * leaves + leaf))
        return lax.ppermute(value, ("sweep", "leaf"), pairs)

    def swap(value, row, bit):
        idle = 2 if bit == 1 else 1
        return permute(value, lambda s, l: (s, l ^ (bit if s == row else idle)))

    def cross(value, bit=0):
        return permute(value, lambda s, l: (twin(s), l ^ bit))

    def halves(value):
        half = value.shape[0] // PARTS
        return [value[k * half : (k + 1) * half] for k in range(PARTS)]

    x = load(source_rows, solve)
    x, *raw = lax.optimization_barrier((x, self_merge, partner_merge, front_map))
    tables, sends = prepare(*(value[0, 0] for value in raw), [0, 1], 1)
    moved = [None] * count

    results = []
    pending = None
    front = None
    for section in range(sections):
        home = host(section)
        if section > 0:
            plane = front
            last = host(section - 1)
            if last != section:
                turn = {last: section, section: last}
                plane = [permute(part, lambda s, l: (turn.get(s, s), l)) for part in front]
            x = [
                mm((rows.astype(F32) + mm(part, plane_factor)).astype(BF), solve).astype(BF)
                for rows, part in zip(halves(source_rows), plane)
            ]
        else:
            x = [x]
        for j in range(count):
            bit = 2**j
            if section == 0 and j == 1:
                sent, *x = lax.optimization_barrier((sends[0], *x))
                moved[1] = cross(sent)
                x, *raw = lax.optimization_barrier((x, *raw))
                more, sends = prepare(*(v[0, 0] for v in raw), list(range(2, count)), 0)
                tables += more
                moved[2:] = [cross(sent) for sent in sends]
            hosted = home != section and j > 0
            own, other = (moved if hosted else tables)[j]
            if hosted and j == 1:
                whole = x[0] if len(x) == 1 else jnp.concatenate(x)
                mine, partner = halves(cross(whole)), halves(cross(whole, bit))
            else:
                mine = x
                partner = [swap(part, home if hosted else section, bit) for part in x]
            own_term = [lax.optimization_barrier(mm(part, own)) for part in mine]
            if pending is not None and j == 2:
                back, owner = pending
                back, own_term = lax.optimization_barrier((back, own_term))
                results.append((owner, [cross(part) for part in back]))
                pending = None
            x = [
                (term + mm(part, other)).astype(BF) for term, part in zip(own_term, partner)
            ]
        front = x if len(x) > 1 else halves(x[0])
        if home == section:
            results.append((section, front))
        else:
            pending = (front, section)
    if pending is not None:
        results.append((pending[1], [cross(part) for part in pending[0]]))
    out = results[0][1]
    for section, result in results[1:]:
        out = [jnp.where(me == section, new, old) for new, old in zip(result, out)]
    return jnp.concatenate(out)[None, None]


def solution(mesh):
    spec = P("sweep", "leaf")
    return jax.shard_map(
        body,
        mesh=mesh,
        in_specs=(spec,) * 6,
        out_specs=spec,
        check_vma=False,
    )
```

```python
import jax
import jax.numpy as jnp
from jax import lax
from jax.experimental import pallas as pl
from jax.experimental.pallas import tpu as pltpu
from jax.sharding import PartitionSpec as P

BF = jnp.bfloat16
F32 = jnp.float32
MIB = 2**20
HINT = 4 * 10**9

HBM = pl.BlockSpec(memory_space=pltpu.HBM)
VMEM = pl.BlockSpec(memory_space=pltpu.VMEM)


def mm(left, right):
    return jnp.dot(left, right, preferred_element_type=F32)


def in_hbm(value):
    return pltpu.with_memory_space_constraint(value, pltpu.HBM)


def cost(flops, moved):
    return pl.CostEstimate(flops=flops, bytes_accessed=moved, transcendentals=0)


def side():
    return lax.rem(lax.axis_index("sweep"), 2)


def call(kernel, outs, args, flops, limit=4, **more):
    moved = sum(a.size * a.dtype.itemsize for a in args) + sum(o.size * 4 for o in outs)
    return pl.pallas_call(
        kernel,
        out_shape=tuple(pltpu.VMEM(o.shape, o.dtype) for o in outs),
        in_specs=[VMEM] * len(args),
        out_specs=(VMEM,) * len(outs),
        compiler_params=pltpu.CompilerParams(vmem_limit_bytes=limit * MIB),
        cost_estimate=cost(flops, moved),
        **more,
    )(*args)


def load_kernel(rows_hbm, solve_hbm, out_ref, rows_ref, solve_ref, sems):
    copies = [
        pltpu.make_async_copy(rows_hbm, rows_ref, sems.at[0]),
        pltpu.make_async_copy(solve_hbm, solve_ref, sems.at[1]),
    ]
    for copy in copies:
        copy.start()
    for copy in copies:
        copy.wait()
    out_ref[...] = mm(rows_ref[...], solve_ref[...]).astype(BF)


def load(rows, solve):
    return pl.pallas_call(
        load_kernel,
        out_shape=pltpu.VMEM(rows.shape, BF),
        in_specs=[HBM, HBM],
        out_specs=VMEM,
        scratch_shapes=[
            pltpu.VMEM(rows.shape, BF),
            pltpu.VMEM(solve.shape, BF),
            pltpu.SemaphoreType.DMA((2,)),
        ],
        compiler_params=pltpu.CompilerParams(vmem_limit_bytes=2 * MIB),
        cost_estimate=cost(2 * rows.size * solve.shape[1], 4 * rows.size + 2 * solve.size),
    )(in_hbm(rows), in_hbm(solve))


def prepare_kernel(levels, own_hbm, partner_hbm, map_hbm, *refs):
    number = len(levels)
    width = own_hbm.shape[1]
    outs, (partner_ref, map_ref, sems, map_sem) = refs[:number], refs[number:]
    map_copy = pltpu.make_async_copy(map_hbm, map_ref, map_sem)
    map_copy.start()
    copies = []
    for k, j in enumerate(levels):
        pair = (
            pltpu.make_async_copy(partner_hbm.at[j], partner_ref.at[k], sems.at[2 * k]),
            pltpu.make_async_copy(own_hbm.at[j], outs[k].at[0], sems.at[2 * k + 1]),
        )
        for copy in pair:
            copy.start()
        copies.append(pair)
    map_copy.wait()
    rows = lax.broadcasted_iota(jnp.int32, (width, width), 0)
    for k, j in enumerate(levels):
        copies[k][0].wait()
        hot = (rows == map_ref[j : j + 1, :]).astype(BF)
        outs[k][1] = mm(hot, partner_ref[k]).astype(BF)
    for pair in copies:
        pair[1].wait()


def prepare(own, partner, index_map, levels):
    width = own.shape[1]
    number = len(levels)
    return list(
        pl.pallas_call(
            lambda *refs: prepare_kernel(levels, *refs),
            out_shape=(pltpu.VMEM((2, width, width), BF),) * number,
            in_specs=[HBM] * 3,
            out_specs=(VMEM,) * number,
            scratch_shapes=[
                pltpu.VMEM((number, width, width), BF),
                pltpu.VMEM(index_map.shape, jnp.int32),
                pltpu.SemaphoreType.DMA((2 * number,)),
                pltpu.SemaphoreType.DMA,
            ],
            compiler_params=pltpu.CompilerParams(vmem_limit_bytes=6 * MIB),
            cost_estimate=cost(2 * number * width**3, 8 * number * width**2),
        )(in_hbm(own), in_hbm(partner), in_hbm(index_map))
    )


def with_factors(parity, own_ref, other_ref, use):
    here = side() == parity
    pl.when(here)(lambda: use(own_ref))
    pl.when(jnp.logical_not(here))(lambda: use(other_ref))


def own_part(parity, rows, own, other):
    def kernel(rows_ref, own_ref, other_ref, out_ref):
        def use(table):
            out_ref[...] = mm(rows_ref[...], table[0])

        with_factors(parity, own_ref, other_ref, use)

    out = jax.ShapeDtypeStruct(rows.shape, F32)
    return call(kernel, [out], [rows, own, other], HINT // 4)[0]


def finish(parity, term, partner, own, other):
    def kernel(term_ref, partner_ref, own_ref, other_ref, out_ref):
        def use(table):
            out_ref[...] = (term_ref[...] + mm(partner_ref[...], table[1])).astype(BF)

        with_factors(parity, own_ref, other_ref, use)

    out = jax.ShapeDtypeStruct(partner.shape, BF)
    return call(kernel, [out], [term, partner, own, other], HINT)[0]


def both_parts(parity, rows, partner, own, other):
    def kernel(rows_ref, partner_ref, own_ref, other_ref, out_ref):
        def use(table):
            total = mm(rows_ref[...], table[0]) + mm(partner_ref[...], table[1])
            out_ref[...] = total.astype(BF)

        with_factors(parity, own_ref, other_ref, use)

    out = jax.ShapeDtypeStruct(rows.shape, BF)
    return call(kernel, [out], [rows, partner, own, other], HINT)[0]


def first_level(x, partner, table):
    def kernel(x_ref, partner_ref, table_ref, stay_ref, cross_ref):
        half = stay_ref.shape[0]
        total = mm(x_ref[...], table_ref[0]) + mm(partner_ref[...], table_ref[1])
        value = total.astype(BF)
        stay_ref[...] = value[:half]

        @pl.when(side() == 0)
        def _():
            cross_ref[...] = value[half:]

        @pl.when(side() == 1)
        def _():
            cross_ref[...] = x_ref[:half]

    out = jax.ShapeDtypeStruct((x.shape[0] // 2, x.shape[1]), BF)
    return call(kernel, [out, out], [x, partner, table], 4 * x.size * x.shape[1])


def second_level(stay, stay_partner, came, came_partner, own, other):
    def kernel(stay_ref, stay_partner_ref, came_ref, came_partner_ref, own_ref, other_ref, out_ref):
        @pl.when(side() == 0)
        def _():
            total = mm(stay_ref[...], own_ref[0]) + mm(stay_partner_ref[...], own_ref[1])
            out_ref[...] = total.astype(BF)

        @pl.when(side() == 1)
        def _():
            total = mm(came_ref[...], other_ref[0]) + mm(came_partner_ref[...], other_ref[1])
            out_ref[...] = total.astype(BF)

    out = jax.ShapeDtypeStruct(stay.shape, BF)
    args = [stay, stay_partner, came, came_partner, own, other]
    return call(kernel, [out], args, HINT)[0]


def pass_on(parity, front, x, came, own, other):
    def kernel(front_ref, x_ref, came_ref, own_ref, other_ref, out_ref):
        half = front_ref.shape[0]

        def known():
            mine = x_ref[parity * half : (parity + 1) * half]
            return jnp.where(side() == parity, mine.astype(F32), came_ref[...].astype(F32))

        def use(table):
            out_ref[...] = (known() + mm(front_ref[...], table[...])).astype(BF)

        with_factors(parity, own_ref, other_ref, use)

    out = jax.ShapeDtypeStruct(front.shape, BF)
    args = [front, x, came, own, other]
    return call(kernel, [out], args, HINT)[0]


def product(coupling, solve):
    def kernel(coupling_hbm, solve_hbm, out_ref, coupling_ref, solve_ref, sems):
        copies = [
            pltpu.make_async_copy(coupling_hbm, coupling_ref, sems.at[0]),
            pltpu.make_async_copy(solve_hbm, solve_ref, sems.at[1]),
        ]
        for copy in copies:
            copy.start()
        for copy in copies:
            copy.wait()
        out_ref[...] = mm(coupling_ref[...], solve_ref[...]).astype(BF)

    return pl.pallas_call(
        kernel,
        out_shape=pltpu.VMEM(coupling.shape, BF),
        in_specs=[HBM, HBM],
        out_specs=VMEM,
        scratch_shapes=[
            pltpu.VMEM(coupling.shape, BF),
            pltpu.VMEM(solve.shape, BF),
            pltpu.SemaphoreType.DMA((2,)),
        ],
        compiler_params=pltpu.CompilerParams(vmem_limit_bytes=4 * MIB),
        cost_estimate=cost(2 * solve.size * coupling.shape[0], 6 * solve.size),
    )(in_hbm(coupling), in_hbm(solve))


def choose(first, second):
    def kernel(first_ref, second_ref, out_ref):
        out_ref[...] = jnp.where(side() == 1, first_ref[...], second_ref[...])

    return call(kernel, [jax.ShapeDtypeStruct(first.shape, BF)], [first, second], 0)[0]


def assemble(even, odd, came):
    def kernel(even_ref, odd_ref, came_ref, out_ref):
        half = even_ref.shape[0]

        @pl.when(side() == 0)
        def _():
            out_ref[:half] = even_ref[...]
            out_ref[half:] = came_ref[...]

        @pl.when(side() == 1)
        def _():
            out_ref[:half] = came_ref[...]
            out_ref[half:] = odd_ref[...]

    out = jax.ShapeDtypeStruct((2 * even.shape[0], even.shape[1]), BF)
    return pl.pallas_call(
        kernel,
        out_shape=out,
        in_specs=[VMEM] * 3,
        out_specs=VMEM,
        compiler_params=pltpu.CompilerParams(vmem_limit_bytes=2 * MIB),
        cost_estimate=cost(0, 8 * even.size),
    )(even, odd, came)


def permute(value, target):
    sections, leaves = lax.axis_size("sweep"), lax.axis_size("leaf")
    pairs = []
    for s in range(sections):
        for l in range(leaves):
            to, leaf = target(s, l)
            pairs.append((s * leaves + l, to * leaves + leaf))
    return lax.ppermute(value, ("sweep", "leaf"), pairs)


def swap(value, bit):
    return permute(value, lambda s, l: (s, l ^ bit))


def cross(value, bit=0):
    return permute(value, lambda s, l: (s ^ 1, l ^ bit))


def paired(sources, solve_tiles, self_merge, partner_merge, coupling, front_map):
    solve = solve_tiles[0, 0]
    sections = lax.axis_size("sweep")
    count = self_merge.shape[2]

    x = load(sources[0, 0], solve)
    x, *raw = lax.optimization_barrier((x, self_merge, partner_merge, front_map))
    own = prepare(*(v[0, 0] for v in raw), [0, 1])
    partner = swap(x, 1)
    stay, crossing = first_level(x, partner, own[0])

    table, stay, crossing = lax.optimization_barrier((own[1], stay, crossing))
    other = [None] * count
    other[1] = cross(table)
    came = cross(crossing)
    came_partner = cross(crossing, 2)
    stay_partner = swap(stay, 2)
    stay, raw[0], raw[1], raw[2], plane_factor = lax.optimization_barrier((stay, *raw, coupling))
    own += prepare(*(v[0, 0] for v in raw), list(range(2, count)))
    x_rows = second_level(stay, stay_partner, came, came_partner, own[1], other[1])

    def behind(rows, *values):
        rows, *values = lax.optimization_barrier((rows, *values))
        return rows, values

    even = odd = None
    received = came
    if sections > 2:
        received = cross(choose(x[: x.shape[0] // 2], x[x.shape[0] // 2 :]))
    for section in range(sections):
        parity = section % 2
        if section > 0:
            if parity == 0:
                turn = {section - 2: section, section - 1: section + 1}
                turn |= {to: s for s, to in turn.items()}
                front = permute(front, lambda s, l: (turn.get(s, s), l))
            if section == 1 and count < 4:
                own_link = product(plane_factor[0, 0], solve)
                other_link, other[0] = cross(own_link), cross(own[0])
            x_rows = pass_on(parity, front, x, received, own_link, other_link)
        for j in range(2 if section == 0 else 0, count):
            if section == 0:
                x_rows, late = behind(x_rows, own[j])
                other[j] = cross(late[0])
            partner = swap(x_rows, 2**j)
            if section == 0 and j == 2 and count > 3:
                x_rows = both_parts(parity, x_rows, partner, own[j], other[j])
                x_rows, late = behind(x_rows, plane_factor)
                own_link = product(late[0][0, 0], solve)
                continue
            term = own_part(parity, x_rows, own[j], other[j])
            if section == 0 and j == 3:
                term, late = behind(term, own_link, own[0])
                other_link, other[0] = cross(late[0]), cross(late[1])
            x_rows = finish(parity, term, partner, own[j], other[j])
        front = x_rows
        if section < 2:
            even, odd = (front, odd) if parity == 0 else (even, front)
        else:
            here = lax.axis_index("sweep") // 2 == section // 2
            if parity == 0:
                even = jnp.where(here, front, even)
            else:
                odd = jnp.where(here, front, odd)
    came = cross(choose(even, odd))
    return assemble(even, odd, came)[None, None]


def single(sources, solve_tiles, self_merge, partner_merge, coupling, front_map):
    rows, solve, link = sources[0, 0], solve_tiles[0, 0], coupling[0, 0]
    sections = lax.axis_size("sweep")
    front = jnp.zeros_like(rows)
    for section in range(sections):
        front = permute(front, lambda s, l: ((s + 1) % sections, l))
        front = jnp.where(lax.axis_index("sweep") == 0, jnp.zeros_like(front), front)
        x = mm((rows.astype(F32) + mm(front, link)).astype(BF), solve).astype(BF)
        for j in range(self_merge.shape[2]):
            mapped = jnp.take(swap(x, 2**j), front_map[0, 0, j], axis=1)
            x = (mm(x, self_merge[0, 0, j]) + mm(mapped, partner_merge[0, 0, j])).astype(BF)
        front = x
    return front[None, None]


def solution(mesh):
    spec = P("sweep", "leaf")
    return jax.shard_map(
        paired if mesh.shape["sweep"] % 2 == 0 else single,
        mesh=mesh,
        in_specs=(spec,) * 6,
        out_specs=spec,
        check_vma=False,
    )
```

```python
import jax
import jax.numpy as jnp
from jax import lax
from jax.experimental import pallas as pl
from jax.experimental.pallas import tpu as pltpu
from jax.sharding import PartitionSpec as P

BF = jnp.bfloat16
F32 = jnp.float32
MIB = 2**20
HINT = 4 * 10**9

HBM = pl.BlockSpec(memory_space=pltpu.HBM)
VMEM = pl.BlockSpec(memory_space=pltpu.VMEM)


def mm(left, right):
    return jnp.dot(left, right, preferred_element_type=F32)


def in_hbm(value):
    return pltpu.with_memory_space_constraint(value, pltpu.HBM)


def cost(flops, moved):
    return pl.CostEstimate(flops=flops, bytes_accessed=moved, transcendentals=0)


def side():
    return lax.rem(lax.axis_index("sweep"), 2)


def call(kernel, outs, args, flops, limit=4, **more):
    moved = sum(a.size * a.dtype.itemsize for a in args) + sum(o.size * 4 for o in outs)
    return pl.pallas_call(
        kernel,
        out_shape=tuple(pltpu.VMEM(o.shape, o.dtype) for o in outs),
        in_specs=[VMEM] * len(args),
        out_specs=(VMEM,) * len(outs),
        compiler_params=pltpu.CompilerParams(vmem_limit_bytes=limit * MIB),
        cost_estimate=cost(flops, moved),
        **more,
    )(*args)


def load_kernel(rows_hbm, solve_hbm, out_ref, rows_ref, solve_ref, sems):
    copies = [
        pltpu.make_async_copy(rows_hbm, rows_ref, sems.at[0]),
        pltpu.make_async_copy(solve_hbm, solve_ref, sems.at[1]),
    ]
    for copy in copies:
        copy.start()
    for copy in copies:
        copy.wait()
    out_ref[...] = mm(rows_ref[...], solve_ref[...]).astype(BF)


def load(rows, solve):
    return pl.pallas_call(
        load_kernel,
        out_shape=pltpu.VMEM(rows.shape, BF),
        in_specs=[HBM, HBM],
        out_specs=VMEM,
        scratch_shapes=[
            pltpu.VMEM(rows.shape, BF),
            pltpu.VMEM(solve.shape, BF),
            pltpu.SemaphoreType.DMA((2,)),
        ],
        compiler_params=pltpu.CompilerParams(vmem_limit_bytes=2 * MIB),
        cost_estimate=cost(2 * rows.size * solve.shape[1], 4 * rows.size + 2 * solve.size),
    )(in_hbm(rows), in_hbm(solve))


def prepare_kernel(levels, single, link, own_hbm, partner_hbm, map_hbm, *refs):
    number = len(levels)
    width = own_hbm.shape[1]
    link_hbm, refs = refs[: 2 * link], refs[2 * link :]
    outs, refs = refs[:number], refs[number:]
    singles, refs = refs[: 2 * single], refs[2 * single :]
    products, (partner_ref, map_ref, link_ref, sems, map_sem) = refs[:link], refs[link:]
    map_copy = pltpu.make_async_copy(map_hbm, map_ref, map_sem)
    map_copy.start()
    copies = []
    for k, j in enumerate(levels):
        pair = (
            pltpu.make_async_copy(partner_hbm.at[j], partner_ref.at[k], sems.at[2 * k]),
            pltpu.make_async_copy(own_hbm.at[j], outs[k].at[0], sems.at[2 * k + 1]),
        )
        for copy in pair:
            copy.start()
        copies.append(pair)
    extra = []
    if single:
        extra.append((own_hbm.at[levels[0]], singles[0]))
    for k, source in enumerate(link_hbm):
        extra.append((source, link_ref.at[k]))
    extra = [
        pltpu.make_async_copy(source, target, sems.at[2 * number + k])
        for k, (source, target) in enumerate(extra)
    ]
    for copy in extra:
        copy.start()
    map_copy.wait()
    rows = lax.broadcasted_iota(jnp.int32, (width, width), 0)
    for k, j in enumerate(levels):
        copies[k][0].wait()
        hot = (rows == map_ref[j : j + 1, :]).astype(BF)
        folded = mm(hot, partner_ref[k]).astype(BF)
        outs[k][1] = folded
        if single and k == 0:
            singles[1][...] = folded
    for copy in extra:
        copy.wait()
    if link:
        products[0][...] = mm(link_ref[0], link_ref[1]).astype(BF)
    for pair in copies:
        pair[1].wait()


def prepare(own, partner, index_map, levels, single=0, link=()):
    width = own.shape[1]
    number = len(levels)
    more = len(link) // 2
    outs = pl.pallas_call(
        lambda *refs: prepare_kernel(levels, single, more, *refs),
        out_shape=(pltpu.VMEM((2, width, width), BF),) * number
        + (pltpu.VMEM((width, width), BF),) * (2 * single + more),
        in_specs=[HBM] * (3 + len(link)),
        out_specs=(VMEM,) * (number + 2 * single + more),
        scratch_shapes=[
            pltpu.VMEM((number, width, width), BF),
            pltpu.VMEM(index_map.shape, jnp.int32),
            pltpu.VMEM((2, width, width), BF),
            pltpu.SemaphoreType.DMA((2 * number + 2,)),
            pltpu.SemaphoreType.DMA,
        ],
        compiler_params=pltpu.CompilerParams(vmem_limit_bytes=8 * MIB),
        cost_estimate=cost(2 * number * width**3, 8 * number * width**2),
    )(*(in_hbm(value) for value in (own, partner, index_map, *link)))
    return list(outs[:number]), list(outs[number:])


def with_factors(parity, own_ref, other_ref, use):
    here = side() == parity
    pl.when(here)(lambda: use(own_ref))
    pl.when(jnp.logical_not(here))(lambda: use(other_ref))


def own_part(parity, rows, own, other):
    def kernel(rows_ref, own_ref, other_ref, out_ref):
        def use(table):
            out_ref[...] = mm(rows_ref[...], table[0])

        with_factors(parity, own_ref, other_ref, use)

    out = jax.ShapeDtypeStruct(rows.shape, F32)
    return call(kernel, [out], [rows, own, other], HINT // 4)[0]


def finish(parity, term, partner, own, other):
    def kernel(term_ref, partner_ref, own_ref, other_ref, out_ref):
        def use(table):
            out_ref[...] = (term_ref[...] + mm(partner_ref[...], table[1])).astype(BF)

        with_factors(parity, own_ref, other_ref, use)

    out = jax.ShapeDtypeStruct(partner.shape, BF)
    return call(kernel, [out], [term, partner, own, other], HINT)[0]


def both_parts(parity, rows, partner, own, other):
    def kernel(rows_ref, partner_ref, own_ref, other_ref, out_ref):
        def use(table):
            total = mm(rows_ref[...], table[0]) + mm(partner_ref[...], table[1])
            out_ref[...] = total.astype(BF)

        with_factors(parity, own_ref, other_ref, use)

    out = jax.ShapeDtypeStruct(rows.shape, BF)
    return call(kernel, [out], [rows, partner, own, other], HINT)[0]


def first_level(x, partner, table):
    def kernel(x_ref, partner_ref, table_ref, stay_ref, cross_ref):
        half = stay_ref.shape[0]
        total = mm(x_ref[...], table_ref[0]) + mm(partner_ref[...], table_ref[1])
        value = total.astype(BF)
        stay_ref[...] = value[:half]

        @pl.when(side() == 0)
        def _():
            cross_ref[...] = value[half:]

        @pl.when(side() == 1)
        def _():
            cross_ref[...] = x_ref[:half]

    out = jax.ShapeDtypeStruct((x.shape[0] // 2, x.shape[1]), BF)
    return call(kernel, [out, out], [x, partner, table], 4 * x.size * x.shape[1])


def second_level(stay, stay_partner, came, came_partner, own, other):
    def kernel(stay_ref, stay_partner_ref, came_ref, came_partner_ref, own_ref, other_ref, out_ref):
        @pl.when(side() == 0)
        def _():
            total = mm(stay_ref[...], own_ref[0]) + mm(stay_partner_ref[...], own_ref[1])
            out_ref[...] = total.astype(BF)

        @pl.when(side() == 1)
        def _():
            total = mm(came_ref[...], other_ref[0]) + mm(came_partner_ref[...], other_ref[1])
            out_ref[...] = total.astype(BF)

    out = jax.ShapeDtypeStruct(stay.shape, BF)
    args = [stay, stay_partner, came, came_partner, own, other]
    return call(kernel, [out], args, HINT)[0]


def pass_on(parity, front, x, came, own, other):
    def kernel(front_ref, x_ref, came_ref, own_ref, other_ref, out_ref):
        half = front_ref.shape[0]

        def known():
            mine = x_ref[parity * half : (parity + 1) * half]
            return jnp.where(side() == parity, mine.astype(F32), came_ref[...].astype(F32))

        def use(table):
            out_ref[...] = (known() + mm(front_ref[...], table[...])).astype(BF)

        with_factors(parity, own_ref, other_ref, use)

    out = jax.ShapeDtypeStruct(front.shape, BF)
    args = [front, x, came, own, other]
    return call(kernel, [out], args, HINT)[0]


def merged_levels(x, partners, tables, others, far, far_other):
    def kernel(x_ref, *refs):
        (near_ref, far_x_ref, far_near_ref), refs = refs[:3], refs[3:]
        out_ref = refs[-1]

        def use(low, high, far_own, far_partner):
            mine = mm(x_ref[...], low[0]) + mm(near_ref[...], low[1])
            sibling = mm(far_x_ref[...], far_own[...]) + mm(far_near_ref[...], far_partner[...])
            total = mm(mine.astype(BF), high[0]) + mm(sibling.astype(BF), high[1])
            out_ref[...] = total.astype(BF)

        here = side() == 1
        pl.when(here)(lambda: use(*refs[0:4]))
        pl.when(jnp.logical_not(here))(lambda: use(*refs[4:8]))

    out = jax.ShapeDtypeStruct(x.shape, BF)
    args = [x, *partners, *tables, *far, *others, *far_other]
    return call(kernel, [out], args, HINT)[0]


def choose(first, second):
    def kernel(first_ref, second_ref, out_ref):
        out_ref[...] = jnp.where(side() == 1, first_ref[...], second_ref[...])

    return call(kernel, [jax.ShapeDtypeStruct(first.shape, BF)], [first, second], 0)[0]


def assemble(even, odd, came):
    def kernel(even_ref, odd_ref, came_ref, out_ref):
        half = even_ref.shape[0]

        @pl.when(side() == 0)
        def _():
            out_ref[:half] = even_ref[...]
            out_ref[half:] = came_ref[...]

        @pl.when(side() == 1)
        def _():
            out_ref[:half] = came_ref[...]
            out_ref[half:] = odd_ref[...]

    out = jax.ShapeDtypeStruct((2 * even.shape[0], even.shape[1]), BF)
    return pl.pallas_call(
        kernel,
        out_shape=out,
        in_specs=[VMEM] * 3,
        out_specs=VMEM,
        compiler_params=pltpu.CompilerParams(vmem_limit_bytes=2 * MIB),
        cost_estimate=cost(0, 8 * even.size),
    )(even, odd, came)


def permute(value, target):
    sections, leaves = lax.axis_size("sweep"), lax.axis_size("leaf")
    pairs = []
    for s in range(sections):
        for l in range(leaves):
            to = target(s, l)
            if to is not None:
                pairs.append((s * leaves + l, to[0] * leaves + to[1]))
    return lax.ppermute(value, ("sweep", "leaf"), pairs)


def swap(value, bit):
    return permute(value, lambda s, l: (s, l ^ bit))


def cross(value, bit=0):
    return permute(value, lambda s, l: (s ^ 1, l ^ bit))


def paired(sources, solve_tiles, self_merge, partner_merge, coupling, front_map):
    solve = solve_tiles[0, 0]
    sections = lax.axis_size("sweep")
    count = self_merge.shape[2]

    def behind(rows, *values):
        rows, *values = lax.optimization_barrier((rows, *values))
        return rows, values

    x = load(sources[0, 0], solve)
    x, *raw = lax.optimization_barrier((x, self_merge, partner_merge, front_map))
    own, low = prepare(*(v[0, 0] for v in raw), [0, 1], 1)
    partner = swap(x, 1)
    stay, crossing = first_level(x, partner, own[0])

    stay, (crossing, high, low[0]) = behind(stay, crossing, own[1], low[0])
    other = [None] * count
    other[1] = cross(high)

    def fetch(table):
        return permute(table, lambda s, l: (s, l ^ (1 + s % 2)))

    far = [fetch(low[0])]
    far_other = []
    came = cross(crossing)
    came_partner = cross(crossing, 2)
    stay_partner = swap(stay, 2)
    stay, raw[0], raw[1], raw[2], plane_factor = lax.optimization_barrier((stay, *raw, coupling))
    more, (own_link,) = prepare(
        *(v[0, 0] for v in raw), list(range(2, count)), link=(plane_factor[0, 0], solve)
    )
    own += more
    x_rows = second_level(stay, stay_partner, came, came_partner, own[1], other[1])

    even = odd = other_link = None
    received = came
    if sections > 2:
        received = cross(choose(x[: x.shape[0] // 2], x[x.shape[0] // 2 :]))
    for section in range(sections):
        parity = section % 2
        if section > 0:
            if parity == 0:
                turn = {section - 2: section, section - 1: section + 1}
                turn |= {to: s for s, to in turn.items()}
                front = permute(front, lambda s, l: (turn.get(s, s), l))
            x_rows = pass_on(parity, front, x, received, own_link, other_link)
        first = 2 if section == 0 or parity == 1 else 0
        if parity == 1:
            if section == 1:
                x_rows, (other[0], *far_other) = behind(x_rows, other[0], *far_other)
            partners = [swap(x_rows, bits) for bits in (1, 2, 3)]
            x_rows = merged_levels(x_rows, partners, own[:2], other[:2], far, far_other)
        for j in range(first, count):
            if section == 0:
                x_rows, (table, far[j - 2]) = behind(x_rows, own[j], far[j - 2])
                other[j] = cross(table)
                if j == 2:
                    x_rows, (low[1],) = behind(x_rows, low[1])
                    far.append(fetch(low[1]))
                if j == 3:
                    x_rows, (own_link,) = behind(x_rows, own_link)
                    other_link = cross(own_link)
            partner = swap(x_rows, 2**j)
            if section == 0 and j == 2 and count > 3:
                x_rows = both_parts(parity, x_rows, partner, own[j], other[j])
                continue
            term = own_part(parity, x_rows, own[j], other[j])
            if section == 0 and j == 3:
                term, (table, *far) = behind(term, own[0], *far)
                other[0], far_other = cross(table), [cross(one) for one in far]
            x_rows = finish(parity, term, partner, own[j], other[j])
        front = x_rows
        if section < 2:
            even, odd = (front, odd) if parity == 0 else (even, front)
        else:
            here = lax.axis_index("sweep") // 2 == section // 2
            if parity == 0:
                even = jnp.where(here, front, even)
            else:
                odd = jnp.where(here, front, odd)
    came = cross(choose(even, odd))
    return assemble(even, odd, came)[None, None]


def single(sources, solve_tiles, self_merge, partner_merge, coupling, front_map):
    rows, solve, link = sources[0, 0], solve_tiles[0, 0], coupling[0, 0]
    sections = lax.axis_size("sweep")
    front = jnp.zeros_like(rows)
    for section in range(sections):
        front = permute(front, lambda s, l: ((s + 1) % sections, l))
        front = jnp.where(lax.axis_index("sweep") == 0, jnp.zeros_like(front), front)
        x = mm((rows.astype(F32) + mm(front, link)).astype(BF), solve).astype(BF)
        for j in range(self_merge.shape[2]):
            mapped = jnp.take(swap(x, 2**j), front_map[0, 0, j], axis=1)
            x = (mm(x, self_merge[0, 0, j]) + mm(mapped, partner_merge[0, 0, j])).astype(BF)
        front = x
    return front[None, None]


def solution(mesh):
    spec = P("sweep", "leaf")
    return jax.shard_map(
        paired if mesh.shape["sweep"] % 2 == 0 else single,
        mesh=mesh,
        in_specs=(spec,) * 6,
        out_specs=spec,
        check_vma=False,
    )
```

```python
import jax
import jax.numpy as jnp
from jax import lax
from jax.experimental import pallas as pl
from jax.experimental.pallas import tpu as pltpu
from jax.sharding import PartitionSpec as P

BF = jnp.bfloat16
F32 = jnp.float32
MIB = 2**20
HINT = 10**8

HBM = pl.BlockSpec(memory_space=pltpu.HBM)
VMEM = pl.BlockSpec(memory_space=pltpu.VMEM)


def mm(left, right):
    return jnp.dot(left, right, preferred_element_type=F32)


def in_hbm(value):
    return pltpu.with_memory_space_constraint(value, pltpu.HBM)


def cost(flops, moved):
    return pl.CostEstimate(flops=flops, bytes_accessed=moved, transcendentals=0)


def side():
    return lax.rem(lax.axis_index("sweep"), 2)


def call(kernel, outs, args, flops, limit=4, **more):
    moved = sum(a.size * a.dtype.itemsize for a in args) + sum(o.size * 4 for o in outs)
    return pl.pallas_call(
        kernel,
        out_shape=tuple(pltpu.VMEM(o.shape, o.dtype) for o in outs),
        in_specs=[VMEM] * len(args),
        out_specs=(VMEM,) * len(outs),
        compiler_params=pltpu.CompilerParams(vmem_limit_bytes=limit * MIB),
        cost_estimate=cost(flops, moved),
        **more,
    )(*args)


def load_kernel(rows_hbm, solve_hbm, out_ref, rows_ref, solve_ref, sems):
    copies = [
        pltpu.make_async_copy(rows_hbm, rows_ref, sems.at[0]),
        pltpu.make_async_copy(solve_hbm, solve_ref, sems.at[1]),
    ]
    for copy in copies:
        copy.start()
    for copy in copies:
        copy.wait()
    out_ref[...] = mm(rows_ref[...], solve_ref[...]).astype(BF)


def load(rows, solve):
    return pl.pallas_call(
        load_kernel,
        out_shape=pltpu.VMEM(rows.shape, BF),
        in_specs=[HBM, HBM],
        out_specs=VMEM,
        scratch_shapes=[
            pltpu.VMEM(rows.shape, BF),
            pltpu.VMEM(solve.shape, BF),
            pltpu.SemaphoreType.DMA((2,)),
        ],
        compiler_params=pltpu.CompilerParams(vmem_limit_bytes=2 * MIB),
        cost_estimate=cost(2 * rows.size * solve.shape[1], 4 * rows.size + 2 * solve.size),
    )(in_hbm(rows), in_hbm(solve))


def prepare_kernel(levels, single, link, own_hbm, partner_hbm, map_hbm, *refs):
    number = len(levels)
    width = own_hbm.shape[1]
    link_hbm, refs = refs[: 2 * link], refs[2 * link :]
    outs, refs = refs[:number], refs[number:]
    singles, refs = refs[: 2 * single], refs[2 * single :]
    products, (partner_ref, map_ref, link_ref, sems, map_sem) = refs[:link], refs[link:]
    map_copy = pltpu.make_async_copy(map_hbm, map_ref, map_sem)
    map_copy.start()
    copies = []
    for k, j in enumerate(levels):
        pair = (
            pltpu.make_async_copy(partner_hbm.at[j], partner_ref.at[k], sems.at[2 * k]),
            pltpu.make_async_copy(own_hbm.at[j], outs[k].at[0], sems.at[2 * k + 1]),
        )
        for copy in pair:
            copy.start()
        copies.append(pair)
    extra = []
    if single:
        extra.append((own_hbm.at[levels[0]], singles[0]))
    for k, source in enumerate(link_hbm):
        extra.append((source, link_ref.at[k]))
    extra = [
        pltpu.make_async_copy(source, target, sems.at[2 * number + k])
        for k, (source, target) in enumerate(extra)
    ]
    for copy in extra:
        copy.start()
    map_copy.wait()
    rows = lax.broadcasted_iota(jnp.int32, (width, width), 0)
    for k, j in enumerate(levels):
        copies[k][0].wait()
        hot = (rows == map_ref[j : j + 1, :]).astype(BF)
        folded = mm(hot, partner_ref[k]).astype(BF)
        outs[k][1] = folded
        if single and k == 0:
            singles[1][...] = folded
    for copy in extra:
        copy.wait()
    if link:
        products[0][...] = mm(link_ref[0], link_ref[1]).astype(BF)
    for pair in copies:
        pair[1].wait()


def prepare(own, partner, index_map, levels, single=0, link=()):
    width = own.shape[1]
    number = len(levels)
    more = len(link) // 2
    outs = pl.pallas_call(
        lambda *refs: prepare_kernel(levels, single, more, *refs),
        out_shape=(pltpu.VMEM((2, width, width), BF),) * number
        + (pltpu.VMEM((width, width), BF),) * (2 * single + more),
        in_specs=[HBM] * (3 + len(link)),
        out_specs=(VMEM,) * (number + 2 * single + more),
        scratch_shapes=[
            pltpu.VMEM((number, width, width), BF),
            pltpu.VMEM(index_map.shape, jnp.int32),
            pltpu.VMEM((2, width, width), BF),
            pltpu.SemaphoreType.DMA((2 * number + 2,)),
            pltpu.SemaphoreType.DMA,
        ],
        compiler_params=pltpu.CompilerParams(vmem_limit_bytes=8 * MIB),
        cost_estimate=cost(2 * number * width**3, 8 * number * width**2),
    )(*(in_hbm(value) for value in (own, partner, index_map, *link)))
    return list(outs[:number]), list(outs[number:])


def own_part(which, rows, table):
    def kernel(rows_ref, table_ref, out_ref):
        @pl.when(side() == which)
        def _():
            out_ref[...] = mm(rows_ref[...], table_ref[0])

    return call(kernel, [jax.ShapeDtypeStruct(rows.shape, F32)], [rows, table], HINT // 4)[0]


def finish(which, term, partner, table):
    def kernel(term_ref, partner_ref, table_ref, out_ref):
        @pl.when(side() == which)
        def _():
            out_ref[...] = (term_ref[...] + mm(partner_ref[...], table_ref[1])).astype(BF)

    out = jax.ShapeDtypeStruct(partner.shape, BF)
    return call(kernel, [out], [term, partner, table], HINT)[0]


def both_parts(which, rows, partner, table, start, count):
    def kernel(rows_ref, partner_ref, table_ref, out_ref):
        @pl.when(side() == which)
        def _():
            block = slice(start, start + count)
            total = mm(rows_ref[block], table_ref[0]) + mm(partner_ref[block], table_ref[1])
            out_ref[...] = total.astype(BF)

    out = jax.ShapeDtypeStruct((count, rows.shape[1]), BF)
    return call(kernel, [out], [rows, partner, table], HINT)[0]


def pass_on(which, front, x, link, start):
    count = front.shape[0]

    def kernel(front_ref, x_ref, link_ref, out_ref):
        @pl.when(side() == which)
        def _():
            known = x_ref[start : start + count].astype(F32)
            out_ref[...] = (known + mm(front_ref[...], link_ref[...])).astype(BF)

    return call(kernel, [jax.ShapeDtypeStruct(front.shape, BF)], [front, x, link], HINT)[0]


def assemble(even, odd):
    half = even[0].shape[0]

    def kernel(even_first, even_second, odd_first, odd_second, out_ref):
        @pl.when(side() == 0)
        def _():
            out_ref[:half] = even_first[...]
            out_ref[half:] = even_second[...]

        @pl.when(side() == 1)
        def _():
            out_ref[:half] = odd_first[...]
            out_ref[half:] = odd_second[...]

    return pl.pallas_call(
        kernel,
        out_shape=jax.ShapeDtypeStruct((2 * half, even[0].shape[1]), BF),
        in_specs=[VMEM] * 4,
        out_specs=VMEM,
        compiler_params=pltpu.CompilerParams(vmem_limit_bytes=2 * MIB),
        cost_estimate=cost(0, 12 * even[0].size),
    )(*even, *odd)


def permute(value, target):
    sections, leaves = lax.axis_size("sweep"), lax.axis_size("leaf")
    pairs = []
    for s in range(sections):
        for l in range(leaves):
            to = target(s, l)
            if to is not None:
                pairs.append((s * leaves + l, to[0] * leaves + to[1]))
    return lax.ppermute(value, ("sweep", "leaf"), pairs)


def swap(value, bit, row=None):
    idle = 2 if bit == 1 else 1
    return permute(value, lambda s, l: (s, l ^ (bit if row in (None, s) else idle)))


def cross(value, bit=0):
    return permute(value, lambda s, l: (s ^ 1, l ^ bit))


def behind(rows, *values):
    rows, *values = lax.optimization_barrier((rows, *values))
    return rows, values


def paired(sources, solve_tiles, self_merge, partner_merge, coupling, front_map):
    solve = solve_tiles[0, 0]
    sections = lax.axis_size("sweep")
    count = self_merge.shape[2]

    x = load(sources[0, 0], solve)
    half = x.shape[0] // 2
    rows, raw = behind(x, self_merge, partner_merge, front_map, coupling)
    own = prepare(*(v[0, 0] for v in raw[:3]), [0, 1])[0]
    other = [None] * count
    own_link = None
    front = None
    even, odd = [], []
    back = None
    for section in range(sections):
        if section % 2 == 0:
            if section > 0:
                turn = {section - 1: section, section: section - 1}
                front = [permute(part, lambda s, l: (turn.get(s, s), l)) for part in front]
                rows = [pass_on(0, part, x, own_link, k * half) for k, part in enumerate(front)]
                rows = jnp.concatenate(rows)
            rows = both_parts(0, rows, swap(rows, 1, section), own[0], 0, 2 * half)
            if section == 0:
                rows, (table,) = behind(rows, own[1])
                other[1] = cross(table)
            came = cross(rows)
            partner = cross(rows, 2)
            if section == 0:
                _, raw = behind(rows, *raw)
                more, (own_link,) = prepare(
                    *(v[0, 0] for v in raw[:3]),
                    list(range(2, count)),
                    link=(raw[3][0, 0], solve),
                )
                own += more
            front = [both_parts(1, came, partner, other[1], k * half, half) for k in range(2)]
            first, tables, row = 2, other, section + 1
        else:
            front = [pass_on(1, part, x, own_link, k * half) for k, part in enumerate(front)]
            first, tables, row = 0, own, section
        for j in range(first, count):
            if section == 0 and j == 2:
                first, (second, *late) = behind(*front, *own[2:])
                front = [first, second]
                other[2:] = [cross(table) for table in late]
            partners = [swap(part, 2**j, row) for part in front]
            terms = [own_part(1, part, tables[j]) for part in front]
            if section % 2 and j == 1:
                terms[1], back = behind(terms[1], *back)
                back = [cross(part) for part in back]
            front = [finish(1, term, part, tables[j]) for term, part in zip(terms, partners)]
        if section % 2 == 0:
            back = front
        elif section == 1:
            even, odd = back, front
        else:
            chosen = lax.axis_index("sweep") // 2 == section // 2
            even = [jnp.where(chosen, new, old) for new, old in zip(back, even)]
            odd = [jnp.where(chosen, new, old) for new, old in zip(front, odd)]
    return assemble(even, odd)[None, None]


def single(sources, solve_tiles, self_merge, partner_merge, coupling, front_map):
    rows, solve, link = sources[0, 0], solve_tiles[0, 0], coupling[0, 0]
    sections = lax.axis_size("sweep")
    front = jnp.zeros_like(rows)
    for section in range(sections):
        front = permute(front, lambda s, l: ((s + 1) % sections, l))
        front = jnp.where(lax.axis_index("sweep") == 0, jnp.zeros_like(front), front)
        x = mm((rows.astype(F32) + mm(front, link)).astype(BF), solve).astype(BF)
        for j in range(self_merge.shape[2]):
            mapped = jnp.take(swap(x, 2**j), front_map[0, 0, j], axis=1)
            x = (mm(x, self_merge[0, 0, j]) + mm(mapped, partner_merge[0, 0, j])).astype(BF)
        front = x
    return front[None, None]


def solution(mesh):
    spec = P("sweep", "leaf")
    return jax.shard_map(
        paired if mesh.shape["sweep"] % 2 == 0 else single,
        mesh=mesh,
        in_specs=(spec,) * 6,
        out_specs=spec,
        check_vma=False,
    )
```

```python
import jax
import jax.numpy as jnp
from jax import lax
from jax.experimental import pallas as pl
from jax.experimental.pallas import tpu as pltpu
from jax.sharding import PartitionSpec as P

BF = jnp.bfloat16
F32 = jnp.float32
MIB = 2**20
HINT = 10**8

HBM = pl.BlockSpec(memory_space=pltpu.HBM)
VMEM = pl.BlockSpec(memory_space=pltpu.VMEM)


def mm(left, right):
    return jnp.dot(left, right, preferred_element_type=F32)


def in_hbm(value):
    return pltpu.with_memory_space_constraint(value, pltpu.HBM)


def cost(flops, moved):
    return pl.CostEstimate(flops=flops, bytes_accessed=moved, transcendentals=0)


def side():
    return lax.rem(lax.axis_index("sweep"), 2)


def call(kernel, outs, args, flops, limit=4, **more):
    moved = sum(a.size * a.dtype.itemsize for a in args) + sum(o.size * 4 for o in outs)
    return pl.pallas_call(
        kernel,
        out_shape=tuple(pltpu.VMEM(o.shape, o.dtype) for o in outs),
        in_specs=[VMEM] * len(args),
        out_specs=(VMEM,) * len(outs),
        compiler_params=pltpu.CompilerParams(vmem_limit_bytes=limit * MIB),
        cost_estimate=cost(flops, moved),
        **more,
    )(*args)


def load_kernel(rows_hbm, solve_hbm, out_ref, rows_ref, solve_ref, sems):
    copies = [
        pltpu.make_async_copy(rows_hbm, rows_ref, sems.at[0]),
        pltpu.make_async_copy(solve_hbm, solve_ref, sems.at[1]),
    ]
    for copy in copies:
        copy.start()
    for copy in copies:
        copy.wait()
    out_ref[...] = mm(rows_ref[...], solve_ref[...]).astype(BF)


def load(rows, solve):
    return pl.pallas_call(
        load_kernel,
        out_shape=pltpu.VMEM(rows.shape, BF),
        in_specs=[HBM, HBM],
        out_specs=VMEM,
        scratch_shapes=[
            pltpu.VMEM(rows.shape, BF),
            pltpu.VMEM(solve.shape, BF),
            pltpu.SemaphoreType.DMA((2,)),
        ],
        compiler_params=pltpu.CompilerParams(vmem_limit_bytes=2 * MIB),
        cost_estimate=cost(2 * rows.size * solve.shape[1], 4 * rows.size + 2 * solve.size),
    )(in_hbm(rows), in_hbm(solve))


def prepare_kernel(levels, single, link, own_hbm, partner_hbm, map_hbm, *refs):
    number = len(levels)
    width = own_hbm.shape[1]
    link_hbm, refs = refs[: 2 * link], refs[2 * link :]
    outs, refs = refs[:number], refs[number:]
    singles, refs = refs[: 2 * single], refs[2 * single :]
    products, (partner_ref, map_ref, link_ref, sems, map_sem) = refs[:link], refs[link:]
    map_copy = pltpu.make_async_copy(map_hbm, map_ref, map_sem)
    map_copy.start()
    copies = []
    for k, j in enumerate(levels):
        pair = (
            pltpu.make_async_copy(partner_hbm.at[j], partner_ref.at[k], sems.at[2 * k]),
            pltpu.make_async_copy(own_hbm.at[j], outs[k].at[0], sems.at[2 * k + 1]),
        )
        for copy in pair:
            copy.start()
        copies.append(pair)
    extra = []
    if single:
        extra.append((own_hbm.at[levels[0]], singles[0]))
    for k, source in enumerate(link_hbm):
        extra.append((source, link_ref.at[k]))
    extra = [
        pltpu.make_async_copy(source, target, sems.at[2 * number + k])
        for k, (source, target) in enumerate(extra)
    ]
    for copy in extra:
        copy.start()
    map_copy.wait()
    rows = lax.broadcasted_iota(jnp.int32, (width, width), 0)
    for k, j in enumerate(levels):
        copies[k][0].wait()
        hot = (rows == map_ref[j : j + 1, :]).astype(BF)
        folded = mm(hot, partner_ref[k]).astype(BF)
        outs[k][1] = folded
        if single and k == 0:
            singles[1][...] = folded
    for copy in extra:
        copy.wait()
    if link:
        products[0][...] = mm(link_ref[0], link_ref[1]).astype(BF)
    for pair in copies:
        pair[1].wait()


def prepare(own, partner, index_map, levels, single=0, link=()):
    width = own.shape[1]
    number = len(levels)
    more = len(link) // 2
    outs = pl.pallas_call(
        lambda *refs: prepare_kernel(levels, single, more, *refs),
        out_shape=(pltpu.VMEM((2, width, width), BF),) * number
        + (pltpu.VMEM((width, width), BF),) * (2 * single + more),
        in_specs=[HBM] * (3 + len(link)),
        out_specs=(VMEM,) * (number + 2 * single + more),
        scratch_shapes=[
            pltpu.VMEM((number, width, width), BF),
            pltpu.VMEM(index_map.shape, jnp.int32),
            pltpu.VMEM((2, width, width), BF),
            pltpu.SemaphoreType.DMA((2 * number + 2,)),
            pltpu.SemaphoreType.DMA,
        ],
        compiler_params=pltpu.CompilerParams(vmem_limit_bytes=8 * MIB),
        cost_estimate=cost(2 * number * width**3, 8 * number * width**2),
    )(*(in_hbm(value) for value in (own, partner, index_map, *link)))
    return list(outs[:number]), list(outs[number:])


def own_part(which, rows, table):
    def kernel(rows_ref, table_ref, out_ref):
        @pl.when(side() == which)
        def _():
            out_ref[...] = mm(rows_ref[...], table_ref[0])

    return call(kernel, [jax.ShapeDtypeStruct(rows.shape, F32)], [rows, table], HINT // 4)[0]


def finish(which, term, partner, table):
    def kernel(term_ref, partner_ref, table_ref, out_ref):
        @pl.when(side() == which)
        def _():
            out_ref[...] = (term_ref[...] + mm(partner_ref[...], table_ref[1])).astype(BF)

    out = jax.ShapeDtypeStruct(partner.shape, BF)
    return call(kernel, [out], [term, partner, table], HINT)[0]


def both_parts(which, rows, partner, table, start, count):
    def kernel(rows_ref, partner_ref, table_ref, out_ref):
        @pl.when(side() == which)
        def _():
            block = slice(start, start + count)
            total = mm(rows_ref[block], table_ref[0]) + mm(partner_ref[block], table_ref[1])
            out_ref[...] = total.astype(BF)

    out = jax.ShapeDtypeStruct((count, rows.shape[1]), BF)
    return call(kernel, [out], [rows, partner, table], HINT)[0]


def pass_on(which, front, x, link, start):
    count = front.shape[0]

    def kernel(front_ref, x_ref, link_ref, out_ref):
        @pl.when(side() == which)
        def _():
            known = x_ref[start : start + count].astype(F32)
            out_ref[...] = (known + mm(front_ref[...], link_ref[...])).astype(BF)

    return call(kernel, [jax.ShapeDtypeStruct(front.shape, BF)], [front, x, link], HINT)[0]


def assemble(even, odd):
    half = even[0].shape[0]

    def kernel(even_first, even_second, odd_first, odd_second, out_ref):
        @pl.when(side() == 0)
        def _():
            out_ref[:half] = even_first[...]
            out_ref[half:] = even_second[...]

        @pl.when(side() == 1)
        def _():
            out_ref[:half] = odd_first[...]
            out_ref[half:] = odd_second[...]

    return pl.pallas_call(
        kernel,
        out_shape=jax.ShapeDtypeStruct((2 * half, even[0].shape[1]), BF),
        in_specs=[VMEM] * 4,
        out_specs=VMEM,
        compiler_params=pltpu.CompilerParams(vmem_limit_bytes=2 * MIB),
        cost_estimate=cost(0, 12 * even[0].size),
    )(*even, *odd)


def permute(value, target):
    sections, leaves = lax.axis_size("sweep"), lax.axis_size("leaf")
    pairs = []
    for s in range(sections):
        for l in range(leaves):
            to = target(s, l)
            if to is not None:
                pairs.append((s * leaves + l, to[0] * leaves + to[1]))
    return lax.ppermute(value, ("sweep", "leaf"), pairs)


def swap(value, bit, row=None):
    idle = 2 if bit == 1 else 1
    return permute(value, lambda s, l: (s, l ^ (bit if row in (None, s) else idle)))


def cross(value, bit=0):
    return permute(value, lambda s, l: (s ^ 1, l ^ bit))


def behind(rows, *values):
    rows, *values = lax.optimization_barrier((rows, *values))
    return rows, values


def paired(sources, solve_tiles, self_merge, partner_merge, coupling, front_map):
    solve = solve_tiles[0, 0]
    sections = lax.axis_size("sweep")
    count = self_merge.shape[2]

    x = load(sources[0, 0], solve)
    half = x.shape[0] // 2
    rows, raw = behind(x, self_merge, partner_merge, front_map, coupling)
    own = prepare(*(v[0, 0] for v in raw[:3]), [0, 1])[0]
    other = [None] * count
    own_link = None
    front = None
    even, odd = [], []
    back = None
    for section in range(sections):
        if section % 2 == 0:
            if section > 0:
                turn = {section - 1: section, section: section - 1}
                front = [permute(part, lambda s, l: (turn.get(s, s), l)) for part in front]
                rows = [pass_on(0, part, x, own_link, k * half) for k, part in enumerate(front)]
                rows = jnp.concatenate(rows)
            rows = both_parts(0, rows, swap(rows, 1, section), own[0], 0, 2 * half)
            if section == 0:
                rows, (table,) = behind(rows, own[1])
                other[1] = cross(table)
            came = cross(rows)
            partner = cross(rows, 2)
            if section == 0:
                _, raw = behind(rows, *raw)
                more, (own_link,) = prepare(
                    *(v[0, 0] for v in raw[:3]),
                    list(range(2, count)),
                    link=(raw[3][0, 0], solve),
                )
                own += more
            front = [both_parts(1, came, partner, other[1], k * half, half) for k in range(2)]
            first, tables, row = 2, other, section + 1
        else:
            front = [pass_on(1, part, x, own_link, k * half) for k, part in enumerate(front)]
            first, tables, row = 0, own, section
        for j in range(first, count):
            if section == 0 and j == 2:
                first, (second, *late) = behind(*front, *own[2:])
                front = [first, second]
                other[2:] = [cross(table) for table in late]
            if section == sections - 1 and j == count - 1:
                last = permute(front[0], lambda s, l: (s, l ^ 2**j) if s == row else None)
                partners = [last, swap(front[1], 2**j, row)]
            else:
                partners = [swap(part, 2**j, row) for part in front]
            terms = [own_part(1, part, tables[j]) for part in front]
            if section % 2 and j == 0:
                terms[1], back = behind(terms[1], *back)
                back = [cross(part) for part in back]
            if section % 2 and j == 1:
                terms[1], back = behind(terms[1], *back)
            front = [finish(1, term, part, tables[j]) for term, part in zip(terms, partners)]
        if section % 2 == 0:
            back = front
        elif section == 1:
            even, odd = back, front
        else:
            chosen = lax.axis_index("sweep") // 2 == section // 2
            even = [jnp.where(chosen, new, old) for new, old in zip(back, even)]
            odd = [jnp.where(chosen, new, old) for new, old in zip(front, odd)]
    return assemble(even, odd)[None, None]


def single(sources, solve_tiles, self_merge, partner_merge, coupling, front_map):
    rows, solve, link = sources[0, 0], solve_tiles[0, 0], coupling[0, 0]
    sections = lax.axis_size("sweep")
    front = jnp.zeros_like(rows)
    for section in range(sections):
        front = permute(front, lambda s, l: ((s + 1) % sections, l))
        front = jnp.where(lax.axis_index("sweep") == 0, jnp.zeros_like(front), front)
        x = mm((rows.astype(F32) + mm(front, link)).astype(BF), solve).astype(BF)
        for j in range(self_merge.shape[2]):
            mapped = jnp.take(swap(x, 2**j), front_map[0, 0, j], axis=1)
            x = (mm(x, self_merge[0, 0, j]) + mm(mapped, partner_merge[0, 0, j])).astype(BF)
        front = x
    return front[None, None]


def solution(mesh):
    spec = P("sweep", "leaf")
    return jax.shard_map(
        paired if mesh.shape["sweep"] % 2 == 0 else single,
        mesh=mesh,
        in_specs=(spec,) * 6,
        out_specs=spec,
        check_vma=False,
    )
```

```python
import jax
import jax.numpy as jnp
from jax import lax
from jax.experimental import pallas as pl
from jax.experimental.pallas import tpu as pltpu
from jax.sharding import PartitionSpec as P

BF = jnp.bfloat16
F32 = jnp.float32
MIB = 2**20
HINT = 10**8

HBM = pl.BlockSpec(memory_space=pltpu.HBM)
VMEM = pl.BlockSpec(memory_space=pltpu.VMEM)


def mm(left, right):
    return jnp.dot(left, right, preferred_element_type=F32)


def in_hbm(value):
    return pltpu.with_memory_space_constraint(value, pltpu.HBM)


def cost(flops, moved):
    return pl.CostEstimate(flops=flops, bytes_accessed=moved, transcendentals=0)


def side():
    return lax.rem(lax.axis_index("sweep"), 2)


def call(kernel, outs, args, flops, limit=4, **more):
    moved = sum(a.size * a.dtype.itemsize for a in args) + sum(o.size * 4 for o in outs)
    return pl.pallas_call(
        kernel,
        out_shape=tuple(pltpu.VMEM(o.shape, o.dtype) for o in outs),
        in_specs=[VMEM] * len(args),
        out_specs=(VMEM,) * len(outs),
        compiler_params=pltpu.CompilerParams(vmem_limit_bytes=limit * MIB),
        cost_estimate=cost(flops, moved),
        **more,
    )(*args)


def load_kernel(rows_hbm, solve_hbm, out_ref, rows_ref, solve_ref, sems):
    copies = [
        pltpu.make_async_copy(rows_hbm, rows_ref, sems.at[0]),
        pltpu.make_async_copy(solve_hbm, solve_ref, sems.at[1]),
    ]
    for copy in copies:
        copy.start()
    for copy in copies:
        copy.wait()
    out_ref[...] = mm(rows_ref[...], solve_ref[...]).astype(BF)


def load(rows, solve):
    return pl.pallas_call(
        load_kernel,
        out_shape=pltpu.VMEM(rows.shape, BF),
        in_specs=[HBM, HBM],
        out_specs=VMEM,
        scratch_shapes=[
            pltpu.VMEM(rows.shape, BF),
            pltpu.VMEM(solve.shape, BF),
            pltpu.SemaphoreType.DMA((2,)),
        ],
        compiler_params=pltpu.CompilerParams(vmem_limit_bytes=2 * MIB),
        cost_estimate=cost(2 * rows.size * solve.shape[1], 4 * rows.size + 2 * solve.size),
    )(in_hbm(rows), in_hbm(solve))


def prepare_kernel(levels, single, link, own_hbm, partner_hbm, map_hbm, *refs):
    number = len(levels)
    width = own_hbm.shape[1]
    link_hbm, refs = refs[: 2 * link], refs[2 * link :]
    outs, refs = refs[:number], refs[number:]
    singles, refs = refs[: 2 * single], refs[2 * single :]
    products, (partner_ref, map_ref, link_ref, sems, map_sem) = refs[:link], refs[link:]
    map_copy = pltpu.make_async_copy(map_hbm, map_ref, map_sem)
    map_copy.start()
    copies = []
    for k, j in enumerate(levels):
        pair = (
            pltpu.make_async_copy(partner_hbm.at[j], partner_ref.at[k], sems.at[2 * k]),
            pltpu.make_async_copy(own_hbm.at[j], outs[k].at[0], sems.at[2 * k + 1]),
        )
        for copy in pair:
            copy.start()
        copies.append(pair)
    extra = []
    if single:
        extra.append((own_hbm.at[levels[0]], singles[0]))
    for k, source in enumerate(link_hbm):
        extra.append((source, link_ref.at[k]))
    extra = [
        pltpu.make_async_copy(source, target, sems.at[2 * number + k])
        for k, (source, target) in enumerate(extra)
    ]
    for copy in extra:
        copy.start()
    map_copy.wait()
    rows = lax.broadcasted_iota(jnp.int32, (width, width), 0)
    for k, j in enumerate(levels):
        copies[k][0].wait()
        hot = (rows == map_ref[j : j + 1, :]).astype(BF)
        folded = mm(hot, partner_ref[k]).astype(BF)
        outs[k][1] = folded
        if single and k == 0:
            singles[1][...] = folded
    for copy in extra:
        copy.wait()
    if link:
        products[0][...] = mm(link_ref[0], link_ref[1]).astype(BF)
    for pair in copies:
        pair[1].wait()


def prepare(own, partner, index_map, levels, single=0, link=()):
    width = own.shape[1]
    number = len(levels)
    more = len(link) // 2
    outs = pl.pallas_call(
        lambda *refs: prepare_kernel(levels, single, more, *refs),
        out_shape=(pltpu.VMEM((2, width, width), BF),) * number
        + (pltpu.VMEM((width, width), BF),) * (2 * single + more),
        in_specs=[HBM] * (3 + len(link)),
        out_specs=(VMEM,) * (number + 2 * single + more),
        scratch_shapes=[
            pltpu.VMEM((number, width, width), BF),
            pltpu.VMEM(index_map.shape, jnp.int32),
            pltpu.VMEM((2, width, width), BF),
            pltpu.SemaphoreType.DMA((2 * number + 2,)),
            pltpu.SemaphoreType.DMA,
        ],
        compiler_params=pltpu.CompilerParams(vmem_limit_bytes=8 * MIB),
        cost_estimate=cost(2 * number * width**3, 8 * number * width**2),
    )(*(in_hbm(value) for value in (own, partner, index_map, *link)))
    return list(outs[:number]), list(outs[number:])


def own_part(which, rows, table):
    def kernel(rows_ref, table_ref, out_ref):
        @pl.when(side() == which)
        def _():
            out_ref[...] = mm(rows_ref[...], table_ref[0])

    return call(kernel, [jax.ShapeDtypeStruct(rows.shape, F32)], [rows, table], HINT // 4)[0]


def finish(which, term, partner, table):
    def kernel(term_ref, partner_ref, table_ref, out_ref):
        @pl.when(side() == which)
        def _():
            out_ref[...] = (term_ref[...] + mm(partner_ref[...], table_ref[1])).astype(BF)

    out = jax.ShapeDtypeStruct(partner.shape, BF)
    return call(kernel, [out], [term, partner, table], HINT)[0]


def both_parts(which, rows, partner, table, start, count):
    def kernel(rows_ref, partner_ref, table_ref, out_ref):
        @pl.when(side() == which)
        def _():
            block = slice(start, start + count)
            total = mm(rows_ref[block], table_ref[0]) + mm(partner_ref[block], table_ref[1])
            out_ref[...] = total.astype(BF)

    out = jax.ShapeDtypeStruct((count, rows.shape[1]), BF)
    return call(kernel, [out], [rows, partner, table], HINT)[0]


def pass_on(which, front, x, link, start):
    count = front.shape[0]

    def kernel(front_ref, x_ref, link_ref, out_ref):
        @pl.when(side() == which)
        def _():
            known = x_ref[start : start + count].astype(F32)
            out_ref[...] = (known + mm(front_ref[...], link_ref[...])).astype(BF)

    return call(kernel, [jax.ShapeDtypeStruct(front.shape, BF)], [front, x, link], HINT)[0]


def write_kernel(which, first_ref, second_ref, out_ref, sems):
    half = first_ref.shape[0]

    @pl.when(side() == which)
    def _():
        copies = [
            pltpu.make_async_copy(first_ref, out_ref.at[pl.ds(0, half)], sems.at[0]),
            pltpu.make_async_copy(second_ref, out_ref.at[pl.ds(half, half)], sems.at[1]),
        ]
        for copy in copies:
            copy.start()
        for copy in copies:
            copy.wait()


def write_first(which, blocks):
    half, width = blocks[0].shape
    return pl.pallas_call(
        lambda first, second, out, sems: write_kernel(which, first, second, out, sems),
        out_shape=pltpu.HBM((2 * half, width), BF),
        in_specs=[VMEM, VMEM],
        out_specs=HBM,
        scratch_shapes=[pltpu.SemaphoreType.DMA((2,))],
        compiler_params=pltpu.CompilerParams(vmem_limit_bytes=2 * MIB),
        cost_estimate=cost(0, 8 * blocks[0].size),
    )(*blocks)


def write_rest(which, out, blocks):
    return pl.pallas_call(
        lambda first, second, _, out, sems: write_kernel(which, first, second, out, sems),
        out_shape=pltpu.HBM(out.shape, BF),
        in_specs=[VMEM, VMEM, HBM],
        out_specs=HBM,
        scratch_shapes=[pltpu.SemaphoreType.DMA((2,))],
        input_output_aliases={2: 0},
        compiler_params=pltpu.CompilerParams(vmem_limit_bytes=2 * MIB),
        cost_estimate=cost(0, 8 * blocks[0].size),
    )(*blocks, out)


def permute(value, target):
    sections, leaves = lax.axis_size("sweep"), lax.axis_size("leaf")
    pairs = []
    for s in range(sections):
        for l in range(leaves):
            to = target(s, l)
            if to is not None:
                pairs.append((s * leaves + l, to[0] * leaves + to[1]))
    return lax.ppermute(value, ("sweep", "leaf"), pairs)


def swap(value, bit, row=None):
    idle = 2 if bit == 1 else 1
    return permute(value, lambda s, l: (s, l ^ (bit if row in (None, s) else idle)))


def cross(value, bit=0):
    return permute(value, lambda s, l: (s ^ 1, l ^ bit))


def behind(rows, *values):
    rows, *values = lax.optimization_barrier((rows, *values))
    return rows, values


def paired(sources, solve_tiles, self_merge, partner_merge, coupling, front_map):
    solve = solve_tiles[0, 0]
    sections = lax.axis_size("sweep")
    count = self_merge.shape[2]

    x = load(sources[0, 0], solve)
    half = x.shape[0] // 2
    rows, raw = behind(x, self_merge, partner_merge, front_map, coupling)
    own = prepare(*(v[0, 0] for v in raw[:3]), [0, 1])[0]
    other = [None] * count
    own_link = None
    front = None
    even, odd = [], []
    back = out = None
    for section in range(sections):
        if section % 2 == 0:
            if section > 0:
                turn = {section - 1: section, section: section - 1}
                front = [permute(part, lambda s, l: (turn.get(s, s), l)) for part in front]
                rows = [pass_on(0, part, x, own_link, k * half) for k, part in enumerate(front)]
                rows = jnp.concatenate(rows)
            rows = both_parts(0, rows, swap(rows, 1, section), own[0], 0, 2 * half)
            if section == 0:
                rows, (table,) = behind(rows, own[1])
                other[1] = cross(table)
            came = cross(rows)
            partner = cross(rows, 2)
            if section == 0:
                _, raw = behind(rows, *raw)
                more, (own_link,) = prepare(
                    *(v[0, 0] for v in raw[:3]),
                    list(range(2, count)),
                    link=(raw[3][0, 0], solve),
                )
                own += more
            front = [both_parts(1, came, partner, other[1], k * half, half) for k in range(2)]
            first, tables, row = 2, other, section + 1
        else:
            front = [pass_on(1, part, x, own_link, k * half) for k, part in enumerate(front)]
            first, tables, row = 0, own, section
        for j in range(first, count):
            if section == 0 and j == 2:
                first, (second, *late) = behind(*front, *own[2:])
                front = [first, second]
                other[2:] = [cross(table) for table in late]
            partners = [swap(part, 2**j, row) for part in front]
            terms = [own_part(1, part, tables[j]) for part in front]
            if section % 2 and j == 1:
                terms[1], back = behind(terms[1], *back)
                back = [cross(part) for part in back]
            if section % 2 and j == 2:
                terms[1], back = behind(terms[1], *back)
                if sections == 2:
                    out = write_first(0, back)
                    terms[1], (out,) = behind(terms[1], out)
            front = [finish(1, term, part, tables[j]) for term, part in zip(terms, partners)]
        if section % 2 == 0:
            back = front
        elif section == 1:
            even, odd = back, front
        else:
            chosen = lax.axis_index("sweep") // 2 == section // 2
            even = [jnp.where(chosen, new, old) for new, old in zip(back, even)]
            odd = [jnp.where(chosen, new, old) for new, old in zip(front, odd)]
    if out is None:
        out = write_first(0, even)
    return write_rest(1, out, odd)[None, None]


def single(sources, solve_tiles, self_merge, partner_merge, coupling, front_map):
    rows, solve, link = sources[0, 0], solve_tiles[0, 0], coupling[0, 0]
    sections = lax.axis_size("sweep")
    front = jnp.zeros_like(rows)
    for section in range(sections):
        front = permute(front, lambda s, l: ((s + 1) % sections, l))
        front = jnp.where(lax.axis_index("sweep") == 0, jnp.zeros_like(front), front)
        x = mm((rows.astype(F32) + mm(front, link)).astype(BF), solve).astype(BF)
        for j in range(self_merge.shape[2]):
            mapped = jnp.take(swap(x, 2**j), front_map[0, 0, j], axis=1)
            x = (mm(x, self_merge[0, 0, j]) + mm(mapped, partner_merge[0, 0, j])).astype(BF)
        front = x
    return front[None, None]


def solution(mesh):
    spec = P("sweep", "leaf")
    return jax.shard_map(
        paired if mesh.shape["sweep"] % 2 == 0 else single,
        mesh=mesh,
        in_specs=(spec,) * 6,
        out_specs=spec,
        check_vma=False,
    )
```

```python
import jax
import jax.numpy as jnp
from jax import lax
from jax.experimental import pallas as pl
from jax.experimental.pallas import tpu as pltpu
from jax.sharding import PartitionSpec as P

BF = jnp.bfloat16
F32 = jnp.float32
MIB = 2**20
HINT = 10**8

HBM = pl.BlockSpec(memory_space=pltpu.HBM)
VMEM = pl.BlockSpec(memory_space=pltpu.VMEM)


def mm(left, right):
    return jnp.dot(left, right, preferred_element_type=F32)


def in_hbm(value):
    return pltpu.with_memory_space_constraint(value, pltpu.HBM)


def cost(flops, moved):
    return pl.CostEstimate(flops=flops, bytes_accessed=moved, transcendentals=0)


def side():
    return lax.rem(lax.axis_index("sweep"), 2)


def call(kernel, outs, args, flops, limit=4, **more):
    moved = sum(a.size * a.dtype.itemsize for a in args) + sum(o.size * 4 for o in outs)
    return pl.pallas_call(
        kernel,
        out_shape=tuple(pltpu.VMEM(o.shape, o.dtype) for o in outs),
        in_specs=[VMEM] * len(args),
        out_specs=(VMEM,) * len(outs),
        compiler_params=pltpu.CompilerParams(vmem_limit_bytes=limit * MIB),
        cost_estimate=cost(flops, moved),
        **more,
    )(*args)


def multiply(which, rows, solve):
    half = rows.shape[0] // 2

    def kernel(rows_ref, solve_ref, first_ref, second_ref):
        @pl.when(side() == which)
        def _():
            value = mm(rows_ref[...], solve_ref[...]).astype(BF)
            first_ref[...] = value[:half]
            second_ref[...] = value[half:]

    out = jax.ShapeDtypeStruct((half, solve.shape[1]), BF)
    return list(call(kernel, [out, out], [rows, solve], HINT))


def prepare_kernel(levels, single, link, own_hbm, partner_hbm, map_hbm, *refs):
    number = len(levels)
    width = own_hbm.shape[1]
    link_hbm, refs = refs[: 2 * link], refs[2 * link :]
    outs, refs = refs[:number], refs[number:]
    singles, refs = refs[: 2 * single], refs[2 * single :]
    products, (partner_ref, map_ref, link_ref, sems, map_sem) = refs[:link], refs[link:]
    map_copy = pltpu.make_async_copy(map_hbm, map_ref, map_sem)
    map_copy.start()
    copies = []
    for k, j in enumerate(levels):
        pair = (
            pltpu.make_async_copy(partner_hbm.at[j], partner_ref.at[k], sems.at[2 * k]),
            pltpu.make_async_copy(own_hbm.at[j], outs[k].at[0], sems.at[2 * k + 1]),
        )
        for copy in pair:
            copy.start()
        copies.append(pair)
    extra = []
    if single:
        extra.append((own_hbm.at[levels[0]], singles[0]))
    for k, source in enumerate(link_hbm):
        extra.append((source, link_ref.at[k]))
    extra = [
        pltpu.make_async_copy(source, target, sems.at[2 * number + k])
        for k, (source, target) in enumerate(extra)
    ]
    for copy in extra:
        copy.start()
    map_copy.wait()
    rows = lax.broadcasted_iota(jnp.int32, (width, width), 0)
    for k, j in enumerate(levels):
        copies[k][0].wait()
        hot = (rows == map_ref[j : j + 1, :]).astype(BF)
        folded = mm(hot, partner_ref[k]).astype(BF)
        outs[k][1] = folded
        if single and k == 0:
            singles[1][...] = folded
    for copy in extra:
        copy.wait()
    if link:
        products[0][...] = mm(link_ref[0], link_ref[1]).astype(BF)
    for pair in copies:
        pair[1].wait()


def prepare(own, partner, index_map, levels, single=0, link=()):
    width = own.shape[1]
    number = len(levels)
    more = len(link) // 2
    outs = pl.pallas_call(
        lambda *refs: prepare_kernel(levels, single, more, *refs),
        out_shape=(pltpu.VMEM((2, width, width), BF),) * number
        + (pltpu.VMEM((width, width), BF),) * (2 * single + more),
        in_specs=[HBM] * (3 + len(link)),
        out_specs=(VMEM,) * (number + 2 * single + more),
        scratch_shapes=[
            pltpu.VMEM((number, width, width), BF),
            pltpu.VMEM(index_map.shape, jnp.int32),
            pltpu.VMEM((2, width, width), BF),
            pltpu.SemaphoreType.DMA((2 * number + 2,)),
            pltpu.SemaphoreType.DMA,
        ],
        compiler_params=pltpu.CompilerParams(vmem_limit_bytes=8 * MIB),
        cost_estimate=cost(2 * number * width**3, 8 * number * width**2),
    )(*(in_hbm(value) for value in (own, partner, index_map, *link)))
    return list(outs[:number]), list(outs[number:])


def level(which, rows, partner, table):
    def kernel(rows_ref, partner_ref, table_ref, out_ref):
        @pl.when(side() == which)
        def _():
            total = mm(rows_ref[...], table_ref[0]) + mm(partner_ref[...], table_ref[1])
            out_ref[...] = total.astype(BF)

    out = jax.ShapeDtypeStruct(rows.shape, BF)
    return call(kernel, [out], [rows, partner, table], HINT)[0]


def pass_on(which, front, known, link):
    def kernel(front_ref, known_ref, link_ref, out_ref):
        @pl.when(side() == which)
        def _():
            more = mm(front_ref[...], link_ref[...])
            out_ref[...] = (known_ref[...].astype(F32) + more).astype(BF)

    out = jax.ShapeDtypeStruct(front.shape, BF)
    return call(kernel, [out], [front, known, link], HINT)[0]


def write_kernel(which, first_ref, second_ref, out_ref, sems):
    half = first_ref.shape[0]

    @pl.when(side() == which)
    def _():
        copies = [
            pltpu.make_async_copy(first_ref, out_ref.at[pl.ds(0, half)], sems.at[0]),
            pltpu.make_async_copy(second_ref, out_ref.at[pl.ds(half, half)], sems.at[1]),
        ]
        for copy in copies:
            copy.start()
        for copy in copies:
            copy.wait()


def write_first(which, blocks):
    half, width = blocks[0].shape
    return pl.pallas_call(
        lambda first, second, out, sems: write_kernel(which, first, second, out, sems),
        out_shape=pltpu.HBM((2 * half, width), BF),
        in_specs=[VMEM, VMEM],
        out_specs=HBM,
        scratch_shapes=[pltpu.SemaphoreType.DMA((2,))],
        compiler_params=pltpu.CompilerParams(vmem_limit_bytes=2 * MIB),
        cost_estimate=cost(0, 8 * blocks[0].size),
    )(*blocks)


def write_rest(which, out, blocks):
    return pl.pallas_call(
        lambda first, second, _, out, sems: write_kernel(which, first, second, out, sems),
        out_shape=pltpu.HBM(out.shape, BF),
        in_specs=[VMEM, VMEM, HBM],
        out_specs=HBM,
        scratch_shapes=[pltpu.SemaphoreType.DMA((2,))],
        input_output_aliases={2: 0},
        compiler_params=pltpu.CompilerParams(vmem_limit_bytes=2 * MIB),
        cost_estimate=cost(0, 8 * blocks[0].size),
    )(*blocks, out)


def permute(value, target):
    sections, leaves = lax.axis_size("sweep"), lax.axis_size("leaf")
    pairs = []
    for s in range(sections):
        for l in range(leaves):
            to = target(s, l)
            if to is not None:
                pairs.append((s * leaves + l, to[0] * leaves + to[1]))
    return lax.ppermute(value, ("sweep", "leaf"), pairs)


def swap(value, bit, row=None):
    idle = 2 if bit == 1 else 1
    return permute(value, lambda s, l: (s, l ^ (bit if row in (None, s) else idle)))


def cross(value, bit=0):
    return permute(value, lambda s, l: (s ^ 1, l ^ bit))


def behind(rows, *values):
    rows, *values = lax.optimization_barrier((rows, *values))
    return rows, values


def paired(sources, solve_tiles, self_merge, partner_merge, coupling, front_map):
    sections = lax.axis_size("sweep")
    count = self_merge.shape[2]
    solve = solve_tiles[0, 0]

    moved = [cross(sources[0, 0]), cross(solve)]
    raw = [self_merge[0, 0], partner_merge[0, 0], front_map[0, 0]]
    own = prepare(*raw, [0, 1])[0]
    table, moved = behind(own[0], *moved)
    known_even = multiply(1, *moved)
    front, (*early,) = known_even, (table, own[1])
    first, (second, *early) = behind(*front, *early)
    other = [cross(one) for one in early]
    front = [first, second]
    known_odd = own_link = other_link = out = None
    even, odd = [], []
    for section in range(sections):
        parity, row = section % 2, section | 1
        tables = own if parity else other
        if section > 0:
            if parity == 0:
                turn = {row - 2: row, row: row - 2}
                front = [permute(part, lambda s, l: (turn.get(s, s), l)) for part in front]
            known = known_odd if parity else known_even
            link = own_link if parity else other_link
            front = [pass_on(1, part, base, link) for part, base in zip(front, known)]
        for j in range(count):
            if section == 0 and j == 1:
                first, (second, *late) = behind(*front, *own[2:])
                front = [first, second]
                other += [cross(one) for one in late]
            partners = [swap(part, 2**j, row) for part in front]
            if section == 0 and j == 0:
                _, late = behind(front[0], *raw, coupling[0, 0], solve)
                more, (own_link,) = prepare(*late[:3], list(range(2, count)), link=tuple(late[3:]))
                own += more
            if section == 0 and j == 1:
                known_odd = multiply(1, sources[0, 0], solve)
                if sections > 2:
                    other_link = cross(own_link)
            if parity and j == 1:
                _, back = behind(front[0], *back)
                back = [cross(part) for part in back]
            if parity and j == 2:
                front[1], back = behind(front[1], *back)
                if sections == 2:
                    out = write_first(0, back)
                    front[1], (out,) = behind(front[1], out)
            front = [level(1, part, other_part, tables[j]) for part, other_part in zip(front, partners)]
        if parity == 0:
            back = front
        elif section == 1:
            even, odd = back, front
        else:
            chosen = lax.axis_index("sweep") // 2 == section // 2
            even = [jnp.where(chosen, new, old) for new, old in zip(back, even)]
            odd = [jnp.where(chosen, new, old) for new, old in zip(front, odd)]
    if out is None:
        out = write_first(0, even)
    return write_rest(1, out, odd)[None, None]


def single(sources, solve_tiles, self_merge, partner_merge, coupling, front_map):
    rows, solve, link = sources[0, 0], solve_tiles[0, 0], coupling[0, 0]
    sections = lax.axis_size("sweep")
    front = jnp.zeros_like(rows)
    for section in range(sections):
        front = permute(front, lambda s, l: ((s + 1) % sections, l))
        front = jnp.where(lax.axis_index("sweep") == 0, jnp.zeros_like(front), front)
        x = mm((rows.astype(F32) + mm(front, link)).astype(BF), solve).astype(BF)
        for j in range(self_merge.shape[2]):
            mapped = jnp.take(swap(x, 2**j), front_map[0, 0, j], axis=1)
            x = (mm(x, self_merge[0, 0, j]) + mm(mapped, partner_merge[0, 0, j])).astype(BF)
        front = x
    return front[None, None]


def solution(mesh):
    spec = P("sweep", "leaf")
    return jax.shard_map(
        paired if mesh.shape["sweep"] % 2 == 0 else single,
        mesh=mesh,
        in_specs=(spec,) * 6,
        out_specs=spec,
        check_vma=False,
    )
```

```python
import jax
import jax.numpy as jnp
from jax import lax
from jax.experimental import pallas as pl
from jax.experimental.pallas import tpu as pltpu
from jax.sharding import PartitionSpec as P

BF = jnp.bfloat16
F32 = jnp.float32
MIB = 2**20
HINT = 10**8

HBM = pl.BlockSpec(memory_space=pltpu.HBM)
VMEM = pl.BlockSpec(memory_space=pltpu.VMEM)


def mm(left, right):
    return jnp.dot(left, right, preferred_element_type=F32)


def in_hbm(value):
    return pltpu.with_memory_space_constraint(value, pltpu.HBM)


def cost(flops, moved):
    return pl.CostEstimate(flops=flops, bytes_accessed=moved, transcendentals=0)


def side():
    return lax.rem(lax.axis_index("sweep"), 2)


def call(kernel, outs, args, flops, limit=4, **more):
    moved = sum(a.size * a.dtype.itemsize for a in args) + sum(o.size * 4 for o in outs)
    return pl.pallas_call(
        kernel,
        out_shape=tuple(pltpu.VMEM(o.shape, o.dtype) for o in outs),
        in_specs=[VMEM] * len(args),
        out_specs=(VMEM,) * len(outs),
        compiler_params=pltpu.CompilerParams(vmem_limit_bytes=limit * MIB),
        cost_estimate=cost(flops, moved),
        **more,
    )(*args)


def load_kernel(rows_hbm, solve_hbm, out_ref, rows_ref, solve_ref, sems):
    copies = [
        pltpu.make_async_copy(rows_hbm, rows_ref, sems.at[0]),
        pltpu.make_async_copy(solve_hbm, solve_ref, sems.at[1]),
    ]
    for copy in copies:
        copy.start()
    for copy in copies:
        copy.wait()
    out_ref[...] = mm(rows_ref[...], solve_ref[...]).astype(BF)


def load(rows, solve):
    return pl.pallas_call(
        load_kernel,
        out_shape=pltpu.VMEM(rows.shape, BF),
        in_specs=[HBM, HBM],
        out_specs=VMEM,
        scratch_shapes=[
            pltpu.VMEM(rows.shape, BF),
            pltpu.VMEM(solve.shape, BF),
            pltpu.SemaphoreType.DMA((2,)),
        ],
        compiler_params=pltpu.CompilerParams(vmem_limit_bytes=2 * MIB),
        cost_estimate=cost(2 * rows.size * solve.shape[1], 4 * rows.size + 2 * solve.size),
    )(in_hbm(rows), in_hbm(solve))


def prepare_kernel(levels, single, link, own_hbm, partner_hbm, map_hbm, *refs):
    number = len(levels)
    width = own_hbm.shape[1]
    link_hbm, refs = refs[: 2 * link], refs[2 * link :]
    outs, refs = refs[:number], refs[number:]
    singles, refs = refs[: 2 * single], refs[2 * single :]
    products, (partner_ref, map_ref, link_ref, sems, map_sem) = refs[:link], refs[link:]
    map_copy = pltpu.make_async_copy(map_hbm, map_ref, map_sem)
    map_copy.start()
    copies = []
    for k, j in enumerate(levels):
        pair = (
            pltpu.make_async_copy(partner_hbm.at[j], partner_ref.at[k], sems.at[2 * k]),
            pltpu.make_async_copy(own_hbm.at[j], outs[k].at[0], sems.at[2 * k + 1]),
        )
        for copy in pair:
            copy.start()
        copies.append(pair)
    extra = []
    if single:
        extra.append((own_hbm.at[levels[0]], singles[0]))
    for k, source in enumerate(link_hbm):
        extra.append((source, link_ref.at[k]))
    extra = [
        pltpu.make_async_copy(source, target, sems.at[2 * number + k])
        for k, (source, target) in enumerate(extra)
    ]
    for copy in extra:
        copy.start()
    map_copy.wait()
    rows = lax.broadcasted_iota(jnp.int32, (width, width), 0)
    for k, j in enumerate(levels):
        copies[k][0].wait()
        hot = (rows == map_ref[j : j + 1, :]).astype(BF)
        folded = mm(hot, partner_ref[k]).astype(BF)
        outs[k][1] = folded
        if single and k == 0:
            singles[1][...] = folded
    for copy in extra:
        copy.wait()
    if link:
        products[0][...] = mm(link_ref[0], link_ref[1]).astype(BF)
    for pair in copies:
        pair[1].wait()


def prepare(own, partner, index_map, levels, single=0, link=()):
    width = own.shape[1]
    number = len(levels)
    more = len(link) // 2
    outs = pl.pallas_call(
        lambda *refs: prepare_kernel(levels, single, more, *refs),
        out_shape=(pltpu.VMEM((2, width, width), BF),) * number
        + (pltpu.VMEM((width, width), BF),) * (2 * single + more),
        in_specs=[HBM] * (3 + len(link)),
        out_specs=(VMEM,) * (number + 2 * single + more),
        scratch_shapes=[
            pltpu.VMEM((number, width, width), BF),
            pltpu.VMEM(index_map.shape, jnp.int32),
            pltpu.VMEM((2, width, width), BF),
            pltpu.SemaphoreType.DMA((2 * number + 2,)),
            pltpu.SemaphoreType.DMA,
        ],
        compiler_params=pltpu.CompilerParams(vmem_limit_bytes=8 * MIB),
        cost_estimate=cost(2 * number * width**3, 8 * number * width**2),
    )(*(in_hbm(value) for value in (own, partner, index_map, *link)))
    return list(outs[:number]), list(outs[number:])


def level(which, rows, partner, table):
    def kernel(rows_ref, partner_ref, table_ref, out_ref):
        @pl.when(side() == which)
        def _():
            total = mm(rows_ref[...], table_ref[0]) + mm(partner_ref[...], table_ref[1])
            out_ref[...] = total.astype(BF)

    out = jax.ShapeDtypeStruct(rows.shape, BF)
    return call(kernel, [out], [rows, partner, table], HINT)[0]


def both_parts(which, rows, partner, table, start, count):
    def kernel(rows_ref, partner_ref, table_ref, out_ref):
        @pl.when(side() == which)
        def _():
            block = slice(start, start + count)
            total = mm(rows_ref[block], table_ref[0]) + mm(partner_ref[block], table_ref[1])
            out_ref[...] = total.astype(BF)

    out = jax.ShapeDtypeStruct((count, rows.shape[1]), BF)
    return call(kernel, [out], [rows, partner, table], HINT)[0]


def pass_on(which, front, x, link, start):
    count = front.shape[0]

    def kernel(front_ref, x_ref, link_ref, out_ref):
        @pl.when(side() == which)
        def _():
            known = x_ref[start : start + count].astype(F32)
            out_ref[...] = (known + mm(front_ref[...], link_ref[...])).astype(BF)

    return call(kernel, [jax.ShapeDtypeStruct(front.shape, BF)], [front, x, link], HINT)[0]


def write_kernel(which, first_ref, second_ref, out_ref, sems):
    half = first_ref.shape[0]

    @pl.when(side() == which)
    def _():
        copies = [
            pltpu.make_async_copy(first_ref, out_ref.at[pl.ds(0, half)], sems.at[0]),
            pltpu.make_async_copy(second_ref, out_ref.at[pl.ds(half, half)], sems.at[1]),
        ]
        for copy in copies:
            copy.start()
        for copy in copies:
            copy.wait()


def write_first(which, blocks):
    half, width = blocks[0].shape
    return pl.pallas_call(
        lambda first, second, out, sems: write_kernel(which, first, second, out, sems),
        out_shape=pltpu.HBM((2 * half, width), BF),
        in_specs=[VMEM, VMEM],
        out_specs=HBM,
        scratch_shapes=[pltpu.SemaphoreType.DMA((2,))],
        compiler_params=pltpu.CompilerParams(vmem_limit_bytes=2 * MIB),
        cost_estimate=cost(0, 8 * blocks[0].size),
    )(*blocks)


def write_rest(which, out, blocks):
    return pl.pallas_call(
        lambda first, second, _, out, sems: write_kernel(which, first, second, out, sems),
        out_shape=pltpu.HBM(out.shape, BF),
        in_specs=[VMEM, VMEM, HBM],
        out_specs=HBM,
        scratch_shapes=[pltpu.SemaphoreType.DMA((2,))],
        input_output_aliases={2: 0},
        compiler_params=pltpu.CompilerParams(vmem_limit_bytes=2 * MIB),
        cost_estimate=cost(0, 8 * blocks[0].size),
    )(*blocks, out)


def permute(value, target):
    sections, leaves = lax.axis_size("sweep"), lax.axis_size("leaf")
    pairs = []
    for s in range(sections):
        for l in range(leaves):
            to = target(s, l)
            if to is not None:
                pairs.append((s * leaves + l, to[0] * leaves + to[1]))
    return lax.ppermute(value, ("sweep", "leaf"), pairs)


def swap(value, bit, row=None):
    idle = 2 if bit == 1 else 1
    return permute(value, lambda s, l: (s, l ^ (bit if row in (None, s) else idle)))


def cross(value, bit=0):
    return permute(value, lambda s, l: (s ^ 1, l ^ bit))


def behind(rows, *values):
    rows, *values = lax.optimization_barrier((rows, *values))
    return rows, values


def paired(sources, solve_tiles, self_merge, partner_merge, coupling, front_map):
    solve = solve_tiles[0, 0]
    sections = lax.axis_size("sweep")
    count = self_merge.shape[2]

    x = load(sources[0, 0], solve)
    half = x.shape[0] // 2
    rows, raw = behind(x, self_merge, partner_merge, front_map, coupling)
    own = prepare(*(v[0, 0] for v in raw[:3]), [0, 1])[0]
    other = [None] * count
    own_link = None
    front = None
    even, odd = [], []
    back = out = None
    for section in range(sections):
        if section % 2 == 0:
            if section > 0:
                turn = {section - 1: section, section: section - 1}
                front = [permute(part, lambda s, l: (turn.get(s, s), l)) for part in front]
                rows = [pass_on(0, part, x, own_link, k * half) for k, part in enumerate(front)]
                rows = jnp.concatenate(rows)
            rows = both_parts(0, rows, swap(rows, 1, section), own[0], 0, 2 * half)
            if section == 0:
                rows, (table,) = behind(rows, own[1])
                other[1] = cross(table)
            came = cross(rows)
            partner = cross(rows, 2)
            if section == 0:
                _, raw = behind(rows, *raw)
                more, (own_link,) = prepare(
                    *(v[0, 0] for v in raw[:3]),
                    list(range(2, count)),
                    link=(raw[3][0, 0], solve),
                )
                own += more
            front = [both_parts(1, came, partner, other[1], k * half, half) for k in range(2)]
            first, tables, row = 2, other, section + 1
        else:
            front = [pass_on(1, part, x, own_link, k * half) for k, part in enumerate(front)]
            first, tables, row = 0, own, section
        for j in range(first, count):
            if section == 0 and j == 2:
                _, late = behind(front[0], *own[2:])
                other[2:] = [cross(table) for table in late]
            partners = [swap(part, 2**j, row) for part in front]
            if section % 2 and j == 1:
                _, back = behind(front[0], *back)
                back = [cross(part) for part in back]
            if section % 2 and j == 2:
                front[1], back = behind(front[1], *back)
                if sections == 2:
                    out = write_first(0, back)
                    front[1], (out,) = behind(front[1], out)
            front = [level(1, part, came, tables[j]) for part, came in zip(front, partners)]
        if section % 2 == 0:
            back = front
        elif section == 1:
            even, odd = back, front
        else:
            chosen = lax.axis_index("sweep") // 2 == section // 2
            even = [jnp.where(chosen, new, old) for new, old in zip(back, even)]
            odd = [jnp.where(chosen, new, old) for new, old in zip(front, odd)]
    if out is None:
        out = write_first(0, even)
    return write_rest(1, out, odd)[None, None]


def single(sources, solve_tiles, self_merge, partner_merge, coupling, front_map):
    rows, solve, link = sources[0, 0], solve_tiles[0, 0], coupling[0, 0]
    sections = lax.axis_size("sweep")
    front = jnp.zeros_like(rows)
    for section in range(sections):
        front = permute(front, lambda s, l: ((s + 1) % sections, l))
        front = jnp.where(lax.axis_index("sweep") == 0, jnp.zeros_like(front), front)
        x = mm((rows.astype(F32) + mm(front, link)).astype(BF), solve).astype(BF)
        for j in range(self_merge.shape[2]):
            mapped = jnp.take(swap(x, 2**j), front_map[0, 0, j], axis=1)
            x = (mm(x, self_merge[0, 0, j]) + mm(mapped, partner_merge[0, 0, j])).astype(BF)
        front = x
    return front[None, None]


def solution(mesh):
    spec = P("sweep", "leaf")
    return jax.shard_map(
        paired if mesh.shape["sweep"] % 2 == 0 else single,
        mesh=mesh,
        in_specs=(spec,) * 6,
        out_specs=spec,
        check_vma=False,
    )
```

```python
import jax
import jax.numpy as jnp
from jax import lax
from jax.experimental import pallas as pl
from jax.experimental.pallas import tpu as pltpu
from jax.sharding import PartitionSpec as P

BF = jnp.bfloat16
F32 = jnp.float32
MIB = 2**20
HINT = 10**8

HBM = pl.BlockSpec(memory_space=pltpu.HBM)
VMEM = pl.BlockSpec(memory_space=pltpu.VMEM)


def mm(left, right):
    return jnp.dot(left, right, preferred_element_type=F32)


def in_hbm(value):
    return pltpu.with_memory_space_constraint(value, pltpu.HBM)


def cost(flops, moved):
    return pl.CostEstimate(flops=flops, bytes_accessed=moved, transcendentals=0)


def side():
    return lax.rem(lax.axis_index("sweep"), 2)


def call(kernel, outs, args, flops, limit=4, **more):
    moved = sum(a.size * a.dtype.itemsize for a in args) + sum(o.size * 4 for o in outs)
    return pl.pallas_call(
        kernel,
        out_shape=tuple(pltpu.VMEM(o.shape, o.dtype) for o in outs),
        in_specs=[VMEM] * len(args),
        out_specs=(VMEM,) * len(outs),
        compiler_params=pltpu.CompilerParams(vmem_limit_bytes=limit * MIB),
        cost_estimate=cost(flops, moved),
        **more,
    )(*args)


def load_kernel(rows_hbm, solve_hbm, out_ref, rows_ref, solve_ref, sems):
    copies = [
        pltpu.make_async_copy(rows_hbm, rows_ref, sems.at[0]),
        pltpu.make_async_copy(solve_hbm, solve_ref, sems.at[1]),
    ]
    for copy in copies:
        copy.start()
    for copy in copies:
        copy.wait()
    out_ref[...] = mm(rows_ref[...], solve_ref[...]).astype(BF)


def load(rows, solve):
    return pl.pallas_call(
        load_kernel,
        out_shape=pltpu.VMEM(rows.shape, BF),
        in_specs=[HBM, HBM],
        out_specs=VMEM,
        scratch_shapes=[
            pltpu.VMEM(rows.shape, BF),
            pltpu.VMEM(solve.shape, BF),
            pltpu.SemaphoreType.DMA((2,)),
        ],
        compiler_params=pltpu.CompilerParams(vmem_limit_bytes=2 * MIB),
        cost_estimate=cost(2 * rows.size * solve.shape[1], 4 * rows.size + 2 * solve.size),
    )(in_hbm(rows), in_hbm(solve))


def prepare_kernel(levels, single, link, own_hbm, partner_hbm, map_hbm, *refs):
    number = len(levels)
    width = own_hbm.shape[1]
    link_hbm, refs = refs[: 2 * link], refs[2 * link :]
    outs, refs = refs[:number], refs[number:]
    singles, refs = refs[: 2 * single], refs[2 * single :]
    products, (partner_ref, map_ref, link_ref, sems, map_sem) = refs[:link], refs[link:]
    map_copy = pltpu.make_async_copy(map_hbm, map_ref, map_sem)
    map_copy.start()
    copies = []
    for k, j in enumerate(levels):
        pair = (
            pltpu.make_async_copy(partner_hbm.at[j], partner_ref.at[k], sems.at[2 * k]),
            pltpu.make_async_copy(own_hbm.at[j], outs[k].at[0], sems.at[2 * k + 1]),
        )
        for copy in pair:
            copy.start()
        copies.append(pair)
    extra = []
    if single:
        extra.append((own_hbm.at[levels[0]], singles[0]))
    for k, source in enumerate(link_hbm):
        extra.append((source, link_ref.at[k]))
    extra = [
        pltpu.make_async_copy(source, target, sems.at[2 * number + k])
        for k, (source, target) in enumerate(extra)
    ]
    for copy in extra:
        copy.start()
    map_copy.wait()
    rows = lax.broadcasted_iota(jnp.int32, (width, width), 0)
    for k, j in enumerate(levels):
        copies[k][0].wait()
        hot = (rows == map_ref[j : j + 1, :]).astype(BF)
        folded = mm(hot, partner_ref[k]).astype(BF)
        outs[k][1] = folded
        if single and k == 0:
            singles[1][...] = folded
    for copy in extra:
        copy.wait()
    if link:
        products[0][...] = mm(link_ref[0], link_ref[1]).astype(BF)
    for pair in copies:
        pair[1].wait()


def prepare(own, partner, index_map, levels, single=0, link=()):
    width = own.shape[1]
    number = len(levels)
    more = len(link) // 2
    outs = pl.pallas_call(
        lambda *refs: prepare_kernel(levels, single, more, *refs),
        out_shape=(pltpu.VMEM((2, width, width), BF),) * number
        + (pltpu.VMEM((width, width), BF),) * (2 * single + more),
        in_specs=[HBM] * (3 + len(link)),
        out_specs=(VMEM,) * (number + 2 * single + more),
        scratch_shapes=[
            pltpu.VMEM((number, width, width), BF),
            pltpu.VMEM(index_map.shape, jnp.int32),
            pltpu.VMEM((2, width, width), BF),
            pltpu.SemaphoreType.DMA((2 * number + 2,)),
            pltpu.SemaphoreType.DMA,
        ],
        compiler_params=pltpu.CompilerParams(vmem_limit_bytes=8 * MIB),
        cost_estimate=cost(2 * number * width**3, 8 * number * width**2),
    )(*(in_hbm(value) for value in (own, partner, index_map, *link)))
    return list(outs[:number]), list(outs[number:])


def level(which, rows, partner, table):
    def kernel(rows_ref, partner_ref, table_ref, out_ref):
        @pl.when(side() == which)
        def _():
            total = mm(rows_ref[...], table_ref[0]) + mm(partner_ref[...], table_ref[1])
            out_ref[...] = total.astype(BF)

    out = jax.ShapeDtypeStruct(rows.shape, BF)
    return call(kernel, [out], [rows, partner, table], HINT)[0]


def both_parts(which, rows, partner, table, start, count):
    def kernel(rows_ref, partner_ref, table_ref, out_ref):
        @pl.when(side() == which)
        def _():
            block = slice(start, start + count)
            total = mm(rows_ref[block], table_ref[0]) + mm(partner_ref[block], table_ref[1])
            out_ref[...] = total.astype(BF)

    out = jax.ShapeDtypeStruct((count, rows.shape[1]), BF)
    return call(kernel, [out], [rows, partner, table], HINT)[0]


def pass_on(which, front, x, link, start):
    count = front.shape[0]

    def kernel(front_ref, x_ref, link_ref, out_ref):
        @pl.when(side() == which)
        def _():
            known = x_ref[start : start + count].astype(F32)
            out_ref[...] = (known + mm(front_ref[...], link_ref[...])).astype(BF)

    return call(kernel, [jax.ShapeDtypeStruct(front.shape, BF)], [front, x, link], HINT)[0]


def write_kernel(which, first_ref, second_ref, out_ref, sems):
    half = first_ref.shape[0]

    @pl.when(side() == which)
    def _():
        copies = [
            pltpu.make_async_copy(first_ref, out_ref.at[pl.ds(0, half)], sems.at[0]),
            pltpu.make_async_copy(second_ref, out_ref.at[pl.ds(half, half)], sems.at[1]),
        ]
        for copy in copies:
            copy.start()
        for copy in copies:
            copy.wait()


def write_first(which, blocks):
    half, width = blocks[0].shape
    return pl.pallas_call(
        lambda first, second, out, sems: write_kernel(which, first, second, out, sems),
        out_shape=pltpu.HBM((2 * half, width), BF),
        in_specs=[VMEM, VMEM],
        out_specs=HBM,
        scratch_shapes=[pltpu.SemaphoreType.DMA((2,))],
        compiler_params=pltpu.CompilerParams(vmem_limit_bytes=2 * MIB),
        cost_estimate=cost(0, 8 * blocks[0].size),
    )(*blocks)


def write_rest(which, out, blocks):
    return pl.pallas_call(
        lambda first, second, _, out, sems: write_kernel(which, first, second, out, sems),
        out_shape=pltpu.HBM(out.shape, BF),
        in_specs=[VMEM, VMEM, HBM],
        out_specs=HBM,
        scratch_shapes=[pltpu.SemaphoreType.DMA((2,))],
        input_output_aliases={2: 0},
        compiler_params=pltpu.CompilerParams(vmem_limit_bytes=2 * MIB),
        cost_estimate=cost(0, 8 * blocks[0].size),
    )(*blocks, out)


def permute(value, target):
    sections, leaves = lax.axis_size("sweep"), lax.axis_size("leaf")
    pairs = []
    for s in range(sections):
        for l in range(leaves):
            to = target(s, l)
            if to is not None:
                pairs.append((s * leaves + l, to[0] * leaves + to[1]))
    return lax.ppermute(value, ("sweep", "leaf"), pairs)


def swap(value, bit, row=None):
    idle = 2 if bit == 1 else 1
    return permute(value, lambda s, l: (s, l ^ (bit if row in (None, s) else idle)))


def cross(value, bit=0):
    return permute(value, lambda s, l: (s ^ 1, l ^ bit))


def behind(rows, *values):
    rows, *values = lax.optimization_barrier((rows, *values))
    return rows, values


def paired(sources, solve_tiles, self_merge, partner_merge, coupling, front_map):
    solve = solve_tiles[0, 0]
    sections = lax.axis_size("sweep")
    count = self_merge.shape[2]

    x = load(sources[0, 0], solve)
    half = x.shape[0] // 2
    rows, raw = behind(x, self_merge, partner_merge, front_map, coupling)
    own = prepare(*(v[0, 0] for v in raw[:3]), [0, 1])[0]
    other = [None] * count
    own_link = None
    front = None
    even, odd = [], []
    back = out = None
    for section in range(sections):
        if section % 2 == 0:
            if section > 0:
                turn = {section - 1: section, section: section - 1}
                front = [permute(part, lambda s, l: (turn.get(s, s), l)) for part in front]
                rows = [pass_on(0, part, x, own_link, k * half) for k, part in enumerate(front)]
                rows = jnp.concatenate(rows)
            if section == 0:
                other[:2] = [cross(table) for table in own]
            came, partner = cross(rows), cross(rows, 1)
            if section == 0:
                _, raw = behind(rows, *raw)
                more, (own_link,) = prepare(
                    *(v[0, 0] for v in raw[:3]),
                    list(range(2, count)),
                    link=(raw[3][0, 0], solve),
                )
                own += more
            front = [both_parts(1, came, partner, other[0], k * half, half) for k in range(2)]
            first, tables, row = 1, other, section + 1
        else:
            front = [pass_on(1, part, x, own_link, k * half) for k, part in enumerate(front)]
            first, tables, row = 0, own, section
        for j in range(first, count):
            if section == 0 and j == 1:
                first, (second, other[1], *late) = behind(*front, other[1], *own[2:])
                front = [first, second]
                other[2:] = [cross(table) for table in late]
            partners = [swap(part, 2**j, row) for part in front]
            if section % 2 and j == 1:
                _, back = behind(front[0], *back)
                back = [cross(part) for part in back]
            if section % 2 and j == 2:
                front[1], back = behind(front[1], *back)
                if sections == 2:
                    out = write_first(0, back)
                    front[1], (out,) = behind(front[1], out)
            front = [level(1, part, came, tables[j]) for part, came in zip(front, partners)]
        if section % 2 == 0:
            back = front
        elif section == 1:
            even, odd = back, front
        else:
            chosen = lax.axis_index("sweep") // 2 == section // 2
            even = [jnp.where(chosen, new, old) for new, old in zip(back, even)]
            odd = [jnp.where(chosen, new, old) for new, old in zip(front, odd)]
    if out is None:
        out = write_first(0, even)
    return write_rest(1, out, odd)[None, None]


def single(sources, solve_tiles, self_merge, partner_merge, coupling, front_map):
    rows, solve, link = sources[0, 0], solve_tiles[0, 0], coupling[0, 0]
    sections = lax.axis_size("sweep")
    front = jnp.zeros_like(rows)
    for section in range(sections):
        front = permute(front, lambda s, l: ((s + 1) % sections, l))
        front = jnp.where(lax.axis_index("sweep") == 0, jnp.zeros_like(front), front)
        x = mm((rows.astype(F32) + mm(front, link)).astype(BF), solve).astype(BF)
        for j in range(self_merge.shape[2]):
            mapped = jnp.take(swap(x, 2**j), front_map[0, 0, j], axis=1)
            x = (mm(x, self_merge[0, 0, j]) + mm(mapped, partner_merge[0, 0, j])).astype(BF)
        front = x
    return front[None, None]


def solution(mesh):
    spec = P("sweep", "leaf")
    return jax.shard_map(
        paired if mesh.shape["sweep"] % 2 == 0 else single,
        mesh=mesh,
        in_specs=(spec,) * 6,
        out_specs=spec,
        check_vma=False,
    )
```

```python
import jax
import jax.numpy as jnp
from jax import lax
from jax.experimental import pallas as pl
from jax.experimental.pallas import tpu as pltpu
from jax.sharding import PartitionSpec as P

BF = jnp.bfloat16
F32 = jnp.float32
MIB = 2**20
HINT = 10**8

HBM = pl.BlockSpec(memory_space=pltpu.HBM)
VMEM = pl.BlockSpec(memory_space=pltpu.VMEM)


def mm(left, right):
    return jnp.dot(left, right, preferred_element_type=F32)


def in_hbm(value):
    return pltpu.with_memory_space_constraint(value, pltpu.HBM)


def cost(flops, moved):
    return pl.CostEstimate(flops=flops, bytes_accessed=moved, transcendentals=0)


def side():
    return lax.rem(lax.axis_index("sweep"), 2)


def call(kernel, outs, args, flops, limit=4, **more):
    moved = sum(a.size * a.dtype.itemsize for a in args) + sum(o.size * 4 for o in outs)
    return pl.pallas_call(
        kernel,
        out_shape=tuple(pltpu.VMEM(o.shape, o.dtype) for o in outs),
        in_specs=[VMEM] * len(args),
        out_specs=(VMEM,) * len(outs),
        compiler_params=pltpu.CompilerParams(vmem_limit_bytes=limit * MIB),
        cost_estimate=cost(flops, moved),
        **more,
    )(*args)


def load_kernel(rows_hbm, solve_hbm, out_ref, rows_ref, solve_ref, sems):
    copies = [
        pltpu.make_async_copy(rows_hbm, rows_ref, sems.at[0]),
        pltpu.make_async_copy(solve_hbm, solve_ref, sems.at[1]),
    ]
    for copy in copies:
        copy.start()
    for copy in copies:
        copy.wait()
    out_ref[...] = mm(rows_ref[...], solve_ref[...]).astype(BF)


def load(rows, solve):
    return pl.pallas_call(
        load_kernel,
        out_shape=pltpu.VMEM(rows.shape, BF),
        in_specs=[HBM, HBM],
        out_specs=VMEM,
        scratch_shapes=[
            pltpu.VMEM(rows.shape, BF),
            pltpu.VMEM(solve.shape, BF),
            pltpu.SemaphoreType.DMA((2,)),
        ],
        compiler_params=pltpu.CompilerParams(vmem_limit_bytes=2 * MIB),
        cost_estimate=cost(2 * rows.size * solve.shape[1], 4 * rows.size + 2 * solve.size),
    )(in_hbm(rows), in_hbm(solve))


def prepare_kernel(levels, single, link, own_hbm, partner_hbm, map_hbm, *refs):
    number = len(levels)
    width = own_hbm.shape[1]
    link_hbm, refs = refs[: 2 * link], refs[2 * link :]
    outs, refs = refs[:number], refs[number:]
    singles, refs = refs[: 2 * single], refs[2 * single :]
    products, (partner_ref, map_ref, link_ref, sems, map_sem) = refs[:link], refs[link:]
    map_copy = pltpu.make_async_copy(map_hbm, map_ref, map_sem)
    map_copy.start()
    copies = []
    for k, j in enumerate(levels):
        pair = (
            pltpu.make_async_copy(partner_hbm.at[j], partner_ref.at[k], sems.at[2 * k]),
            pltpu.make_async_copy(own_hbm.at[j], outs[k].at[0], sems.at[2 * k + 1]),
        )
        for copy in pair:
            copy.start()
        copies.append(pair)
    extra = []
    if single:
        extra.append((own_hbm.at[levels[0]], singles[0]))
    for k, source in enumerate(link_hbm):
        extra.append((source, link_ref.at[k]))
    extra = [
        pltpu.make_async_copy(source, target, sems.at[2 * number + k])
        for k, (source, target) in enumerate(extra)
    ]
    for copy in extra:
        copy.start()
    map_copy.wait()
    rows = lax.broadcasted_iota(jnp.int32, (width, width), 0)
    for k, j in enumerate(levels):
        copies[k][0].wait()
        hot = (rows == map_ref[j : j + 1, :]).astype(BF)
        folded = mm(hot, partner_ref[k]).astype(BF)
        outs[k][1] = folded
        if single and k == 0:
            singles[1][...] = folded
    for copy in extra:
        copy.wait()
    if link:
        products[0][...] = mm(link_ref[0], link_ref[1]).astype(BF)
    for pair in copies:
        pair[1].wait()


def prepare(own, partner, index_map, levels, single=0, link=()):
    width = own.shape[1]
    number = len(levels)
    more = len(link) // 2
    outs = pl.pallas_call(
        lambda *refs: prepare_kernel(levels, single, more, *refs),
        out_shape=(pltpu.VMEM((2, width, width), BF),) * number
        + (pltpu.VMEM((width, width), BF),) * (2 * single + more),
        in_specs=[HBM] * (3 + len(link)),
        out_specs=(VMEM,) * (number + 2 * single + more),
        scratch_shapes=[
            pltpu.VMEM((number, width, width), BF),
            pltpu.VMEM(index_map.shape, jnp.int32),
            pltpu.VMEM((2, width, width), BF),
            pltpu.SemaphoreType.DMA((2 * number + 2,)),
            pltpu.SemaphoreType.DMA,
        ],
        compiler_params=pltpu.CompilerParams(vmem_limit_bytes=8 * MIB),
        cost_estimate=cost(2 * number * width**3, 8 * number * width**2),
    )(*(in_hbm(value) for value in (own, partner, index_map, *link)))
    return list(outs[:number]), list(outs[number:])


def level(which, rows, partner, table):
    def kernel(rows_ref, partner_ref, table_ref, out_ref):
        @pl.when(side() == which)
        def _():
            total = mm(rows_ref[...], table_ref[0]) + mm(partner_ref[...], table_ref[1])
            out_ref[...] = total.astype(BF)

    out = jax.ShapeDtypeStruct(rows.shape, BF)
    return call(kernel, [out], [rows, partner, table], HINT)[0]


def both_parts(which, rows, partner, table, start, count):
    def kernel(rows_ref, partner_ref, table_ref, out_ref):
        @pl.when(side() == which)
        def _():
            block = slice(start, start + count)
            total = mm(rows_ref[block], table_ref[0]) + mm(partner_ref[block], table_ref[1])
            out_ref[...] = total.astype(BF)

    out = jax.ShapeDtypeStruct((count, rows.shape[1]), BF)
    return call(kernel, [out], [rows, partner, table], HINT)[0]


def pass_on(which, front, x, link, start):
    count = front.shape[0]

    def kernel(front_ref, x_ref, link_ref, out_ref):
        @pl.when(side() == which)
        def _():
            known = x_ref[start : start + count].astype(F32)
            out_ref[...] = (known + mm(front_ref[...], link_ref[...])).astype(BF)

    return call(kernel, [jax.ShapeDtypeStruct(front.shape, BF)], [front, x, link], HINT)[0]


def write_kernel(which, first_ref, second_ref, out_ref, sems):
    half = first_ref.shape[0]

    @pl.when(side() == which)
    def _():
        copies = [
            pltpu.make_async_copy(first_ref, out_ref.at[pl.ds(0, half)], sems.at[0]),
            pltpu.make_async_copy(second_ref, out_ref.at[pl.ds(half, half)], sems.at[1]),
        ]
        for copy in copies:
            copy.start()
        for copy in copies:
            copy.wait()


def write_first(which, blocks):
    half, width = blocks[0].shape
    return pl.pallas_call(
        lambda first, second, out, sems: write_kernel(which, first, second, out, sems),
        out_shape=pltpu.HBM((2 * half, width), BF),
        in_specs=[VMEM, VMEM],
        out_specs=HBM,
        scratch_shapes=[pltpu.SemaphoreType.DMA((2,))],
        compiler_params=pltpu.CompilerParams(vmem_limit_bytes=2 * MIB),
        cost_estimate=cost(0, 8 * blocks[0].size),
    )(*blocks)


def write_rest(which, out, blocks):
    return pl.pallas_call(
        lambda first, second, _, out, sems: write_kernel(which, first, second, out, sems),
        out_shape=pltpu.HBM(out.shape, BF),
        in_specs=[VMEM, VMEM, HBM],
        out_specs=HBM,
        scratch_shapes=[pltpu.SemaphoreType.DMA((2,))],
        input_output_aliases={2: 0},
        compiler_params=pltpu.CompilerParams(vmem_limit_bytes=2 * MIB),
        cost_estimate=cost(0, 8 * blocks[0].size),
    )(*blocks, out)


def permute(value, target):
    sections, leaves = lax.axis_size("sweep"), lax.axis_size("leaf")
    pairs = []
    for s in range(sections):
        for l in range(leaves):
            to = target(s, l)
            if to is not None:
                pairs.append((s * leaves + l, to[0] * leaves + to[1]))
    return lax.ppermute(value, ("sweep", "leaf"), pairs)


def swap(value, bit, row):
    def target(s, l):
        ring = 2 if (l ^ l >> 1) & 1 else 1
        return s, l ^ (bit if s == row else ring)

    return permute(value, target)


def cross(value, bit=0):
    return permute(value, lambda s, l: (s ^ 1, l ^ bit))


def behind(rows, *values):
    rows, *values = lax.optimization_barrier((rows, *values))
    return rows, values


def paired(sources, solve_tiles, self_merge, partner_merge, coupling, front_map):
    solve = solve_tiles[0, 0]
    sections = lax.axis_size("sweep")
    count = self_merge.shape[2]

    x = load(sources[0, 0], solve)
    half = x.shape[0] // 2
    rows, raw = behind(x, self_merge, partner_merge, front_map, coupling)
    own = prepare(*(v[0, 0] for v in raw[:3]), [0, 1])[0]
    other = [None] * count
    own_link = None
    front = None
    even, odd = [], []
    back = out = None
    for section in range(sections):
        if section % 2 == 0:
            if section > 0:
                turn = {section - 1: section, section: section - 1}
                front = [permute(part, lambda s, l: (turn.get(s, s), l)) for part in front]
                rows = [pass_on(0, part, x, own_link, k * half) for k, part in enumerate(front)]
                rows = jnp.concatenate(rows)
            rows = both_parts(0, rows, swap(rows, 1, section), own[0], 0, 2 * half)
            if section == 0:
                rows, (table,) = behind(rows, own[1])
                other[1] = cross(table)
            came = cross(rows)
            partner = cross(rows, 2)
            if section == 0:
                _, raw = behind(rows, *raw)
                more, (own_link,) = prepare(
                    *(v[0, 0] for v in raw[:3]),
                    list(range(2, count)),
                    link=(raw[3][0, 0], solve),
                )
                own += more
            front = [both_parts(1, came, partner, other[1], k * half, half) for k in range(2)]
            first, tables, row = 2, other, section + 1
        else:
            front = [pass_on(1, part, x, own_link, k * half) for k, part in enumerate(front)]
            first, tables, row = 0, own, section
        for j in range(first, count):
            if section == 0 and j == 2:
                _, late = behind(front[0], *own[2:])
                other[2:] = [cross(table) for table in late]
            partners = [swap(part, 2**j, row) for part in front]
            if section % 2 and j == 1:
                _, back = behind(front[0], *back)
                back = [cross(part) for part in back]
            if section % 2 and j == 2:
                front[1], back = behind(front[1], *back)
                if sections == 2:
                    out = write_first(0, back)
                    front[1], (out,) = behind(front[1], out)
            front = [level(1, part, came, tables[j]) for part, came in zip(front, partners)]
        if section % 2 == 0:
            back = front
        elif section == 1:
            even, odd = back, front
        else:
            chosen = lax.axis_index("sweep") // 2 == section // 2
            even = [jnp.where(chosen, new, old) for new, old in zip(back, even)]
            odd = [jnp.where(chosen, new, old) for new, old in zip(front, odd)]
    if out is None:
        out = write_first(0, even)
    return write_rest(1, out, odd)[None, None]


def single(sources, solve_tiles, self_merge, partner_merge, coupling, front_map):
    rows, solve, link = sources[0, 0], solve_tiles[0, 0], coupling[0, 0]
    sections = lax.axis_size("sweep")
    front = jnp.zeros_like(rows)
    for section in range(sections):
        front = permute(front, lambda s, l: ((s + 1) % sections, l))
        front = jnp.where(lax.axis_index("sweep") == 0, jnp.zeros_like(front), front)
        x = mm((rows.astype(F32) + mm(front, link)).astype(BF), solve).astype(BF)
        for j in range(self_merge.shape[2]):
            mapped = jnp.take(swap(x, 2**j), front_map[0, 0, j], axis=1)
            x = (mm(x, self_merge[0, 0, j]) + mm(mapped, partner_merge[0, 0, j])).astype(BF)
        front = x
    return front[None, None]


def solution(mesh):
    spec = P("sweep", "leaf")
    return jax.shard_map(
        paired if mesh.shape["sweep"] % 2 == 0 else single,
        mesh=mesh,
        in_specs=(spec,) * 6,
        out_specs=spec,
        check_vma=False,
    )
```

```python
import jax
import jax.numpy as jnp
from jax import lax
from jax.experimental import pallas as pl
from jax.experimental.pallas import tpu as pltpu
from jax.sharding import PartitionSpec as P

BF = jnp.bfloat16
F32 = jnp.float32
MIB = 2**20
HINT = 10**8

HBM = pl.BlockSpec(memory_space=pltpu.HBM)
VMEM = pl.BlockSpec(memory_space=pltpu.VMEM)


def mm(left, right):
    return jnp.dot(left, right, preferred_element_type=F32)


def in_hbm(value):
    return pltpu.with_memory_space_constraint(value, pltpu.HBM)


def cost(flops, moved):
    return pl.CostEstimate(flops=flops, bytes_accessed=moved, transcendentals=0)


def side():
    return lax.rem(lax.axis_index("sweep"), 2)


def call(kernel, outs, args, flops, limit=4, **more):
    moved = sum(a.size * a.dtype.itemsize for a in args) + sum(o.size * 4 for o in outs)
    return pl.pallas_call(
        kernel,
        out_shape=tuple(pltpu.VMEM(o.shape, o.dtype) for o in outs),
        in_specs=[VMEM] * len(args),
        out_specs=(VMEM,) * len(outs),
        compiler_params=pltpu.CompilerParams(vmem_limit_bytes=limit * MIB),
        cost_estimate=cost(flops, moved),
        **more,
    )(*args)


def load_kernel(rows_hbm, solve_hbm, out_ref, rows_ref, solve_ref, sems):
    copies = [
        pltpu.make_async_copy(rows_hbm, rows_ref, sems.at[0]),
        pltpu.make_async_copy(solve_hbm, solve_ref, sems.at[1]),
    ]
    for copy in copies:
        copy.start()
    for copy in copies:
        copy.wait()
    out_ref[...] = mm(rows_ref[...], solve_ref[...]).astype(BF)


def load(rows, solve):
    return pl.pallas_call(
        load_kernel,
        out_shape=pltpu.VMEM(rows.shape, BF),
        in_specs=[HBM, HBM],
        out_specs=VMEM,
        scratch_shapes=[
            pltpu.VMEM(rows.shape, BF),
            pltpu.VMEM(solve.shape, BF),
            pltpu.SemaphoreType.DMA((2,)),
        ],
        compiler_params=pltpu.CompilerParams(vmem_limit_bytes=2 * MIB),
        cost_estimate=cost(2 * rows.size * solve.shape[1], 4 * rows.size + 2 * solve.size),
    )(in_hbm(rows), in_hbm(solve))


def prepare_kernel(levels, single, link, joined, own_hbm, partner_hbm, map_hbm, *refs):
    number = len(levels)
    width = own_hbm.shape[1]
    link_hbm, refs = refs[: 2 * link], refs[2 * link :]
    if joined:
        outs = [refs[0].at[pl.ds(2 * k, 2)] for k in range(number)]
        refs = refs[1:]
    else:
        outs, refs = refs[:number], refs[number:]
    singles, refs = refs[: 2 * single], refs[2 * single :]
    products, (partner_ref, map_ref, link_ref, sems, map_sem) = refs[:link], refs[link:]
    map_copy = pltpu.make_async_copy(map_hbm, map_ref, map_sem)
    map_copy.start()
    copies = []
    for k, j in enumerate(levels):
        pair = (
            pltpu.make_async_copy(partner_hbm.at[j], partner_ref.at[k], sems.at[2 * k]),
            pltpu.make_async_copy(own_hbm.at[j], outs[k].at[0], sems.at[2 * k + 1]),
        )
        for copy in pair:
            copy.start()
        copies.append(pair)
    extra = []
    if single:
        extra.append((own_hbm.at[levels[0]], singles[0]))
    for k, source in enumerate(link_hbm):
        extra.append((source, link_ref.at[k]))
    extra = [
        pltpu.make_async_copy(source, target, sems.at[2 * number + k])
        for k, (source, target) in enumerate(extra)
    ]
    for copy in extra:
        copy.start()
    map_copy.wait()
    rows = lax.broadcasted_iota(jnp.int32, (width, width), 0)
    for k, j in enumerate(levels):
        copies[k][0].wait()
        hot = (rows == map_ref[j : j + 1, :]).astype(BF)
        folded = mm(hot, partner_ref[k]).astype(BF)
        outs[k][1] = folded
        if single and k == 0:
            singles[1][...] = folded
    for copy in extra:
        copy.wait()
    if link:
        products[0][...] = mm(link_ref[0], link_ref[1]).astype(BF)
    for pair in copies:
        pair[1].wait()


def prepare(own, partner, index_map, levels, single=0, link=(), joined=False):
    width = own.shape[1]
    number = len(levels)
    more = len(link) // 2
    tables = 1 if joined else number
    outs = pl.pallas_call(
        lambda *refs: prepare_kernel(levels, single, more, joined, *refs),
        out_shape=(pltpu.VMEM((2 * number // tables, width, width), BF),) * tables
        + (pltpu.VMEM((width, width), BF),) * (2 * single + more),
        in_specs=[HBM] * (3 + len(link)),
        out_specs=(VMEM,) * (tables + 2 * single + more),
        scratch_shapes=[
            pltpu.VMEM((number, width, width), BF),
            pltpu.VMEM(index_map.shape, jnp.int32),
            pltpu.VMEM((2, width, width), BF),
            pltpu.SemaphoreType.DMA((2 * number + 2,)),
            pltpu.SemaphoreType.DMA,
        ],
        compiler_params=pltpu.CompilerParams(vmem_limit_bytes=8 * MIB),
        cost_estimate=cost(2 * number * width**3, 8 * number * width**2),
    )(*(in_hbm(value) for value in (own, partner, index_map, *link)))
    return list(outs[:tables]), list(outs[tables:])


def level(which, rows, partner, table, at):
    def kernel(rows_ref, partner_ref, table_ref, out_ref):
        @pl.when(side() == which)
        def _():
            total = mm(rows_ref[...], table_ref[at]) + mm(partner_ref[...], table_ref[at + 1])
            out_ref[...] = total.astype(BF)

    out = jax.ShapeDtypeStruct(rows.shape, BF)
    return call(kernel, [out], [rows, partner, table], HINT)[0]


def both_parts(which, rows, partner, table, start, count):
    def kernel(rows_ref, partner_ref, table_ref, out_ref):
        @pl.when(side() == which)
        def _():
            block = slice(start, start + count)
            total = mm(rows_ref[block], table_ref[0]) + mm(partner_ref[block], table_ref[1])
            out_ref[...] = total.astype(BF)

    out = jax.ShapeDtypeStruct((count, rows.shape[1]), BF)
    return call(kernel, [out], [rows, partner, table], HINT)[0]


def pass_on(which, front, x, link, start):
    count = front.shape[0]

    def kernel(front_ref, x_ref, link_ref, out_ref):
        @pl.when(side() == which)
        def _():
            known = x_ref[start : start + count].astype(F32)
            out_ref[...] = (known + mm(front_ref[...], link_ref[...])).astype(BF)

    return call(kernel, [jax.ShapeDtypeStruct(front.shape, BF)], [front, x, link], HINT)[0]


def write_kernel(which, first_ref, second_ref, out_ref, sems):
    half = first_ref.shape[0]

    @pl.when(side() == which)
    def _():
        copies = [
            pltpu.make_async_copy(first_ref, out_ref.at[pl.ds(0, half)], sems.at[0]),
            pltpu.make_async_copy(second_ref, out_ref.at[pl.ds(half, half)], sems.at[1]),
        ]
        for copy in copies:
            copy.start()
        for copy in copies:
            copy.wait()


def write_first(which, blocks):
    half, width = blocks[0].shape
    return pl.pallas_call(
        lambda first, second, out, sems: write_kernel(which, first, second, out, sems),
        out_shape=pltpu.HBM((2 * half, width), BF),
        in_specs=[VMEM, VMEM],
        out_specs=HBM,
        scratch_shapes=[pltpu.SemaphoreType.DMA((2,))],
        compiler_params=pltpu.CompilerParams(vmem_limit_bytes=2 * MIB),
        cost_estimate=cost(0, 8 * blocks[0].size),
    )(*blocks)


def write_rest(which, out, blocks):
    return pl.pallas_call(
        lambda first, second, _, out, sems: write_kernel(which, first, second, out, sems),
        out_shape=pltpu.HBM(out.shape, BF),
        in_specs=[VMEM, VMEM, HBM],
        out_specs=HBM,
        scratch_shapes=[pltpu.SemaphoreType.DMA((2,))],
        input_output_aliases={2: 0},
        compiler_params=pltpu.CompilerParams(vmem_limit_bytes=2 * MIB),
        cost_estimate=cost(0, 8 * blocks[0].size),
    )(*blocks, out)


def finish(which, out, first, rows, partner, table, at):
    half, width = rows.shape

    def kernel(first_ref, rows_ref, partner_ref, table_ref, _, out_ref, second_ref, sems):
        @pl.when(side() == which)
        def _():
            head = pltpu.make_async_copy(first_ref, out_ref.at[pl.ds(0, half)], sems.at[0])
            head.start()
            total = mm(rows_ref[...], table_ref[at]) + mm(partner_ref[...], table_ref[at + 1])
            second_ref[...] = total.astype(BF)
            tail = pltpu.make_async_copy(second_ref, out_ref.at[pl.ds(half, half)], sems.at[1])
            tail.start()
            head.wait()
            tail.wait()

    return pl.pallas_call(
        kernel,
        out_shape=pltpu.HBM(out.shape, BF),
        in_specs=[VMEM] * 4 + [HBM],
        out_specs=HBM,
        scratch_shapes=[pltpu.VMEM((half, width), BF), pltpu.SemaphoreType.DMA((2,))],
        input_output_aliases={4: 0},
        compiler_params=pltpu.CompilerParams(vmem_limit_bytes=4 * MIB),
        cost_estimate=cost(HINT, 8 * rows.size),
    )(first, rows, partner, table, out)


def permute(value, target):
    sections, leaves = lax.axis_size("sweep"), lax.axis_size("leaf")
    pairs = []
    for s in range(sections):
        for l in range(leaves):
            to = target(s, l)
            if to is not None:
                pairs.append((s * leaves + l, to[0] * leaves + to[1]))
    return lax.ppermute(value, ("sweep", "leaf"), pairs)


def swap(value, bit, row):
    def target(s, l):
        ring = 2 if (l ^ l >> 1) & 1 else 1
        return s, l ^ (bit if s == row else ring)

    return permute(value, target)


def cross(value, bit=0):
    return permute(value, lambda s, l: (s ^ 1, l ^ bit))


def behind(rows, *values):
    rows, *values = lax.optimization_barrier((rows, *values))
    return rows, values


def paired(sources, solve_tiles, self_merge, partner_merge, coupling, front_map):
    solve = solve_tiles[0, 0]
    sections = lax.axis_size("sweep")
    count = self_merge.shape[2]

    x = load(sources[0, 0], solve)
    half = x.shape[0] // 2
    rows, raw = behind(x, self_merge, partner_merge, front_map, coupling)
    own = [(table, 0) for table in prepare(*(v[0, 0] for v in raw[:3]), [0, 1])[0]]
    other = [None] * count
    own_link = later = None
    front = None
    even, odd = [], []
    back = out = None
    for section in range(sections):
        if section % 2 == 0:
            if section > 0:
                turn = {section - 1: section, section: section - 1}
                front = [permute(part, lambda s, l: (turn.get(s, s), l)) for part in front]
                rows = [pass_on(0, part, x, own_link, k * half) for k, part in enumerate(front)]
                rows = jnp.concatenate(rows)
            rows = both_parts(0, rows, swap(rows, 1, section), own[0][0], 0, 2 * half)
            if section == 0:
                rows, (table,) = behind(rows, own[1][0])
                other[1] = (cross(table), 0)
            came = cross(rows)
            partner = cross(rows, 2)
            if section == 0:
                _, raw = behind(rows, *raw)
                (later,), (own_link,) = prepare(
                    *(v[0, 0] for v in raw[:3]),
                    list(range(2, count)),
                    link=(raw[3][0, 0], solve),
                    joined=True,
                )
                own += [(later, 2 * k) for k in range(count - 2)]
            front = [both_parts(1, came, partner, other[1][0], k * half, half) for k in range(2)]
            first, tables, row = 2, other, section + 1
        else:
            front = [pass_on(1, part, x, own_link, k * half) for k, part in enumerate(front)]
            first, tables, row = 0, own, section
        for j in range(first, count):
            if section == 0 and j == 2:
                late = cross(behind(front[0], later)[1][0])
                other[2:] = [(late, 2 * k) for k in range(count - 2)]
            partners = [swap(part, 2**j, row) for part in front]
            if section % 2 and j == 1:
                _, back = behind(front[0], *back)
                back = [cross(part) for part in back]
            if section % 2 and j == 2:
                front[1], back = behind(front[1], *back)
                if sections == 2:
                    out = write_first(0, back)
                    front[1], (out,) = behind(front[1], out)
            if sections == 2 and section == 1 and j == count - 1:
                first = level(1, front[0], partners[0], *tables[j])
                return finish(1, out, first, front[1], partners[1], *tables[j])[None, None]
            front = [level(1, part, came, *tables[j]) for part, came in zip(front, partners)]
        if section % 2 == 0:
            back = front
        elif section == 1:
            even, odd = back, front
        else:
            chosen = lax.axis_index("sweep") // 2 == section // 2
            even = [jnp.where(chosen, new, old) for new, old in zip(back, even)]
            odd = [jnp.where(chosen, new, old) for new, old in zip(front, odd)]
    if out is None:
        out = write_first(0, even)
    return write_rest(1, out, odd)[None, None]


def single(sources, solve_tiles, self_merge, partner_merge, coupling, front_map):
    rows, solve, link = sources[0, 0], solve_tiles[0, 0], coupling[0, 0]
    sections = lax.axis_size("sweep")
    front = jnp.zeros_like(rows)
    for section in range(sections):
        front = permute(front, lambda s, l: ((s + 1) % sections, l))
        front = jnp.where(lax.axis_index("sweep") == 0, jnp.zeros_like(front), front)
        x = mm((rows.astype(F32) + mm(front, link)).astype(BF), solve).astype(BF)
        for j in range(self_merge.shape[2]):
            mapped = jnp.take(
                permute(x, lambda s, l: (s, l ^ 2**j)), front_map[0, 0, j], axis=1
            )
            x = (mm(x, self_merge[0, 0, j]) + mm(mapped, partner_merge[0, 0, j])).astype(BF)
        front = x
    return front[None, None]


def solution(mesh):
    spec = P("sweep", "leaf")
    return jax.shard_map(
        paired if mesh.shape["sweep"] % 2 == 0 else single,
        mesh=mesh,
        in_specs=(spec,) * 6,
        out_specs=spec,
        check_vma=False,
    )
```

```python
import jax
import jax.numpy as jnp
from jax import lax
from jax.experimental import pallas as pl
from jax.experimental.pallas import tpu as pltpu
from jax.sharding import PartitionSpec as P

BF = jnp.bfloat16
F32 = jnp.float32
MIB = 2**20
HINT = 10**8

HBM = pl.BlockSpec(memory_space=pltpu.HBM)
VMEM = pl.BlockSpec(memory_space=pltpu.VMEM)


def mm(left, right):
    return jnp.dot(left, right, preferred_element_type=F32)


def in_hbm(value):
    return pltpu.with_memory_space_constraint(value, pltpu.HBM)


def cost(flops, moved):
    return pl.CostEstimate(flops=flops, bytes_accessed=moved, transcendentals=0)


def side():
    return lax.rem(lax.axis_index("sweep"), 2)


def call(kernel, outs, args, flops, limit=4, **more):
    moved = sum(a.size * a.dtype.itemsize for a in args) + sum(o.size * 4 for o in outs)
    return pl.pallas_call(
        kernel,
        out_shape=tuple(pltpu.VMEM(o.shape, o.dtype) for o in outs),
        in_specs=[VMEM] * len(args),
        out_specs=(VMEM,) * len(outs),
        compiler_params=pltpu.CompilerParams(vmem_limit_bytes=limit * MIB),
        cost_estimate=cost(flops, moved),
        **more,
    )(*args)


def load_kernel(rows_hbm, solve_hbm, out_ref, rows_ref, solve_ref, sems):
    copies = [
        pltpu.make_async_copy(rows_hbm, rows_ref, sems.at[0]),
        pltpu.make_async_copy(solve_hbm, solve_ref, sems.at[1]),
    ]
    for copy in copies:
        copy.start()
    for copy in copies:
        copy.wait()
    out_ref[...] = mm(rows_ref[...], solve_ref[...]).astype(BF)


def load(rows, solve):
    return pl.pallas_call(
        load_kernel,
        out_shape=pltpu.VMEM(rows.shape, BF),
        in_specs=[HBM, HBM],
        out_specs=VMEM,
        scratch_shapes=[
            pltpu.VMEM(rows.shape, BF),
            pltpu.VMEM(solve.shape, BF),
            pltpu.SemaphoreType.DMA((2,)),
        ],
        compiler_params=pltpu.CompilerParams(vmem_limit_bytes=2 * MIB),
        cost_estimate=cost(2 * rows.size * solve.shape[1], 4 * rows.size + 2 * solve.size),
    )(in_hbm(rows), in_hbm(solve))


def prepare_kernel(levels, single, link, own_hbm, partner_hbm, map_hbm, *refs):
    number = len(levels)
    width = own_hbm.shape[1]
    link_hbm, refs = refs[: 2 * link], refs[2 * link :]
    outs, refs = refs[:number], refs[number:]
    singles, refs = refs[: 2 * single], refs[2 * single :]
    products, (partner_ref, map_ref, link_ref, sems, map_sem) = refs[:link], refs[link:]
    map_copy = pltpu.make_async_copy(map_hbm, map_ref, map_sem)
    map_copy.start()
    copies = []
    for k, j in enumerate(levels):
        pair = (
            pltpu.make_async_copy(partner_hbm.at[j], partner_ref.at[k], sems.at[2 * k]),
            pltpu.make_async_copy(own_hbm.at[j], outs[k].at[0], sems.at[2 * k + 1]),
        )
        for copy in pair:
            copy.start()
        copies.append(pair)
    extra = []
    if single:
        extra.append((own_hbm.at[levels[0]], singles[0]))
    for k, source in enumerate(link_hbm):
        extra.append((source, link_ref.at[k]))
    extra = [
        pltpu.make_async_copy(source, target, sems.at[2 * number + k])
        for k, (source, target) in enumerate(extra)
    ]
    for copy in extra:
        copy.start()
    map_copy.wait()
    rows = lax.broadcasted_iota(jnp.int32, (width, width), 0)
    for k, j in enumerate(levels):
        copies[k][0].wait()
        hot = (rows == map_ref[j : j + 1, :]).astype(BF)
        folded = mm(hot, partner_ref[k]).astype(BF)
        outs[k][1] = folded
        if single and k == 0:
            singles[1][...] = folded
    for copy in extra:
        copy.wait()
    if link:
        products[0][...] = mm(link_ref[0], link_ref[1]).astype(BF)
    for pair in copies:
        pair[1].wait()


def prepare(own, partner, index_map, levels, single=0, link=()):
    width = own.shape[1]
    number = len(levels)
    more = len(link) // 2
    outs = pl.pallas_call(
        lambda *refs: prepare_kernel(levels, single, more, *refs),
        out_shape=(pltpu.VMEM((2, width, width), BF),) * number
        + (pltpu.VMEM((width, width), BF),) * (2 * single + more),
        in_specs=[HBM] * (3 + len(link)),
        out_specs=(VMEM,) * (number + 2 * single + more),
        scratch_shapes=[
            pltpu.VMEM((number, width, width), BF),
            pltpu.VMEM(index_map.shape, jnp.int32),
            pltpu.VMEM((2, width, width), BF),
            pltpu.SemaphoreType.DMA((2 * number + 2,)),
            pltpu.SemaphoreType.DMA,
        ],
        compiler_params=pltpu.CompilerParams(vmem_limit_bytes=8 * MIB),
        cost_estimate=cost(2 * number * width**3, 8 * number * width**2),
    )(*(in_hbm(value) for value in (own, partner, index_map, *link)))
    return list(outs[:number]), list(outs[number:])


def level(which, rows, partner, table):
    def kernel(rows_ref, partner_ref, table_ref, out_ref):
        @pl.when(side() == which)
        def _():
            total = mm(rows_ref[...], table_ref[0]) + mm(partner_ref[...], table_ref[1])
            out_ref[...] = total.astype(BF)

    out = jax.ShapeDtypeStruct(rows.shape, BF)
    return call(kernel, [out], [rows, partner, table], HINT)[0]


def both_parts(which, rows, partner, table, start, count):
    def kernel(rows_ref, partner_ref, table_ref, out_ref):
        @pl.when(side() == which)
        def _():
            block = slice(start, start + count)
            total = mm(rows_ref[block], table_ref[0]) + mm(partner_ref[block], table_ref[1])
            out_ref[...] = total.astype(BF)

    out = jax.ShapeDtypeStruct((count, rows.shape[1]), BF)
    return call(kernel, [out], [rows, partner, table], HINT)[0]


def pass_on(which, front, x, link, start):
    count = front.shape[0]

    def kernel(front_ref, x_ref, link_ref, out_ref):
        @pl.when(side() == which)
        def _():
            known = x_ref[start : start + count].astype(F32)
            out_ref[...] = (known + mm(front_ref[...], link_ref[...])).astype(BF)

    return call(kernel, [jax.ShapeDtypeStruct(front.shape, BF)], [front, x, link], HINT)[0]


def write_kernel(which, first_ref, second_ref, out_ref, sems):
    half = first_ref.shape[0]

    @pl.when(side() == which)
    def _():
        copies = [
            pltpu.make_async_copy(first_ref, out_ref.at[pl.ds(0, half)], sems.at[0]),
            pltpu.make_async_copy(second_ref, out_ref.at[pl.ds(half, half)], sems.at[1]),
        ]
        for copy in copies:
            copy.start()
        for copy in copies:
            copy.wait()


def write_first(which, blocks):
    half, width = blocks[0].shape
    return pl.pallas_call(
        lambda first, second, out, sems: write_kernel(which, first, second, out, sems),
        out_shape=pltpu.HBM((2 * half, width), BF),
        in_specs=[VMEM, VMEM],
        out_specs=HBM,
        scratch_shapes=[pltpu.SemaphoreType.DMA((2,))],
        compiler_params=pltpu.CompilerParams(vmem_limit_bytes=2 * MIB),
        cost_estimate=cost(0, 8 * blocks[0].size),
    )(*blocks)


def write_rest(which, out, blocks):
    return pl.pallas_call(
        lambda first, second, _, out, sems: write_kernel(which, first, second, out, sems),
        out_shape=pltpu.HBM(out.shape, BF),
        in_specs=[VMEM, VMEM, HBM],
        out_specs=HBM,
        scratch_shapes=[pltpu.SemaphoreType.DMA((2,))],
        input_output_aliases={2: 0},
        compiler_params=pltpu.CompilerParams(vmem_limit_bytes=2 * MIB),
        cost_estimate=cost(0, 8 * blocks[0].size),
    )(*blocks, out)


def permute(value, target):
    sections, leaves = lax.axis_size("sweep"), lax.axis_size("leaf")
    pairs = []
    for s in range(sections):
        for l in range(leaves):
            to = target(s, l)
            if to is not None:
                pairs.append((s * leaves + l, to[0] * leaves + to[1]))
    return lax.ppermute(value, ("sweep", "leaf"), pairs)


def swap(value, bit, row):
    def target(s, l):
        ring = 2 if (l ^ l >> 1) & 1 else 1
        return s, l ^ (bit if s == row else ring)

    return permute(value, target)


def cross(value, bit=0):
    return permute(value, lambda s, l: (s ^ 1, l ^ bit))


def behind(rows, *values):
    rows, *values = lax.optimization_barrier((rows, *values))
    return rows, values


def paired(sources, solve_tiles, self_merge, partner_merge, coupling, front_map):
    solve = solve_tiles[0, 0]
    sections = lax.axis_size("sweep")
    count = self_merge.shape[2]

    x = load(sources[0, 0], solve)
    half = x.shape[0] // 2
    rows, raw = behind(x, self_merge, partner_merge, front_map, coupling)
    own = prepare(*(v[0, 0] for v in raw[:3]), [0, 1])[0]
    other = [None] * count
    own_link = None
    front = None
    even, odd = [], []
    back = out = None
    for section in range(sections):
        if section % 2 == 0:
            if section > 0:
                turn = {section - 1: section, section: section - 1}
                front = [permute(part, lambda s, l: (turn.get(s, s), l)) for part in front]
                rows = [pass_on(0, part, x, own_link, k * half) for k, part in enumerate(front)]
                rows = jnp.concatenate(rows)
            rows = both_parts(0, rows, swap(rows, 1, section), own[0], 0, 2 * half)
            if section == 0:
                rows, (table,) = behind(rows, own[1])
                other[1] = cross(table)
            came = cross(rows)
            partner = cross(rows, 2)
            if section == 0:
                _, raw = behind(rows, *raw)
                more, (own_link,) = prepare(
                    *(v[0, 0] for v in raw[:3]),
                    list(range(2, count)),
                    link=(raw[3][0, 0], solve),
                )
                own += more
            front = [both_parts(1, came, partner, other[1], k * half, half) for k in range(2)]
            first, tables, row = 2, other, section + 1
        else:
            front = [pass_on(1, part, x, own_link, k * half) for k, part in enumerate(front)]
            first, tables, row = 0, own, section
        for j in range(first, count):
            if section == 0 and j == 2:
                _, late = behind(front[0], *own[2:])
                other[2:] = [cross(table) for table in late]
            partners = [swap(part, 2**j, row) for part in front]
            if section % 2 and j == 1:
                _, back = behind(front[0], *back)
                back = [cross(part) for part in back]
            if section % 2 and j == 2:
                front[1], back = behind(front[1], *back)
                if sections == 2:
                    out = write_first(0, back)
                    front[1], (out,) = behind(front[1], out)
            front = [level(1, part, came, tables[j]) for part, came in zip(front, partners)]
        if section % 2 == 0:
            back = front
        elif section == 1:
            even, odd = back, front
        else:
            chosen = lax.axis_index("sweep") // 2 == section // 2
            even = [jnp.where(chosen, new, old) for new, old in zip(back, even)]
            odd = [jnp.where(chosen, new, old) for new, old in zip(front, odd)]
    if out is None:
        out = write_first(0, even)
    return write_rest(1, out, odd)[None, None]


def single(sources, solve_tiles, self_merge, partner_merge, coupling, front_map):
    rows, solve, link = sources[0, 0], solve_tiles[0, 0], coupling[0, 0]
    sections = lax.axis_size("sweep")
    front = jnp.zeros_like(rows)
    for section in range(sections):
        front = permute(front, lambda s, l: ((s + 1) % sections, l))
        front = jnp.where(lax.axis_index("sweep") == 0, jnp.zeros_like(front), front)
        x = mm((rows.astype(F32) + mm(front, link)).astype(BF), solve).astype(BF)
        for j in range(self_merge.shape[2]):
            other = permute(x, lambda s, l, bit=2**j: (s, l ^ bit))
            mapped = jnp.take(other, front_map[0, 0, j], axis=1)
            x = (mm(x, self_merge[0, 0, j]) + mm(mapped, partner_merge[0, 0, j])).astype(BF)
        front = x
    return front[None, None]


def solution(mesh):
    spec = P("sweep", "leaf")
    return jax.shard_map(
        paired if mesh.shape["sweep"] % 2 == 0 else single,
        mesh=mesh,
        in_specs=(spec,) * 6,
        out_specs=spec,
        check_vma=False,
    )
```

```python
import jax
import jax.numpy as jnp
from jax import lax
from jax.experimental import pallas as pl
from jax.experimental.pallas import tpu as pltpu
from jax.sharding import PartitionSpec as P

BF = jnp.bfloat16
F32 = jnp.float32
MIB = 2**20
HINT = 10**8

HBM = pl.BlockSpec(memory_space=pltpu.HBM)
VMEM = pl.BlockSpec(memory_space=pltpu.VMEM)


def mm(left, right):
    return jnp.dot(left, right, preferred_element_type=F32)


def in_hbm(value):
    return pltpu.with_memory_space_constraint(value, pltpu.HBM)


def cost(flops, moved):
    return pl.CostEstimate(flops=flops, bytes_accessed=moved, transcendentals=0)


def side():
    return lax.rem(lax.axis_index("sweep"), 2)


def call(kernel, outs, args, flops, limit=4, **more):
    moved = sum(a.size * a.dtype.itemsize for a in args) + sum(o.size * 4 for o in outs)
    return pl.pallas_call(
        kernel,
        out_shape=tuple(pltpu.VMEM(o.shape, o.dtype) for o in outs),
        in_specs=[VMEM] * len(args),
        out_specs=(VMEM,) * len(outs),
        compiler_params=pltpu.CompilerParams(vmem_limit_bytes=limit * MIB),
        cost_estimate=cost(flops, moved),
        **more,
    )(*args)


def load_kernel(rows_hbm, solve_hbm, out_ref, rows_ref, solve_ref, sems):
    copies = [
        pltpu.make_async_copy(rows_hbm, rows_ref, sems.at[0]),
        pltpu.make_async_copy(solve_hbm, solve_ref, sems.at[1]),
    ]
    for copy in copies:
        copy.start()
    for copy in copies:
        copy.wait()
    out_ref[...] = mm(rows_ref[...], solve_ref[...]).astype(BF)


def load(rows, solve):
    return pl.pallas_call(
        load_kernel,
        out_shape=pltpu.VMEM(rows.shape, BF),
        in_specs=[HBM, HBM],
        out_specs=VMEM,
        scratch_shapes=[
            pltpu.VMEM(rows.shape, BF),
            pltpu.VMEM(solve.shape, BF),
            pltpu.SemaphoreType.DMA((2,)),
        ],
        compiler_params=pltpu.CompilerParams(vmem_limit_bytes=2 * MIB),
        cost_estimate=cost(2 * rows.size * solve.shape[1], 4 * rows.size + 2 * solve.size),
    )(in_hbm(rows), in_hbm(solve))


def prepare_kernel(levels, single, link, own_hbm, partner_hbm, map_hbm, *refs):
    number = len(levels)
    width = own_hbm.shape[1]
    link_hbm, refs = refs[: 2 * link], refs[2 * link :]
    outs, refs = refs[:number], refs[number:]
    singles, refs = refs[: 2 * single], refs[2 * single :]
    products, (partner_ref, map_ref, link_ref, sems, map_sem) = refs[:link], refs[link:]
    map_copy = pltpu.make_async_copy(map_hbm, map_ref, map_sem)
    map_copy.start()
    copies = []
    for k, j in enumerate(levels):
        pair = (
            pltpu.make_async_copy(partner_hbm.at[j], partner_ref.at[k], sems.at[2 * k]),
            pltpu.make_async_copy(own_hbm.at[j], outs[k].at[0], sems.at[2 * k + 1]),
        )
        for copy in pair:
            copy.start()
        copies.append(pair)
    extra = []
    if single:
        extra.append((own_hbm.at[levels[0]], singles[0]))
    for k, source in enumerate(link_hbm):
        extra.append((source, link_ref.at[k]))
    extra = [
        pltpu.make_async_copy(source, target, sems.at[2 * number + k])
        for k, (source, target) in enumerate(extra)
    ]
    for copy in extra:
        copy.start()
    map_copy.wait()
    rows = lax.broadcasted_iota(jnp.int32, (width, width), 0)
    for k, j in enumerate(levels):
        copies[k][0].wait()
        hot = (rows == map_ref[j : j + 1, :]).astype(BF)
        folded = mm(hot, partner_ref[k]).astype(BF)
        outs[k][1] = folded
        if single and k == 0:
            singles[1][...] = folded
    for copy in extra:
        copy.wait()
    if link:
        products[0][...] = mm(link_ref[0], link_ref[1]).astype(BF)
    for pair in copies:
        pair[1].wait()


def prepare(own, partner, index_map, levels, single=0, link=()):
    width = own.shape[1]
    number = len(levels)
    more = len(link) // 2
    outs = pl.pallas_call(
        lambda *refs: prepare_kernel(levels, single, more, *refs),
        out_shape=(pltpu.VMEM((2, width, width), BF),) * number
        + (pltpu.VMEM((width, width), BF),) * (2 * single + more),
        in_specs=[HBM] * (3 + len(link)),
        out_specs=(VMEM,) * (number + 2 * single + more),
        scratch_shapes=[
            pltpu.VMEM((number, width, width), BF),
            pltpu.VMEM(index_map.shape, jnp.int32),
            pltpu.VMEM((2, width, width), BF),
            pltpu.SemaphoreType.DMA((2 * number + 2,)),
            pltpu.SemaphoreType.DMA,
        ],
        compiler_params=pltpu.CompilerParams(vmem_limit_bytes=8 * MIB),
        cost_estimate=cost(2 * number * width**3, 8 * number * width**2),
    )(*(in_hbm(value) for value in (own, partner, index_map, *link)))
    return list(outs[:number]), list(outs[number:])


def level(which, rows, partner, table):
    def kernel(rows_ref, partner_ref, table_ref, out_ref):
        @pl.when(side() == which)
        def _():
            total = mm(rows_ref[...], table_ref[0]) + mm(partner_ref[...], table_ref[1])
            out_ref[...] = total.astype(BF)

    out = jax.ShapeDtypeStruct(rows.shape, BF)
    return call(kernel, [out], [rows, partner, table], HINT)[0]


def both_parts(which, rows, partner, table, start, count):
    def kernel(rows_ref, partner_ref, table_ref, out_ref):
        @pl.when(side() == which)
        def _():
            block = slice(start, start + count)
            total = mm(rows_ref[block], table_ref[0]) + mm(partner_ref[block], table_ref[1])
            out_ref[...] = total.astype(BF)

    out = jax.ShapeDtypeStruct((count, rows.shape[1]), BF)
    return call(kernel, [out], [rows, partner, table], HINT)[0]


def pass_on(which, front, x, link, start):
    count = front.shape[0]

    def kernel(front_ref, x_ref, link_ref, out_ref):
        @pl.when(side() == which)
        def _():
            known = x_ref[start : start + count].astype(F32)
            out_ref[...] = (known + mm(front_ref[...], link_ref[...])).astype(BF)

    return call(kernel, [jax.ShapeDtypeStruct(front.shape, BF)], [front, x, link], HINT)[0]


def write_kernel(which, first_ref, second_ref, out_ref, sems):
    half = first_ref.shape[0]

    @pl.when(side() == which)
    def _():
        copies = [
            pltpu.make_async_copy(first_ref, out_ref.at[pl.ds(0, half)], sems.at[0]),
            pltpu.make_async_copy(second_ref, out_ref.at[pl.ds(half, half)], sems.at[1]),
        ]
        for copy in copies:
            copy.start()
        for copy in copies:
            copy.wait()


def write_first(which, blocks):
    half, width = blocks[0].shape
    return pl.pallas_call(
        lambda first, second, out, sems: write_kernel(which, first, second, out, sems),
        out_shape=pltpu.HBM((2 * half, width), BF),
        in_specs=[VMEM, VMEM],
        out_specs=HBM,
        scratch_shapes=[pltpu.SemaphoreType.DMA((2,))],
        compiler_params=pltpu.CompilerParams(vmem_limit_bytes=2 * MIB),
        cost_estimate=cost(0, 8 * blocks[0].size),
    )(*blocks)


def write_rest(which, out, blocks):
    return pl.pallas_call(
        lambda first, second, _, out, sems: write_kernel(which, first, second, out, sems),
        out_shape=pltpu.HBM(out.shape, BF),
        in_specs=[VMEM, VMEM, HBM],
        out_specs=HBM,
        scratch_shapes=[pltpu.SemaphoreType.DMA((2,))],
        input_output_aliases={2: 0},
        compiler_params=pltpu.CompilerParams(vmem_limit_bytes=2 * MIB),
        cost_estimate=cost(0, 8 * blocks[0].size),
    )(*blocks, out)


def permute(value, target):
    sections, leaves = lax.axis_size("sweep"), lax.axis_size("leaf")
    pairs = []
    for s in range(sections):
        for l in range(leaves):
            to = target(s, l)
            if to is not None:
                pairs.append((s * leaves + l, to[0] * leaves + to[1]))
    return lax.ppermute(value, ("sweep", "leaf"), pairs)


def swap(value, bit, row):
    def target(s, l):
        ring = 2 if (l ^ l >> 1) & 1 else 1
        idle = 3 - bit if bit < 3 else ring
        return s, l ^ (bit if s == row else idle)

    return permute(value, target)


def cross(value, bit=0):
    return permute(value, lambda s, l: (s ^ 1, l ^ bit))


def behind(rows, *values):
    rows, *values = lax.optimization_barrier((rows, *values))
    return rows, values


def paired(sources, solve_tiles, self_merge, partner_merge, coupling, front_map):
    solve = solve_tiles[0, 0]
    sections = lax.axis_size("sweep")
    count = self_merge.shape[2]

    x = load(sources[0, 0], solve)
    half = x.shape[0] // 2
    rows, raw = behind(x, self_merge, partner_merge, front_map, coupling)
    own = prepare(*(v[0, 0] for v in raw[:3]), [0, 1])[0]
    other = [None] * count
    own_link = None
    front = None
    even, odd = [], []
    back = out = None
    for section in range(sections):
        if section % 2 == 0:
            if section > 0:
                turn = {section - 1: section, section: section - 1}
                front = [permute(part, lambda s, l: (turn.get(s, s), l)) for part in front]
                rows = [pass_on(0, part, x, own_link, k * half) for k, part in enumerate(front)]
                rows = jnp.concatenate(rows)
            rows = both_parts(0, rows, swap(rows, 1, section), own[0], 0, 2 * half)
            if section == 0:
                rows, (table,) = behind(rows, own[1])
                other[1] = cross(table)
            came = cross(rows)
            partner = cross(rows, 2)
            if section == 0:
                _, raw = behind(rows, *raw)
                more, (own_link,) = prepare(
                    *(v[0, 0] for v in raw[:3]),
                    list(range(2, count)),
                    link=(raw[3][0, 0], solve),
                )
                own += more
            front = [both_parts(1, came, partner, other[1], k * half, half) for k in range(2)]
            first, tables, row = 2, other, section + 1
        else:
            front = [pass_on(1, part, x, own_link, k * half) for k, part in enumerate(front)]
            first, tables, row = 0, own, section
        for j in range(first, count):
            if section == 0 and j == 2:
                _, late = behind(front[0], *own[2:])
                other[2:] = [cross(table) for table in late]
            partners = [swap(part, 2**j, row) for part in front]
            if section % 2 and j == 1:
                _, back = behind(front[0], *back)
                back = [cross(part) for part in back]
            if section % 2 and j == 2:
                front[1], back = behind(front[1], *back)
                if sections == 2:
                    out = write_first(0, back)
                    front[1], (out,) = behind(front[1], out)
            front = [level(1, part, came, tables[j]) for part, came in zip(front, partners)]
        if section % 2 == 0:
            back = front
        elif section == 1:
            even, odd = back, front
        else:
            chosen = lax.axis_index("sweep") // 2 == section // 2
            even = [jnp.where(chosen, new, old) for new, old in zip(back, even)]
            odd = [jnp.where(chosen, new, old) for new, old in zip(front, odd)]
    if out is None:
        out = write_first(0, even)
    return write_rest(1, out, odd)[None, None]


def single(sources, solve_tiles, self_merge, partner_merge, coupling, front_map):
    rows, solve, link = sources[0, 0], solve_tiles[0, 0], coupling[0, 0]
    sections = lax.axis_size("sweep")
    front = jnp.zeros_like(rows)
    for section in range(sections):
        front = permute(front, lambda s, l: ((s + 1) % sections, l))
        front = jnp.where(lax.axis_index("sweep") == 0, jnp.zeros_like(front), front)
        x = mm((rows.astype(F32) + mm(front, link)).astype(BF), solve).astype(BF)
        for j in range(self_merge.shape[2]):
            other = permute(x, lambda s, l, bit=2**j: (s, l ^ bit))
            mapped = jnp.take(other, front_map[0, 0, j], axis=1)
            x = (mm(x, self_merge[0, 0, j]) + mm(mapped, partner_merge[0, 0, j])).astype(BF)
        front = x
    return front[None, None]


def solution(mesh):
    spec = P("sweep", "leaf")
    return jax.shard_map(
        paired if mesh.shape["sweep"] % 2 == 0 else single,
        mesh=mesh,
        in_specs=(spec,) * 6,
        out_specs=spec,
        check_vma=False,
    )
```

```python
import jax
import jax.numpy as jnp
from jax import lax
from jax.experimental import pallas as pl
from jax.experimental.pallas import tpu as pltpu
from jax.sharding import PartitionSpec as P

BF = jnp.bfloat16
F32 = jnp.float32
MIB = 2**20
HINT = 10**8

HBM = pl.BlockSpec(memory_space=pltpu.HBM)
VMEM = pl.BlockSpec(memory_space=pltpu.VMEM)


def mm(left, right):
    return jnp.dot(left, right, preferred_element_type=F32)


def in_hbm(value):
    return pltpu.with_memory_space_constraint(value, pltpu.HBM)


def cost(flops, moved):
    return pl.CostEstimate(flops=flops, bytes_accessed=moved, transcendentals=0)


def side():
    return lax.rem(lax.axis_index("sweep"), 2)


def call(kernel, outs, args, flops, limit=4, **more):
    moved = sum(a.size * a.dtype.itemsize for a in args) + sum(o.size * 4 for o in outs)
    return pl.pallas_call(
        kernel,
        out_shape=tuple(pltpu.VMEM(o.shape, o.dtype) for o in outs),
        in_specs=[VMEM] * len(args),
        out_specs=(VMEM,) * len(outs),
        compiler_params=pltpu.CompilerParams(vmem_limit_bytes=limit * MIB),
        cost_estimate=cost(flops, moved),
        **more,
    )(*args)


def load_kernel(rows_hbm, solve_hbm, out_ref, rows_ref, solve_ref, sems):
    copies = [
        pltpu.make_async_copy(rows_hbm, rows_ref, sems.at[0]),
        pltpu.make_async_copy(solve_hbm, solve_ref, sems.at[1]),
    ]
    for copy in copies:
        copy.start()
    for copy in copies:
        copy.wait()
    out_ref[...] = mm(rows_ref[...], solve_ref[...]).astype(BF)


def load(rows, solve):
    return pl.pallas_call(
        load_kernel,
        out_shape=pltpu.VMEM(rows.shape, BF),
        in_specs=[HBM, HBM],
        out_specs=VMEM,
        scratch_shapes=[
            pltpu.VMEM(rows.shape, BF),
            pltpu.VMEM(solve.shape, BF),
            pltpu.SemaphoreType.DMA((2,)),
        ],
        compiler_params=pltpu.CompilerParams(vmem_limit_bytes=2 * MIB),
        cost_estimate=cost(2 * rows.size * solve.shape[1], 4 * rows.size + 2 * solve.size),
    )(in_hbm(rows), in_hbm(solve))


def prepare_kernel(levels, single, link, own_hbm, partner_hbm, map_hbm, *refs):
    number = len(levels)
    width = own_hbm.shape[1]
    link_hbm, refs = refs[: 2 * link], refs[2 * link :]
    outs, refs = refs[:number], refs[number:]
    singles, refs = refs[: 2 * single], refs[2 * single :]
    products, (partner_ref, map_ref, link_ref, sems, map_sem) = refs[:link], refs[link:]
    map_copy = pltpu.make_async_copy(map_hbm, map_ref, map_sem)
    map_copy.start()
    copies = []
    for k, j in enumerate(levels):
        pair = (
            pltpu.make_async_copy(partner_hbm.at[j], partner_ref.at[k], sems.at[2 * k]),
            pltpu.make_async_copy(own_hbm.at[j], outs[k].at[0], sems.at[2 * k + 1]),
        )
        for copy in pair:
            copy.start()
        copies.append(pair)
    extra = []
    if single:
        extra.append((own_hbm.at[levels[0]], singles[0]))
    for k, source in enumerate(link_hbm):
        extra.append((source, link_ref.at[k]))
    extra = [
        pltpu.make_async_copy(source, target, sems.at[2 * number + k])
        for k, (source, target) in enumerate(extra)
    ]
    for copy in extra:
        copy.start()
    map_copy.wait()
    rows = lax.broadcasted_iota(jnp.int32, (width, width), 0)
    for k, j in enumerate(levels):
        copies[k][0].wait()
        hot = (rows == map_ref[j : j + 1, :]).astype(BF)
        folded = mm(hot, partner_ref[k]).astype(BF)
        outs[k][1] = folded
        if single and k == 0:
            singles[1][...] = folded
    for copy in extra:
        copy.wait()
    if link:
        products[0][...] = mm(link_ref[0], link_ref[1]).astype(BF)
    for pair in copies:
        pair[1].wait()


def prepare(own, partner, index_map, levels, single=0, link=()):
    width = own.shape[1]
    number = len(levels)
    more = len(link) // 2
    outs = pl.pallas_call(
        lambda *refs: prepare_kernel(levels, single, more, *refs),
        out_shape=(pltpu.VMEM((2, width, width), BF),) * number
        + (pltpu.VMEM((width, width), BF),) * (2 * single + more),
        in_specs=[HBM] * (3 + len(link)),
        out_specs=(VMEM,) * (number + 2 * single + more),
        scratch_shapes=[
            pltpu.VMEM((number, width, width), BF),
            pltpu.VMEM(index_map.shape, jnp.int32),
            pltpu.VMEM((2, width, width), BF),
            pltpu.SemaphoreType.DMA((2 * number + 2,)),
            pltpu.SemaphoreType.DMA,
        ],
        compiler_params=pltpu.CompilerParams(vmem_limit_bytes=8 * MIB),
        cost_estimate=cost(2 * number * width**3, 8 * number * width**2),
    )(*(in_hbm(value) for value in (own, partner, index_map, *link)))
    return list(outs[:number]), list(outs[number:])


def level(which, rows, partner, table):
    def kernel(rows_ref, partner_ref, table_ref, out_ref):
        @pl.when(side() == which)
        def _():
            total = mm(rows_ref[...], table_ref[0]) + mm(partner_ref[...], table_ref[1])
            out_ref[...] = total.astype(BF)

    out = jax.ShapeDtypeStruct(rows.shape, BF)
    return call(kernel, [out], [rows, partner, table], HINT)[0]


def both_parts(which, rows, partner, table, start, count):
    def kernel(rows_ref, partner_ref, table_ref, out_ref):
        @pl.when(side() == which)
        def _():
            block = slice(start, start + count)
            total = mm(rows_ref[block], table_ref[0]) + mm(partner_ref[block], table_ref[1])
            out_ref[...] = total.astype(BF)

    out = jax.ShapeDtypeStruct((count, rows.shape[1]), BF)
    return call(kernel, [out], [rows, partner, table], HINT)[0]


def pass_on(which, front, x, link, start):
    count = front.shape[0]

    def kernel(front_ref, x_ref, link_ref, out_ref):
        @pl.when(side() == which)
        def _():
            known = x_ref[start : start + count].astype(F32)
            out_ref[...] = (known + mm(front_ref[...], link_ref[...])).astype(BF)

    return call(kernel, [jax.ShapeDtypeStruct(front.shape, BF)], [front, x, link], HINT)[0]


def write_kernel(which, first_ref, second_ref, out_ref, sems):
    half = first_ref.shape[0]

    @pl.when(side() == which)
    def _():
        copies = [
            pltpu.make_async_copy(first_ref, out_ref.at[pl.ds(0, half)], sems.at[0]),
            pltpu.make_async_copy(second_ref, out_ref.at[pl.ds(half, half)], sems.at[1]),
        ]
        for copy in copies:
            copy.start()
        for copy in copies:
            copy.wait()


def write_first(which, blocks):
    half, width = blocks[0].shape
    return pl.pallas_call(
        lambda first, second, out, sems: write_kernel(which, first, second, out, sems),
        out_shape=pltpu.HBM((2 * half, width), BF),
        in_specs=[VMEM, VMEM],
        out_specs=HBM,
        scratch_shapes=[pltpu.SemaphoreType.DMA((2,))],
        compiler_params=pltpu.CompilerParams(vmem_limit_bytes=2 * MIB),
        cost_estimate=cost(0, 8 * blocks[0].size),
    )(*blocks)


def write_rest(which, out, blocks):
    return pl.pallas_call(
        lambda first, second, _, out, sems: write_kernel(which, first, second, out, sems),
        out_shape=pltpu.HBM(out.shape, BF),
        in_specs=[VMEM, VMEM, HBM],
        out_specs=HBM,
        scratch_shapes=[pltpu.SemaphoreType.DMA((2,))],
        input_output_aliases={2: 0},
        compiler_params=pltpu.CompilerParams(vmem_limit_bytes=2 * MIB),
        cost_estimate=cost(0, 8 * blocks[0].size),
    )(*blocks, out)


def finish(which, out, first, rows, partner, table, at):
    half, width = rows.shape

    def kernel(first_ref, rows_ref, partner_ref, table_ref, _, out_ref, second_ref, sems):
        @pl.when(side() == which)
        def _():
            head = pltpu.make_async_copy(first_ref, out_ref.at[pl.ds(0, half)], sems.at[0])
            head.start()
            total = mm(rows_ref[...], table_ref[at]) + mm(partner_ref[...], table_ref[at + 1])
            second_ref[...] = total.astype(BF)
            tail = pltpu.make_async_copy(second_ref, out_ref.at[pl.ds(half, half)], sems.at[1])
            tail.start()
            head.wait()
            tail.wait()

    return pl.pallas_call(
        kernel,
        out_shape=pltpu.HBM(out.shape, BF),
        in_specs=[VMEM] * 4 + [HBM],
        out_specs=HBM,
        scratch_shapes=[pltpu.VMEM((half, width), BF), pltpu.SemaphoreType.DMA((2,))],
        input_output_aliases={4: 0},
        compiler_params=pltpu.CompilerParams(vmem_limit_bytes=4 * MIB),
        cost_estimate=cost(HINT, 8 * rows.size),
    )(first, rows, partner, table, out)


def permute(value, target):
    sections, leaves = lax.axis_size("sweep"), lax.axis_size("leaf")
    pairs = []
    for s in range(sections):
        for l in range(leaves):
            to = target(s, l)
            if to is not None:
                pairs.append((s * leaves + l, to[0] * leaves + to[1]))
    return lax.ppermute(value, ("sweep", "leaf"), pairs)


def swap(value, bit, row):
    def target(s, l):
        ring = 2 if (l ^ l >> 1) & 1 else 1
        return s, l ^ (bit if s == row else ring)

    return permute(value, target)


def cross(value, bit=0):
    return permute(value, lambda s, l: (s ^ 1, l ^ bit))


def behind(rows, *values):
    rows, *values = lax.optimization_barrier((rows, *values))
    return rows, values


def paired(sources, solve_tiles, self_merge, partner_merge, coupling, front_map):
    solve = solve_tiles[0, 0]
    sections = lax.axis_size("sweep")
    count = self_merge.shape[2]

    x = load(sources[0, 0], solve)
    half = x.shape[0] // 2
    rows, raw = behind(x, self_merge, partner_merge, front_map, coupling)
    own = prepare(*(v[0, 0] for v in raw[:3]), [0, 1])[0]
    other = [None] * count
    own_link = None
    front = None
    even, odd = [], []
    back = out = None
    for section in range(sections):
        if section % 2 == 0:
            if section > 0:
                turn = {section - 1: section, section: section - 1}
                front = [permute(part, lambda s, l: (turn.get(s, s), l)) for part in front]
                rows = [pass_on(0, part, x, own_link, k * half) for k, part in enumerate(front)]
                rows = jnp.concatenate(rows)
            rows = both_parts(0, rows, swap(rows, 1, section), own[0], 0, 2 * half)
            if section == 0:
                rows, (table,) = behind(rows, own[1])
                other[1] = cross(table)
            came = cross(rows)
            partner = cross(rows, 2)
            if section == 0:
                _, raw = behind(rows, *raw)
                more, (own_link,) = prepare(
                    *(v[0, 0] for v in raw[:3]),
                    list(range(2, count)),
                    link=(raw[3][0, 0], solve),
                )
                own += more
            front = [both_parts(1, came, partner, other[1], k * half, half) for k in range(2)]
            first, tables, row = 2, other, section + 1
        else:
            front = [pass_on(1, part, x, own_link, k * half) for k, part in enumerate(front)]
            first, tables, row = 0, own, section
        for j in range(first, count):
            if section == 0 and j == 2:
                _, late = behind(front[0], *own[2:])
                other[2:] = [cross(table) for table in late]
            partners = [swap(part, 2**j, row) for part in front]
            if section % 2 and j == 1:
                _, back = behind(front[0], *back)
                back = [cross(part) for part in back]
            if section % 2 and j == 2:
                front[1], back = behind(front[1], *back)
                if sections == 2:
                    out = write_first(0, back)
                    front[1], (out,) = behind(front[1], out)
            if sections == 2 and section == 1 and j == count - 1:
                head = level(1, front[0], partners[0], tables[j])
                return finish(1, out, head, front[1], partners[1], tables[j], 0)[None, None]
            front = [level(1, part, came, tables[j]) for part, came in zip(front, partners)]
        if section % 2 == 0:
            back = front
        elif section == 1:
            even, odd = back, front
        else:
            chosen = lax.axis_index("sweep") // 2 == section // 2
            even = [jnp.where(chosen, new, old) for new, old in zip(back, even)]
            odd = [jnp.where(chosen, new, old) for new, old in zip(front, odd)]
    if out is None:
        out = write_first(0, even)
    return write_rest(1, out, odd)[None, None]


def single(sources, solve_tiles, self_merge, partner_merge, coupling, front_map):
    rows, solve, link = sources[0, 0], solve_tiles[0, 0], coupling[0, 0]
    sections = lax.axis_size("sweep")
    front = jnp.zeros_like(rows)
    for section in range(sections):
        front = permute(front, lambda s, l: ((s + 1) % sections, l))
        front = jnp.where(lax.axis_index("sweep") == 0, jnp.zeros_like(front), front)
        x = mm((rows.astype(F32) + mm(front, link)).astype(BF), solve).astype(BF)
        for j in range(self_merge.shape[2]):
            other = permute(x, lambda s, l, bit=2**j: (s, l ^ bit))
            mapped = jnp.take(other, front_map[0, 0, j], axis=1)
            x = (mm(x, self_merge[0, 0, j]) + mm(mapped, partner_merge[0, 0, j])).astype(BF)
        front = x
    return front[None, None]


def solution(mesh):
    spec = P("sweep", "leaf")
    return jax.shard_map(
        paired if mesh.shape["sweep"] % 2 == 0 else single,
        mesh=mesh,
        in_specs=(spec,) * 6,
        out_specs=spec,
        check_vma=False,
    )
```
